32 devices in a mesh: groups: 2 (over x), col: 16 (over z, y, core).
Axes of the slice: x: 2, y: 2, z: 4, core: 2. Of those that a mesh axis runs over, the one named last changes fastest.
Arguments:
- inputs: bfloat16 [64, 8192], P(('groups', 'col')), parts along dimension 0, may hold values from -6 to 6
- cotangent: bfloat16 [64, 8192], P(('groups', 'col')), parts along dimension 0, may hold values from -6 to 6
- gate_tiles: bfloat16 [192, 20, 128, 128], P('col'), may hold values from -0.15625 to 0.15625
- up_tiles: bfloat16 [192, 20, 128, 128], P('col'), may hold values from -0.15625 to 0.15625
- down_tiles: bfloat16 [192, 20, 128, 128], P('col'), may hold values from -0.078125 to 0.078125
- kept_rows: int32 [192, 20], P('col'), may hold values from 0 to 63, as said below
- kept_count: int32 [192], P('col'), may hold values from 6 to 20, as said below
Outputs:
- output: bfloat16 [64, 8192], P(('groups', 'col')), parts along dimension 0
- x_grad: bfloat16 [64, 8192], P(('groups', 'col')), parts along dimension 0
- gate_grad: bfloat16 [384, 20, 128, 128], P(('groups', 'col')), parts along dimension 0
- up_grad: bfloat16 [384, 20, 128, 128], P(('groups', 'col')), parts along dimension 0
- down_grad: bfloat16 [384, 20, 128, 128], P(('groups', 'col')), parts along dimension 0
The draws below stay inside these ranges and needn't reach their ends.
There are 2 independent parts, one for each index of `groups`. The reference program is written for one: setup_inputs(seed, part) draws one part's arguments, and reference() takes and returns one part's arrays. A program takes and returns all parts, laid end to end along the dimension named above; an argument that names none is the same for every part. Nothing has to cross between parts.
Inputs may be any that keep to these rules, and one draw needn't show every extreme that they name: `kept_count`: how many slots of a column block are kept, the kept ones first; some block keeps 20, some 20 // 3. `kept_rows`: the 20 slots of a column block name different row blocks.
All inputs are finite; a program needn't handle non-finite values.
Results may differ from the reference program's by a relative error of at most 0.005.
Values may be sent and summed in bfloat16 or wider, within the bound.
No kernel may reach another device: no remote copies, remote signals or barrier semaphores. Data moves between devices by JAX's collectives and lax.ppermute only.
A program may use at most 128 MiB of HBM per device.

```python
import jax
import jax.numpy as jnp
from jax import lax

D = 8192
FF = 24576
BLK = 128
CAP = 20
TOKENS = 32
RB = 64
CB = 192


def draw_kept_count(key, part):
    key = jax.random.fold_in(key, 11)
    first, second = jax.random.split(key)
    counts = jax.random.randint(first, (CB,), CAP // 3, CAP + 1)
    order = jax.random.permutation(second, CB)
    counts = counts.at[order[0]].set(CAP).at[order[1]].set(CAP // 3)
    return counts.astype(jnp.int32)


def draw_kept_rows(key, part):
    key = jax.random.fold_in(key, 12)
    scores = jax.random.randint(key, (CB, RB), 0, 2 ** 20) * RB + jnp.arange(RB, dtype=jnp.int32)[None, :]
    order = jnp.argsort(scores, axis=1, stable=True)
    return order[:, :CAP].astype(jnp.int32)


def level_of(key, dims, cuts, low, high):
    def one(position, blocks):
        heights = jax.random.uniform(jax.random.fold_in(jax.random.fold_in(key, 6), position), (blocks,), jnp.float32, low / len(cuts), high / len(cuts))
        return jnp.repeat(jnp.exp(heights), dims[position] // blocks).reshape((-1,) + (1,) * (len(dims) - position - 1))

    loudness = one(*cuts[0])
    for cut in cuts[1:]:
        loudness = loudness * one(*cut)
    return loudness


def gaussian(rng, shape, deviation, reach, pieces=(), kind=jnp.bfloat16):
    result = deviation * jax.random.normal(rng, shape, jnp.float32)
    if pieces:
        result = result * level_of(rng, shape, pieces, -0.22, 0.18)
    return jnp.clip(result, -reach, reach).astype(kind)


def setup_inputs(seed: int = 0, part: int = 0) -> dict:
    streams_of = jax.random.split(jax.random.key(seed), 8)
    part_splits = jax.random.split(jax.random.fold_in(streams_of[7], part), 8)
    inputs = gaussian(part_splits[0], (TOKENS, D), 1.0, 6.0, ((0, 16),))
    cotangent = gaussian(part_splits[1], (TOKENS, D), 1.0, 6.0, ((0, 16),))
    gate_tiles = gaussian(streams_of[2], (CB, CAP, BLK, BLK), ((CAP // 3 + CAP) * BLK // 2) ** -0.5, 0.15625, ((0, 16),))
    up_tiles = gaussian(streams_of[3], (CB, CAP, BLK, BLK), ((CAP // 3 + CAP) * BLK // 2) ** -0.5, 0.15625, ((0, 16),))
    down_tiles = gaussian(streams_of[4], (CB, CAP, BLK, BLK), ((CAP // 3 + CAP) * FF // (2 * RB)) ** -0.5, 0.078125, ((0, 16),))
    kept_rows = draw_kept_rows(jax.random.fold_in(streams_of[7], 71), part)
    kept_count = draw_kept_count(jax.random.fold_in(streams_of[7], 71), part)
    return {"inputs": inputs, "cotangent": cotangent, "gate_tiles": gate_tiles, "up_tiles": up_tiles, "down_tiles": down_tiles, "kept_rows": kept_rows, "kept_count": kept_count}


def reference(inputs, cotangent, gate_tiles, up_tiles, down_tiles, kept_rows, kept_count):
    highest = lax.Precision.HIGHEST
    tokens = inputs.shape[0]
    x3 = inputs.reshape(tokens, RB, BLK).astype(jnp.float32)
    dy3 = cotangent.reshape(tokens, RB, BLK).astype(jnp.float32)
    slot_ids = jnp.arange(CAP, dtype=jnp.int32)
    block_ids = jnp.arange(RB, dtype=jnp.int32)

    def step(carry, item):
        out_acc, grad_acc = carry
        gate, upper, down, rows, count = item
        live = slot_ids < count
        maskf = live.astype(jnp.float32)[:, None, None]
        gate_f = gate.astype(jnp.float32) * maskf
        up_f = upper.astype(jnp.float32) * maskf
        down_f = down.astype(jnp.float32) * maskf
        xg = x3[:, rows]
        dyg = dy3[:, rows]
        gate_pre = jnp.einsum('tsk,skn->tn', xg, gate_f, precision=highest)
        up_pre = jnp.einsum('tsk,skn->tn', xg, up_f, precision=highest)
        sig = jax.nn.sigmoid(gate_pre)
        act = gate_pre * sig
        hidden = (act * up_pre).astype(jnp.bfloat16)
        hidden_f = lax.optimization_barrier(hidden).astype(jnp.float32)
        onehot = (rows[:, None] == block_ids[None, :]).astype(jnp.float32) * live.astype(jnp.float32)[:, None]
        y_slots = jnp.einsum('tk,skn->tsn', hidden_f, down_f, precision=highest)
        out_acc = out_acc + jnp.einsum('sr,tsn->trn', onehot, y_slots, precision=highest)
        d_hidden = jnp.einsum('tsn,skn->tk', dyg, down_f, precision=highest)
        d_gate = (d_hidden * up_pre * sig * (1.0 + gate_pre * (1.0 - sig))).astype(jnp.bfloat16)
        d_up = (d_hidden * act).astype(jnp.bfloat16)
        d_gate_f = lax.optimization_barrier(d_gate).astype(jnp.float32)
        d_up_f = lax.optimization_barrier(d_up).astype(jnp.float32)
        x_slots = jnp.einsum('tn,skn->tsk', d_gate_f, gate_f, precision=highest) + jnp.einsum('tn,skn->tsk', d_up_f, up_f, precision=highest)
        grad_acc = grad_acc + jnp.einsum('sr,tsk->trk', onehot, x_slots, precision=highest)
        gate_grad = (jnp.einsum('tsk,tn->skn', xg, d_gate_f, precision=highest) * maskf).astype(jnp.bfloat16)
        up_grad = (jnp.einsum('tsk,tn->skn', xg, d_up_f, precision=highest) * maskf).astype(jnp.bfloat16)
        down_grad = (jnp.einsum('tk,tsn->skn', hidden_f, dyg, precision=highest) * maskf).astype(jnp.bfloat16)
        return (out_acc, grad_acc), (gate_grad, up_grad, down_grad)

    start = (jnp.zeros((tokens, RB, BLK), jnp.float32), jnp.zeros((tokens, RB, BLK), jnp.float32))
    (out_acc, grad_acc), grads = lax.scan(step, start, (gate_tiles, up_tiles, down_tiles, kept_rows, kept_count))
    output = out_acc.reshape(tokens, D).astype(jnp.bfloat16)
    x_grad = grad_acc.reshape(tokens, D).astype(jnp.bfloat16)
    return (output, x_grad, grads[0], grads[1], grads[2])
```

```python
import functools

import jax
import jax.numpy as jnp
from jax import lax
from jax.experimental import pallas as pl
from jax.experimental.pallas import tpu as pltpu
from jax.sharding import PartitionSpec as P

NT = (((1,), (1,)), ((), ()))
TN = (((0,), (0,)), ((), ()))
CHUNK = 4


def slot_offsets(rows_ref, count_ref, c, dead, blk):
    count = count_ref[c]
    capacity = rows_ref.shape[1]
    return [
        pl.multiple_of(jnp.where(s < count, rows_ref[c, s], dead) * blk, blk)
        for s in range(capacity)
    ]


def add_to_rows(acc, offs, parts, blk):
    old = [acc[:, pl.ds(o, blk)] for o in offs]
    for i, o in enumerate(offs):
        acc[:, pl.ds(o, blk)] = old[i] + parts[:, i * blk : (i + 1) * blk]


def emit_halves(acc, keep_ref, send_ref, width):
    half = keep_ref.shape[0]
    keep_ref[...] = acc[:half, :width]
    send_ref[...] = acc[half:, :width].astype(send_ref.dtype)


def forward_kernel(
    rows_ref, count_ref, x_ref, wg_ref, wu_ref, wd_ref,
    gate_ref, up_ref, hidden_ref, xpad_ref, keep_ref, send_ref, acc,
):
    tokens, width = x_ref.shape
    blocks, capacity, blk, _ = wg_ref.shape
    xpad_ref[:, :width] = x_ref[...]
    xpad_ref[:, width:] = jnp.zeros((tokens, blk), xpad_ref.dtype)
    acc[...] = jnp.zeros_like(acc)

    def block(c, carry):
        offs = slot_offsets(rows_ref, count_ref, c, width // blk, blk)
        xg = jnp.concatenate([xpad_ref[:, pl.ds(o, blk)] for o in offs], axis=1)
        w = jnp.concatenate(
            [wg_ref[c].reshape(capacity * blk, blk), wu_ref[c].reshape(capacity * blk, blk)],
            axis=1,
        )
        pre = jnp.dot(xg, w, preferred_element_type=jnp.float32)
        gate, up = pre[:, :blk], pre[:, blk:]
        gate_ref[c] = gate
        up_ref[c] = up
        act = gate * (1.0 / (1.0 + jnp.exp(-gate)))
        hidden = (act * up).astype(jnp.bfloat16)
        hidden_ref[c] = hidden
        for s in range(0, capacity, CHUNK):
            wd = jnp.concatenate([wd_ref[c, s + i] for i in range(CHUNK)], axis=1)
            y = jnp.dot(hidden, wd, preferred_element_type=jnp.float32)
            add_to_rows(acc, offs[s : s + CHUNK], y, blk)
        return carry

    lax.fori_loop(0, blocks, block, 0)
    emit_halves(acc, keep_ref, send_ref, width)


def backward_kernel(
    rows_ref, count_ref, dy_ref, gate_ref, up_ref, wg_ref, wu_ref, wd_ref,
    d_ref, dypad_ref, keep_ref, send_ref, acc,
):
    tokens, width = dy_ref.shape
    blocks, capacity, blk, _ = wg_ref.shape
    dypad_ref[:, :width] = dy_ref[...]
    dypad_ref[:, width:] = jnp.zeros((tokens, blk), dypad_ref.dtype)
    acc[...] = jnp.zeros_like(acc)

    def block(c, carry):
        offs = slot_offsets(rows_ref, count_ref, c, width // blk, blk)
        dyg = jnp.concatenate([dypad_ref[:, pl.ds(o, blk)] for o in offs], axis=1)
        wd = jnp.concatenate([wd_ref[c, s] for s in range(capacity)], axis=1)
        d_hidden = lax.dot_general(dyg, wd, NT, preferred_element_type=jnp.float32)
        gate, up = gate_ref[c], up_ref[c]
        sig = 1.0 / (1.0 + jnp.exp(-gate))
        act = gate * sig
        d_gate = (d_hidden * up * sig * (1.0 + gate * (1.0 - sig))).astype(jnp.bfloat16)
        d_up = (d_hidden * act).astype(jnp.bfloat16)
        d = jnp.concatenate([d_gate, d_up], axis=1)
        d_ref[c] = d
        for s in range(0, capacity, CHUNK):
            w = jnp.concatenate(
                [
                    wg_ref[c, s : s + CHUNK].reshape(CHUNK * blk, blk),
                    wu_ref[c, s : s + CHUNK].reshape(CHUNK * blk, blk),
                ],
                axis=1,
            )
            x_slots = lax.dot_general(d, w, NT, preferred_element_type=jnp.float32)
            add_to_rows(acc, offs[s : s + CHUNK], x_slots, blk)
        return carry

    lax.fori_loop(0, blocks, block, 0)
    emit_halves(acc, keep_ref, send_ref, width)


def gate_up_grad_kernel(rows_ref, count_ref, xpad_ref, d_ref, gate_grad_ref, up_grad_ref):
    _, capacity, blk, _ = gate_grad_ref.shape
    c = pl.program_id(0)
    offs = slot_offsets(rows_ref, count_ref, c, xpad_ref.shape[1] // blk - 1, blk)
    d = d_ref[c]
    for s in range(capacity):
        full = lax.dot_general(
            xpad_ref[:, pl.ds(offs[s], blk)], d, TN, preferred_element_type=jnp.float32
        ).astype(jnp.bfloat16)
        gate_grad_ref[0, s] = full[:, :blk]
        up_grad_ref[0, s] = full[:, blk:]


def down_grad_kernel(rows_ref, count_ref, dypad_ref, hidden_ref, down_grad_ref):
    _, capacity, blk, _ = down_grad_ref.shape
    c = pl.program_id(0)
    offs = slot_offsets(rows_ref, count_ref, c, dypad_ref.shape[1] // blk - 1, blk)
    hidden = hidden_ref[c]
    for s in range(0, capacity, 2):
        dys = jnp.concatenate([dypad_ref[:, pl.ds(o, blk)] for o in offs[s : s + 2]], axis=1)
        full = lax.dot_general(hidden, dys, TN, preferred_element_type=jnp.float32)
        full = full.astype(jnp.bfloat16)
        down_grad_ref[0, s] = full[:, :blk]
        down_grad_ref[0, s + 1] = full[:, blk:]


def swap(value, bit, n):
    return lax.ppermute(value, "col", [(i, i ^ bit) for i in range(n)])


def gather_tokens(value, bits, n):
    held = value[None]
    for bit in bits:
        held = jnp.concatenate([held, swap(held, bit, n)], axis=0)
    return held.reshape(held.shape[0] * held.shape[1], held.shape[2])


def scatter_step(keep, send, bit, n):
    total = keep + swap(send, bit, n).astype(jnp.float32)
    half = total.shape[0] // 2
    return total[:half], total[half:].astype(jnp.bfloat16)


def scatter_tokens(keep, send, bits, n):
    for bit in bits[:-1]:
        keep, send = scatter_step(keep, send, bit, n)
    return (keep + swap(send, bits[-1], n).astype(jnp.float32)).astype(jnp.bfloat16)


def local(n, inputs, cotangent, gate_tiles, up_tiles, down_tiles, kept_rows, kept_count):
    blocks, capacity, blk, _ = gate_tiles.shape
    mine, width = inputs.shape
    tokens = mine * n
    bits = [1 << i for i in range(n.bit_length() - 1)]
    smem = pl.BlockSpec(memory_space=pltpu.SMEM)
    vmem = pl.BlockSpec(memory_space=pltpu.VMEM)
    params = pltpu.CompilerParams(vmem_limit_bytes=16 * 1024 * 1024)
    wg, wu, wd = (
        pltpu.with_memory_space_constraint(t, pltpu.VMEM) for t in (gate_tiles, up_tiles, down_tiles)
    )
    tile_bytes = blocks * capacity * blk * blk * 2

    def shape(dims, dtype):
        return pltpu.VMEM(dims, dtype)

    x_all = gather_tokens(inputs, bits[::-1], n)
    dy_all = gather_tokens(cotangent, bits[::-1], n)
    gate, up, hidden, xpad, keep, send = pl.pallas_call(
        forward_kernel,
        in_specs=[smem, smem] + [vmem] * 4,
        out_specs=[vmem] * 6,
        out_shape=[
            shape((blocks, tokens, blk), jnp.float32),
            shape((blocks, tokens, blk), jnp.float32),
            shape((blocks, tokens, blk), jnp.bfloat16),
            shape((tokens, width + blk), jnp.bfloat16),
            shape((tokens // 2, width), jnp.float32),
            shape((tokens // 2, width), jnp.bfloat16),
        ],
        scratch_shapes=[pltpu.VMEM((tokens, width + blk), jnp.float32)],
        compiler_params=params,
        cost_estimate=pl.CostEstimate(
            flops=6 * tokens * tile_bytes // 2, bytes_accessed=3 * tile_bytes, transcendentals=0
        ),
        name="forward",
    )(kept_rows, kept_count, x_all, wg, wu, wd)
    output = scatter_tokens(keep, send, bits, n)
    d, dypad, keep, send = pl.pallas_call(
        backward_kernel,
        in_specs=[smem, smem] + [vmem] * 6,
        out_specs=[vmem] * 4,
        out_shape=[
            shape((blocks, tokens, 2 * blk), jnp.bfloat16),
            shape((tokens, width + blk), jnp.bfloat16),
            shape((tokens // 2, width), jnp.float32),
            shape((tokens // 2, width), jnp.bfloat16),
        ],
        scratch_shapes=[pltpu.VMEM((tokens, width + blk), jnp.float32)],
        compiler_params=params,
        cost_estimate=pl.CostEstimate(
            flops=6 * tokens * tile_bytes // 2, bytes_accessed=3 * tile_bytes, transcendentals=0
        ),
        name="backward",
    )(kept_rows, kept_count, dy_all, gate, up, wg, wu, wd)
    x_grad = scatter_tokens(keep, send, bits, n)

    def grads(kernel, padded, factor, count, name):
        tile = pl.BlockSpec((1, capacity, blk, blk), lambda c: (c, 0, 0, 0))
        return pl.pallas_call(
            kernel,
            grid=(blocks,),
            in_specs=[smem, smem, vmem, vmem],
            out_specs=[tile] * count,
            out_shape=[jax.ShapeDtypeStruct(gate_tiles.shape, jnp.bfloat16)] * count,
            compiler_params=pltpu.CompilerParams(vmem_limit_bytes=16 * 1024 * 1024),
            cost_estimate=pl.CostEstimate(
                flops=2 * count * tokens * tile_bytes // 2,
                bytes_accessed=count * tile_bytes,
                transcendentals=0,
            ),
            name=name,
        )(kept_rows, kept_count, padded, factor)

    (down_grad,) = grads(down_grad_kernel, dypad, hidden, 1, "down_grad")
    gate_grad, up_grad = grads(gate_up_grad_kernel, xpad, d, 2, "gate_up_grad")
    return output, x_grad, gate_grad, up_grad, down_grad


def solution(mesh):
    tiles = P("col", None, None, None)
    tokens = P(("groups", "col"), None)
    grads = P(("groups", "col"), None, None, None)
    return jax.shard_map(
        functools.partial(local, mesh.shape["col"]),
        mesh=mesh,
        in_specs=(tokens, tokens, tiles, tiles, tiles, P("col", None), P("col")),
        out_specs=(tokens, tokens, grads, grads, grads),
        check_vma=False,
    )
```

```python
import functools

import jax
import jax.numpy as jnp
from jax import lax
from jax.experimental import pallas as pl
from jax.experimental.pallas import tpu as pltpu
from jax.sharding import PartitionSpec as P

NT = (((1,), (1,)), ((), ()))
TN = (((0,), (0,)), ((), ()))
CHUNK = 4


def slot_offsets(rows_ref, count_ref, c, dead, blk):
    count = count_ref[c]
    capacity = rows_ref.shape[1]
    return [
        pl.multiple_of(jnp.where(s < count, rows_ref[c, s], dead) * blk, blk)
        for s in range(capacity)
    ]


def add_to_rows(acc, offs, parts, blk):
    old = [acc[:, pl.ds(o, blk)] for o in offs]
    for i, o in enumerate(offs):
        acc[:, pl.ds(o, blk)] = old[i] + parts[:, i * blk : (i + 1) * blk]


def emit_halves(acc, keep_ref, send_ref, width):
    half = keep_ref.shape[0]
    keep_ref[...] = acc[:half, :width]
    send_ref[...] = acc[half:, :width].astype(send_ref.dtype)


def layer_kernel(
    rows_ref, count_ref, x_ref, dy_ref, wg_hbm, wu_hbm, wd_hbm,
    hidden_ref, d_ref, xpad_ref, dypad_ref, out_keep, out_send, grad_keep, grad_send,
    out_acc, grad_acc, wg_ref, wu_ref, wd_ref, sems,
):
    tokens, width = x_ref.shape
    blocks, capacity, blk, _ = wg_ref.shape

    def copies(c):
        return [
            pltpu.make_async_copy(src.at[c], dst.at[c], sems.at[i, c])
            for i, (src, dst) in enumerate(((wg_hbm, wg_ref), (wu_hbm, wu_ref), (wd_hbm, wd_ref)))
        ]

    for c in range(blocks):
        for copy in copies(c):
            copy.start()
    for pad, values in ((xpad_ref, x_ref), (dypad_ref, dy_ref)):
        pad[:, :width] = values[...]
        pad[:, width:] = jnp.zeros((tokens, blk), pad.dtype)
    out_acc[...] = jnp.zeros_like(out_acc)
    grad_acc[...] = jnp.zeros_like(grad_acc)

    def inward(c):
        offs = slot_offsets(rows_ref, count_ref, c, width // blk, blk)
        xg = jnp.concatenate([xpad_ref[:, pl.ds(o, blk)] for o in offs], axis=1)
        w = jnp.concatenate(
            [wg_ref[c].reshape(capacity * blk, blk), wu_ref[c].reshape(capacity * blk, blk)],
            axis=1,
        )
        pre = jnp.dot(xg, w, preferred_element_type=jnp.float32)
        dyg = jnp.concatenate([dypad_ref[:, pl.ds(o, blk)] for o in offs], axis=1)
        wd = jnp.concatenate([wd_ref[c, s] for s in range(capacity)], axis=1)
        d_hidden = lax.dot_general(dyg, wd, NT, preferred_element_type=jnp.float32)
        gate, up = pre[:, :blk], pre[:, blk:]
        sig = 1.0 / (1.0 + jnp.exp(-gate))
        act = gate * sig
        hidden_ref[c] = (act * up).astype(jnp.bfloat16)
        d_ref[c, :, :blk] = (d_hidden * up * sig * (1.0 + gate * (1.0 - sig))).astype(jnp.bfloat16)
        d_ref[c, :, blk:] = (d_hidden * act).astype(jnp.bfloat16)

    def outward(c):
        offs = slot_offsets(rows_ref, count_ref, c, width // blk, blk)
        hidden = hidden_ref[c]
        d = d_ref[c]
        for s in range(0, capacity, CHUNK):
            wd = jnp.concatenate([wd_ref[c, s + i] for i in range(CHUNK)], axis=1)
            y = jnp.dot(hidden, wd, preferred_element_type=jnp.float32)
            add_to_rows(out_acc, offs[s : s + CHUNK], y, blk)
            w = jnp.concatenate(
                [
                    wg_ref[c, s : s + CHUNK].reshape(CHUNK * blk, blk),
                    wu_ref[c, s : s + CHUNK].reshape(CHUNK * blk, blk),
                ],
                axis=1,
            )
            x_slots = lax.dot_general(d, w, NT, preferred_element_type=jnp.float32)
            add_to_rows(grad_acc, offs[s : s + CHUNK], x_slots, blk)

    def arrived(c):
        for copy in copies(c):
            copy.wait()

    arrived(0)
    inward(0)

    def step(c, carry):
        arrived(c)
        outward(c - 1)
        inward(c)
        return carry

    lax.fori_loop(1, blocks, step, 0)
    outward(blocks - 1)
    emit_halves(out_acc, out_keep, out_send, width)
    emit_halves(grad_acc, grad_keep, grad_send, width)


def gate_up_grad_kernel(rows_ref, count_ref, xpad_ref, d_ref, gate_grad_ref, up_grad_ref):
    _, capacity, blk, _ = gate_grad_ref.shape
    c = pl.program_id(0)
    offs = slot_offsets(rows_ref, count_ref, c, xpad_ref.shape[1] // blk - 1, blk)
    d = d_ref[c]
    for s in range(capacity):
        full = lax.dot_general(
            xpad_ref[:, pl.ds(offs[s], blk)], d, TN, preferred_element_type=jnp.float32
        ).astype(jnp.bfloat16)
        gate_grad_ref[0, s] = full[:, :blk]
        up_grad_ref[0, s] = full[:, blk:]


def down_grad_kernel(rows_ref, count_ref, dypad_ref, hidden_ref, down_grad_ref):
    _, capacity, blk, _ = down_grad_ref.shape
    c = pl.program_id(0)
    offs = slot_offsets(rows_ref, count_ref, c, dypad_ref.shape[1] // blk - 1, blk)
    hidden = hidden_ref[c]
    for s in range(0, capacity, 2):
        dys = jnp.concatenate([dypad_ref[:, pl.ds(o, blk)] for o in offs[s : s + 2]], axis=1)
        full = lax.dot_general(hidden, dys, TN, preferred_element_type=jnp.float32)
        full = full.astype(jnp.bfloat16)
        down_grad_ref[0, s] = full[:, :blk]
        down_grad_ref[0, s + 1] = full[:, blk:]


def swap(value, bit, n):
    return lax.ppermute(value, "col", [(i, i ^ bit) for i in range(n)])


def gather_start(value, n):
    held = jnp.zeros((n,) + value.shape, value.dtype)
    return lax.dynamic_update_slice_in_dim(held, value[None], 0, 0)


def gather_hop(held, size, bit, n):
    return lax.dynamic_update_slice_in_dim(held, swap(held[:size], bit, n), size, 0)


def arrange(held, order, wanted):
    levels = len(order)
    split = held.reshape((2,) * levels + held.shape[1:])
    axis = {bit: levels - 1 - i for i, bit in enumerate(order)}
    perm = [axis[bit] for bit in wanted[::-1]] + [levels, levels + 1]
    moved = split.transpose(perm) if perm != sorted(perm) else split
    return moved.reshape(held.shape[0] * held.shape[1], held.shape[2])


def scatter_halves(total, bit, left):
    at = left.index(bit)
    rows, width = total.shape
    split = total.reshape(1 << at, 2, rows >> (at + 1), width)
    return [split[:, i].reshape(rows // 2, width) for i in range(2)], left[:at] + left[at + 1 :]


def local(n, inputs, cotangent, gate_tiles, up_tiles, down_tiles, kept_rows, kept_count):
    blocks, capacity, blk, _ = gate_tiles.shape
    mine, width = inputs.shape
    tokens = mine * n
    bits = [1 << i for i in range(n.bit_length() - 1)]
    smem = pl.BlockSpec(memory_space=pltpu.SMEM)
    vmem = pl.BlockSpec(memory_space=pltpu.VMEM)
    hbm = pl.BlockSpec(memory_space=pltpu.HBM)
    tile_bytes = blocks * capacity * blk * blk * 2

    x_order = bits[::-1]
    dy_order = bits[1:2] + bits[:1:-1] + bits[:1]
    x_held, dy_held = gather_start(inputs, n), gather_start(cotangent, n)
    for i in range(len(bits)):
        x_held = gather_hop(x_held, 1 << i, x_order[i], n)
        dy_held = gather_hop(dy_held, 1 << i, dy_order[i], n)
    x_all = arrange(x_held, x_order, x_order)
    dy_all = arrange(dy_held, dy_order, x_order)

    halves = [
        pltpu.VMEM((tokens // 2, width), jnp.float32),
        pltpu.VMEM((tokens // 2, width), jnp.bfloat16),
    ]
    hidden, d, xpad, dypad, out_keep, out_send, grad_keep, grad_send = pl.pallas_call(
        layer_kernel,
        in_specs=[smem, smem, vmem, vmem, hbm, hbm, hbm],
        out_specs=[vmem] * 8,
        out_shape=[
            pltpu.VMEM((blocks, tokens, blk), jnp.bfloat16),
            pltpu.VMEM((blocks, tokens, 2 * blk), jnp.bfloat16),
            pltpu.VMEM((tokens, width + blk), jnp.bfloat16),
            pltpu.VMEM((tokens, width + blk), jnp.bfloat16),
        ]
        + halves
        + halves,
        scratch_shapes=[
            pltpu.VMEM((tokens, width + blk), jnp.float32),
            pltpu.VMEM((tokens, width + blk), jnp.float32),
            pltpu.VMEM(gate_tiles.shape, jnp.bfloat16),
            pltpu.VMEM(gate_tiles.shape, jnp.bfloat16),
            pltpu.VMEM(gate_tiles.shape, jnp.bfloat16),
            pltpu.SemaphoreType.DMA((3, blocks)),
        ],
        compiler_params=pltpu.CompilerParams(vmem_limit_bytes=44 * 1024 * 1024),
        cost_estimate=pl.CostEstimate(
            flops=12 * tokens * tile_bytes // 2, bytes_accessed=3 * tile_bytes, transcendentals=0
        ),
        name="layer",
    )(kept_rows, kept_count, x_all, dy_all, gate_tiles, up_tiles, down_tiles)

    def grads(kernel, padded, factor, count, name):
        tile = pl.BlockSpec((1, capacity, blk, blk), lambda c: (c, 0, 0, 0))
        return pl.pallas_call(
            kernel,
            grid=(blocks,),
            in_specs=[smem, smem, vmem, vmem],
            out_specs=[tile] * count,
            out_shape=[jax.ShapeDtypeStruct(gate_tiles.shape, jnp.bfloat16)] * count,
            compiler_params=pltpu.CompilerParams(vmem_limit_bytes=16 * 1024 * 1024),
            cost_estimate=pl.CostEstimate(
                flops=2 * count * tokens * tile_bytes // 2,
                bytes_accessed=count * tile_bytes,
                transcendentals=0,
            ),
            name=name,
        )(kept_rows, kept_count, padded, factor)

    (down_grad,) = grads(down_grad_kernel, dypad, hidden, 1, "down_grad")
    gate_grad, up_grad = grads(gate_up_grad_kernel, xpad, d, 2, "gate_up_grad")

    out_hops = bits
    grad_hops = bits[:1] + bits[2:] + bits[1:2]
    chains = [[out_keep, out_send, bits[1:]], [grad_keep, grad_send, bits[1:]]]
    for i in range(len(bits)):
        for chain, hops in zip(chains, (out_hops, grad_hops)):
            keep, send, left = chain
            total = keep + swap(send, hops[i], n).astype(jnp.float32)
            if i + 1 < len(bits):
                (keep, send), left = scatter_halves(total, hops[i + 1], left)
                chain[:] = [keep, send.astype(jnp.bfloat16), left]
            else:
                chain[:] = [total.astype(jnp.bfloat16), None, left]
    return chains[0][0], chains[1][0], gate_grad, up_grad, down_grad


def solution(mesh):
    tiles = P("col", None, None, None)
    tokens = P(("groups", "col"), None)
    grads = P(("groups", "col"), None, None, None)
    return jax.shard_map(
        functools.partial(local, mesh.shape["col"]),
        mesh=mesh,
        in_specs=(tokens, tokens, tiles, tiles, tiles, P("col", None), P("col")),
        out_specs=(tokens, tokens, grads, grads, grads),
        check_vma=False,
    )
```

```python
import functools

import jax
import jax.numpy as jnp
from jax import lax
from jax.experimental import pallas as pl
from jax.experimental.pallas import tpu as pltpu
from jax.sharding import PartitionSpec as P

NT = (((1,), (1,)), ((), ()))
TN = (((0,), (0,)), ((), ()))
CHUNK = 4


def slot_offsets(rows_ref, count_ref, c, dead, blk):
    count = count_ref[c]
    capacity = rows_ref.shape[1]
    return [
        pl.multiple_of(jnp.where(s < count, rows_ref[c, s], dead) * blk, blk)
        for s in range(capacity)
    ]


def add_to_rows(acc, offs, parts, blk):
    old = [acc[:, pl.ds(o, blk)] for o in offs]
    for i, o in enumerate(offs):
        acc[:, pl.ds(o, blk)] = old[i] + parts[:, i * blk : (i + 1) * blk]


def emit_halves(acc, keep_ref, send_ref, width):
    half = keep_ref.shape[0]
    keep_ref[...] = acc[:half, :width]
    send_ref[...] = acc[half:, :width].astype(send_ref.dtype)


def tile_copies(sources, targets, sems, c):
    return [
        pltpu.make_async_copy(src.at[c], dst.at[c], sems.at[i, c])
        for i, (src, dst) in enumerate(zip(sources, targets))
    ]


def padded_copy(pad, values):
    tokens, width = values.shape
    pad[:, :width] = values[...]
    pad[:, width:] = jnp.zeros((tokens, pad.shape[1] - width), pad.dtype)


def pipelined(blocks, inward, outward):
    inward(0)

    def step(c, carry):
        outward(c - 1)
        inward(c)
        return carry

    lax.fori_loop(1, blocks, step, 0)
    outward(blocks - 1)


def forward_kernel(
    rows_ref, count_ref, x_ref, wg_hbm, wu_hbm, wd_hbm,
    wg_ref, wu_ref, wd_ref, gate_ref, up_ref, hidden_ref, xpad_ref, keep_ref, send_ref,
    acc, sems,
):
    width = x_ref.shape[1]
    blocks, capacity, blk, _ = wg_ref.shape
    copies = functools.partial(
        tile_copies, (wg_hbm, wu_hbm, wd_hbm), (wg_ref, wu_ref, wd_ref), sems
    )
    for c in range(blocks):
        for copy in copies(c):
            copy.start()
    padded_copy(xpad_ref, x_ref)
    acc[...] = jnp.zeros_like(acc)

    def inward(c):
        for copy in copies(c):
            copy.wait()
        offs = slot_offsets(rows_ref, count_ref, c, width // blk, blk)
        xg = jnp.concatenate([xpad_ref[:, pl.ds(o, blk)] for o in offs], axis=1)
        w = jnp.concatenate(
            [wg_ref[c].reshape(capacity * blk, blk), wu_ref[c].reshape(capacity * blk, blk)],
            axis=1,
        )
        pre = jnp.dot(xg, w, preferred_element_type=jnp.float32)
        gate, up = pre[:, :blk], pre[:, blk:]
        gate_ref[c] = gate
        up_ref[c] = up
        act = gate * (1.0 / (1.0 + jnp.exp(-gate)))
        hidden_ref[c] = (act * up).astype(jnp.bfloat16)

    def outward(c):
        offs = slot_offsets(rows_ref, count_ref, c, width // blk, blk)
        hidden = hidden_ref[c]
        for s in range(0, capacity, CHUNK):
            wd = jnp.concatenate([wd_ref[c, s + i] for i in range(CHUNK)], axis=1)
            y = jnp.dot(hidden, wd, preferred_element_type=jnp.float32)
            add_to_rows(acc, offs[s : s + CHUNK], y, blk)

    pipelined(blocks, inward, outward)
    emit_halves(acc, keep_ref, send_ref, width)


def backward_kernel(
    rows_ref, count_ref, dy_ref, gate_ref, up_ref, wg_ref, wu_ref, wd_ref,
    d_ref, dypad_ref, keep_ref, send_ref, acc,
):
    width = dy_ref.shape[1]
    blocks, capacity, blk, _ = wg_ref.shape
    padded_copy(dypad_ref, dy_ref)
    acc[...] = jnp.zeros_like(acc)

    def inward(c):
        offs = slot_offsets(rows_ref, count_ref, c, width // blk, blk)
        dyg = jnp.concatenate([dypad_ref[:, pl.ds(o, blk)] for o in offs], axis=1)
        wd = jnp.concatenate([wd_ref[c, s] for s in range(capacity)], axis=1)
        d_hidden = lax.dot_general(dyg, wd, NT, preferred_element_type=jnp.float32)
        gate, up = gate_ref[c], up_ref[c]
        sig = 1.0 / (1.0 + jnp.exp(-gate))
        act = gate * sig
        d_ref[c, :, :blk] = (d_hidden * up * sig * (1.0 + gate * (1.0 - sig))).astype(jnp.bfloat16)
        d_ref[c, :, blk:] = (d_hidden * act).astype(jnp.bfloat16)

    def outward(c):
        offs = slot_offsets(rows_ref, count_ref, c, width // blk, blk)
        d = d_ref[c]
        for s in range(0, capacity, CHUNK):
            w = jnp.concatenate(
                [
                    wg_ref[c, s : s + CHUNK].reshape(CHUNK * blk, blk),
                    wu_ref[c, s : s + CHUNK].reshape(CHUNK * blk, blk),
                ],
                axis=1,
            )
            x_slots = lax.dot_general(d, w, NT, preferred_element_type=jnp.float32)
            add_to_rows(acc, offs[s : s + CHUNK], x_slots, blk)

    pipelined(blocks, inward, outward)
    emit_halves(acc, keep_ref, send_ref, width)


def gate_up_products(pad_ref, d, offs, blk, stages, i):
    for s, o in enumerate(offs):
        full = lax.dot_general(
            pad_ref[:, pl.ds(o, blk)], d, TN, preferred_element_type=jnp.float32
        ).astype(jnp.bfloat16)
        stages[0][i, s] = full[:, :blk]
        stages[1][i, s] = full[:, blk:]


def down_products(pad_ref, hidden, offs, blk, stages, i):
    for s in range(0, len(offs), 2):
        dys = jnp.concatenate([pad_ref[:, pl.ds(o, blk)] for o in offs[s : s + 2]], axis=1)
        full = lax.dot_general(hidden, dys, TN, preferred_element_type=jnp.float32)
        full = full.astype(jnp.bfloat16)
        stages[0][i, s] = full[:, :blk]
        stages[0][i, s + 1] = full[:, blk:]


def grad_kernel(products, first, count, outs, behind, *refs):
    rows_ref, count_ref, pad_ref, factor_ref = refs[:4]
    grad_refs = refs[4 + behind : 4 + behind + outs]
    stages = refs[4 + behind + outs : -1]
    sems = refs[-1]
    blk = stages[0].shape[-1]

    def copies(i):
        return [
            pltpu.make_async_copy(stage.at[i], grad.at[first + i], sems.at[k, i])
            for k, (stage, grad) in enumerate(zip(stages, grad_refs))
        ]

    def step(i, carry):
        offs = slot_offsets(rows_ref, count_ref, first + i, pad_ref.shape[1] // blk - 1, blk)
        products(pad_ref, factor_ref[first + i], offs, blk, stages, i)
        for copy in copies(i):
            copy.start()
        return carry

    lax.fori_loop(0, count, step, 0)
    for i in range(count):
        for copy in copies(i):
            copy.wait()


def seed_kernel(x_ref, dy_ref, x_held, dy_held):
    x_held[0] = x_ref[...]
    dy_held[0] = dy_ref[...]


def swap(value, bit, n):
    return lax.ppermute(value, "col", [(i, i ^ bit) for i in range(n)])


def gather_hop(held, send, size, bit, n):
    return lax.dynamic_update_slice_in_dim(held, swap(send, bit, n), size, 0)


def arrange(held, order, wanted):
    levels = len(order)
    split = held.reshape((2,) * levels + held.shape[1:])
    axis = {bit: levels - 1 - i for i, bit in enumerate(order)}
    perm = [axis[bit] for bit in wanted[::-1]] + [levels, levels + 1]
    moved = split.transpose(perm) if perm != sorted(perm) else split
    return moved.reshape(held.shape[0] * held.shape[1], held.shape[2])


def local(n, inputs, cotangent, gate_tiles, up_tiles, down_tiles, kept_rows, kept_count):
    blocks, capacity, blk, _ = gate_tiles.shape
    mine, width = inputs.shape
    tokens = mine * n
    bits = [1 << i for i in range(n.bit_length() - 1)]
    hops = len(bits)
    smem = pl.BlockSpec(memory_space=pltpu.SMEM)
    vmem = pl.BlockSpec(memory_space=pltpu.VMEM)
    hbm = pl.BlockSpec(memory_space=pltpu.HBM)
    tile_bytes = blocks * capacity * blk * blk * 2
    tiles_in = [pltpu.with_memory_space_constraint(t, pltpu.HBM) for t in (gate_tiles, up_tiles, down_tiles)]

    def cost(products, tiles, part=1.0):
        return pl.CostEstimate(
            flops=int(products * tokens * tile_bytes * part),
            bytes_accessed=int(tiles * tile_bytes * part),
            transcendentals=0,
        )

    x_order = bits[::-1]
    dy_order = bits[1:2] + bits[:1:-1] + bits[:1]
    x_held, dy_held = pl.pallas_call(
        seed_kernel,
        in_specs=[vmem, vmem],
        out_specs=[vmem, vmem],
        out_shape=[pltpu.VMEM((n, mine, width), inputs.dtype)] * 2,
        name="seed",
    )(inputs, cotangent)
    for i in range(hops):
        if i == 0:
            x_held = gather_hop(x_held, inputs[None], 1, x_order[0], n)
            dy_held = gather_hop(dy_held, cotangent[None], 1, dy_order[0], n)
        else:
            x_held = gather_hop(x_held, x_held[: 1 << i], 1 << i, x_order[i], n)
            dy_held = gather_hop(dy_held, dy_held[: 1 << i], 1 << i, dy_order[i], n)
    x_all = arrange(x_held, x_order, x_order)
    dy_all = arrange(dy_held, dy_order, x_order)

    tiles = pltpu.VMEM(gate_tiles.shape, jnp.bfloat16)
    padded = pltpu.VMEM((tokens, width + blk), jnp.bfloat16)
    keep_half = pltpu.VMEM((tokens // 2, width), jnp.float32)
    send_half = pltpu.VMEM((tokens // 2, width), jnp.bfloat16)
    params = pltpu.CompilerParams(vmem_limit_bytes=8 * 1024 * 1024)
    acc = pltpu.VMEM((tokens, width + blk), jnp.float32)
    wg, wu, wd, gate, up, hidden, xpad, out_keep, out_send = pl.pallas_call(
        forward_kernel,
        in_specs=[smem, smem, vmem, hbm, hbm, hbm],
        out_specs=[vmem] * 9,
        out_shape=[tiles] * 3
        + [pltpu.VMEM((blocks, tokens, blk), jnp.float32)] * 2
        + [pltpu.VMEM((blocks, tokens, blk), jnp.bfloat16), padded, keep_half, send_half],
        scratch_shapes=[acc, pltpu.SemaphoreType.DMA((3, blocks))],
        compiler_params=params,
        cost_estimate=cost(3, 3),
        name="forward",
    )(kept_rows, kept_count, x_all, *tiles_in)
    d, dypad, grad_keep, grad_send = pl.pallas_call(
        backward_kernel,
        in_specs=[smem, smem] + [vmem] * 6,
        out_specs=[vmem] * 4,
        out_shape=[
            pltpu.VMEM((blocks, tokens, 2 * blk), jnp.bfloat16),
            padded,
            keep_half,
            send_half,
        ],
        scratch_shapes=[acc],
        compiler_params=params,
        cost_estimate=cost(3, 3),
        name="backward",
    )(kept_rows, kept_count, dy_all, gate, up, wg, wu, wd)

    def grads(products, pad, factor, first, count, outs, earlier, after, name):
        behind = len(earlier) + len(after)
        return pl.pallas_call(
            functools.partial(grad_kernel, products, first, count, outs, behind),
            in_specs=[smem, smem, vmem, vmem] + [hbm] * len(earlier) + [pl.BlockSpec(memory_space=pl.ANY)] * len(after),
            out_specs=[hbm] * outs,
            out_shape=[jax.ShapeDtypeStruct(gate_tiles.shape, jnp.bfloat16)] * outs,
            scratch_shapes=[pltpu.VMEM((count,) + gate_tiles.shape[1:], jnp.bfloat16)] * outs
            + [pltpu.SemaphoreType.DMA((outs, count))],
            input_output_aliases={4 + k: k for k in range(len(earlier))},
            compiler_params=pltpu.CompilerParams(vmem_limit_bytes=24 * 1024 * 1024),
            cost_estimate=cost(outs, outs, count / blocks),
            name=name,
        )(kept_rows, kept_count, pad, factor, *earlier, *after)

    cuts = [0, -(-blocks // 3), -(-2 * blocks // 3), blocks]
    (down_grad,) = grads(down_products, dypad, hidden, 0, blocks, 1, [], [d], "down_grad")
    gate_up = []
    out_total = out_keep + swap(out_send, bits[0], n).astype(jnp.float32)
    grad_total = (grad_keep, grad_send)
    for i in range(hops):
        keep, send = grad_total
        got = swap(send, bits[i], n)
        grad_total = keep + got.astype(jnp.float32)
        if i + 1 < hops:
            half = grad_total.shape[0] // 2
            grad_total = (grad_total[:half], grad_total[half:].astype(jnp.bfloat16))
            half = out_total.shape[0] // 2
            out_total = out_total[:half] + swap(
                out_total[half:].astype(jnp.bfloat16), bits[i + 1], n
            ).astype(jnp.float32)
        if i < 3:
            gate_up = grads(
                gate_up_products, xpad, d, cuts[i], cuts[i + 1] - cuts[i], 2, gate_up, [got],
                "gate_up_grad",
            )
    return (
        out_total.astype(jnp.bfloat16),
        grad_total.astype(jnp.bfloat16),
        gate_up[0],
        gate_up[1],
        down_grad,
    )


def solution(mesh):
    tiles = P("col", None, None, None)
    tokens = P(("groups", "col"), None)
    grads = P(("groups", "col"), None, None, None)
    return jax.shard_map(
        functools.partial(local, mesh.shape["col"]),
        mesh=mesh,
        in_specs=(tokens, tokens, tiles, tiles, tiles, P("col", None), P("col")),
        out_specs=(tokens, tokens, grads, grads, grads),
        check_vma=False,
    )
```

```python
import functools

import jax
import jax.numpy as jnp
from jax import lax
from jax.experimental import pallas as pl
from jax.experimental.pallas import tpu as pltpu
from jax.sharding import PartitionSpec as P

NT = (((1,), (1,)), ((), ()))
TN = (((0,), (0,)), ((), ()))
CHUNK = 4


def offsets_kernel(dead, blk, rows_ref, count_ref, offs_ref):
    blocks, capacity = rows_ref.shape

    def block(c, carry):
        count = count_ref[c]
        for s in range(capacity):
            offs_ref[c, s] = jnp.where(s < count, rows_ref[c, s], dead) * blk
        return carry

    lax.fori_loop(0, blocks, block, 0)


def slot_offsets(offs_ref, c, blk):
    return [pl.multiple_of(offs_ref[c, s], blk) for s in range(offs_ref.shape[1])]


def add_to_rows(acc, offs, parts, blk):
    old = [acc[:, pl.ds(o, blk)] for o in offs]
    for i, o in enumerate(offs):
        acc[:, pl.ds(o, blk)] = old[i] + parts[:, i * blk : (i + 1) * blk]


def emit_halves(acc, keep_ref, send_ref, width):
    half = keep_ref.shape[0]
    keep_ref[...] = acc[:half, :width]
    send_ref[...] = acc[half:, :width].astype(send_ref.dtype)


def tile_copies(sources, targets, sems, c):
    return [
        pltpu.make_async_copy(src.at[c], dst.at[c], sems.at[i, c])
        for i, (src, dst) in enumerate(zip(sources, targets))
    ]


def padded_copy(pad, near, far):
    half, width = near.shape
    pad[:half, :width] = near[...]
    pad[half:, :width] = far[...]
    pad[:, width:] = jnp.zeros((2 * half, pad.shape[1] - width), pad.dtype)


def pipelined(blocks, inward, outward):
    inward(0)

    def step(c, carry):
        outward(c - 1)
        inward(c)
        return carry

    lax.fori_loop(1, blocks, step, 0)
    outward(blocks - 1)


def forward_kernel(
    offs_ref, near_ref, far_ref, wg_hbm, wu_hbm, wd_hbm,
    gate_ref, up_ref, hidden_ref, xpad_ref, keep_ref, send_ref,
    acc, wg_ref, wu_ref, wd_ref, sems,
):
    width = near_ref.shape[1]
    blocks, capacity, blk, _ = wg_ref.shape
    copies = functools.partial(
        tile_copies, (wg_hbm, wu_hbm, wd_hbm), (wg_ref, wu_ref, wd_ref), sems
    )
    for c in range(blocks):
        for copy in copies(c):
            copy.start()
    padded_copy(xpad_ref, near_ref, far_ref)
    acc[...] = jnp.zeros_like(acc)

    def inward(c):
        for copy in copies(c):
            copy.wait()
        offs = slot_offsets(offs_ref, c, blk)
        xg = jnp.concatenate([xpad_ref[:, pl.ds(o, blk)] for o in offs], axis=1)
        w = jnp.concatenate(
            [wg_ref[c].reshape(capacity * blk, blk), wu_ref[c].reshape(capacity * blk, blk)],
            axis=1,
        )
        pre = jnp.dot(xg, w, preferred_element_type=jnp.float32)
        gate, up = pre[:, :blk], pre[:, blk:]
        gate_ref[c] = gate
        up_ref[c] = up
        act = gate * (1.0 / (1.0 + jnp.exp(-gate)))
        hidden_ref[c] = (act * up).astype(jnp.bfloat16)

    def outward(c):
        offs = slot_offsets(offs_ref, c, blk)
        hidden = hidden_ref[c]
        for s in range(0, capacity, CHUNK):
            wd = jnp.concatenate([wd_ref[c, s + i] for i in range(CHUNK)], axis=1)
            y = jnp.dot(hidden, wd, preferred_element_type=jnp.float32)
            add_to_rows(acc, offs[s : s + CHUNK], y, blk)

    pipelined(blocks, inward, outward)
    emit_halves(acc, keep_ref, send_ref, width)


def backward_kernel(
    offs_ref, near_ref, far_ref, gate_ref, up_ref, wg_hbm, wu_hbm, wd_hbm,
    d_ref, dypad_ref, keep_ref, send_ref,
    acc, wg_ref, wu_ref, wd_ref, sems,
):
    width = near_ref.shape[1]
    blocks, capacity, blk, _ = wg_ref.shape
    copies = functools.partial(
        tile_copies, (wg_hbm, wu_hbm, wd_hbm), (wg_ref, wu_ref, wd_ref), sems
    )
    for c in range(blocks):
        for copy in copies(c):
            copy.start()
    padded_copy(dypad_ref, near_ref, far_ref)
    acc[...] = jnp.zeros_like(acc)

    def inward(c):
        for copy in copies(c):
            copy.wait()
        offs = slot_offsets(offs_ref, c, blk)
        dyg = jnp.concatenate([dypad_ref[:, pl.ds(o, blk)] for o in offs], axis=1)
        wd = jnp.concatenate([wd_ref[c, s] for s in range(capacity)], axis=1)
        d_hidden = lax.dot_general(dyg, wd, NT, preferred_element_type=jnp.float32)
        gate, up = gate_ref[c], up_ref[c]
        sig = 1.0 / (1.0 + jnp.exp(-gate))
        act = gate * sig
        d_ref[c, :, :blk] = (d_hidden * up * sig * (1.0 + gate * (1.0 - sig))).astype(jnp.bfloat16)
        d_ref[c, :, blk:] = (d_hidden * act).astype(jnp.bfloat16)

    def outward(c):
        offs = slot_offsets(offs_ref, c, blk)
        d = d_ref[c]
        for s in range(0, capacity, CHUNK):
            w = jnp.concatenate(
                [
                    wg_ref[c, s : s + CHUNK].reshape(CHUNK * blk, blk),
                    wu_ref[c, s : s + CHUNK].reshape(CHUNK * blk, blk),
                ],
                axis=1,
            )
            x_slots = lax.dot_general(d, w, NT, preferred_element_type=jnp.float32)
            add_to_rows(acc, offs[s : s + CHUNK], x_slots, blk)

    pipelined(blocks, inward, outward)
    emit_halves(acc, keep_ref, send_ref, width)


def gate_up_products(pad_ref, d, offs, blk, stages, i):
    for s, o in enumerate(offs):
        full = lax.dot_general(
            pad_ref[:, pl.ds(o, blk)], d, TN, preferred_element_type=jnp.float32
        ).astype(jnp.bfloat16)
        stages[0][i, s] = full[:, :blk]
        stages[1][i, s] = full[:, blk:]


def down_products(pad_ref, hidden, offs, blk, stages, i):
    for s in range(0, len(offs), 2):
        dys = jnp.concatenate([pad_ref[:, pl.ds(o, blk)] for o in offs[s : s + 2]], axis=1)
        full = lax.dot_general(hidden, dys, TN, preferred_element_type=jnp.float32)
        full = full.astype(jnp.bfloat16)
        stages[0][i, s] = full[:, :blk]
        stages[0][i, s + 1] = full[:, blk:]


def grad_kernel(products, first, count, outs, behind, *refs):
    offs_ref, pad_ref, factor_ref = refs[:3]
    grad_refs = refs[3 + behind : 3 + behind + outs]
    stages = refs[3 + behind + outs : -1]
    sems = refs[-1]
    blk = stages[0].shape[-1]

    def copies(i):
        return [
            pltpu.make_async_copy(stage.at[i], grad.at[first + i], sems.at[k, i])
            for k, (stage, grad) in enumerate(zip(stages, grad_refs))
        ]

    def step(i, carry):
        offs = slot_offsets(offs_ref, first + i, blk)
        products(pad_ref, factor_ref[first + i], offs, blk, stages, i)
        for copy in copies(i):
            copy.start()
        return carry

    lax.fori_loop(0, count, step, 0)
    for i in range(count):
        for copy in copies(i):
            copy.wait()


def swap_cores(value, n):
    return lax.ppermute(value, "col", [(i, i ^ 1) for i in range(n)])


def exchange(value, n):
    groups = [list(range(core, n, 2)) for core in range(2)]
    return lax.all_to_all(value, "col", 0, 0, axis_index_groups=groups, tiled=True)


def gather_tokens(value, n):
    mine, width = value.shape
    near = exchange(jnp.broadcast_to(value[None], (n // 2, mine, width)), n)
    far = swap_cores(near, n)
    return near.reshape(n // 2 * mine, width), far.reshape(n // 2 * mine, width)


def scatter_start(keep, send, n):
    got = swap_cores(send, n)
    total = (keep + got.astype(jnp.float32)).astype(jnp.bfloat16)
    return total.reshape(n // 2, keep.shape[0] * 2 // n, keep.shape[1])


def scatter_end(parts):
    return jnp.sum(parts.astype(jnp.float32), axis=0).astype(jnp.bfloat16)


def local(n, inputs, cotangent, gate_tiles, up_tiles, down_tiles, kept_rows, kept_count):
    blocks, capacity, blk, _ = gate_tiles.shape
    mine, width = inputs.shape
    tokens = mine * n
    smem = pl.BlockSpec(memory_space=pltpu.SMEM)
    vmem = pl.BlockSpec(memory_space=pltpu.VMEM)
    hbm = pl.BlockSpec(memory_space=pltpu.HBM)
    tile_bytes = blocks * capacity * blk * blk * 2
    tiles_in = [
        pltpu.with_memory_space_constraint(t, pltpu.HBM) for t in (gate_tiles, up_tiles, down_tiles)
    ]

    def cost(products, tiles, part=1.0):
        return pl.CostEstimate(
            flops=int(products * tokens * tile_bytes * part),
            bytes_accessed=int(tiles * tile_bytes * part),
            transcendentals=0,
        )

    offs = pl.pallas_call(
        functools.partial(offsets_kernel, width // blk, blk),
        in_specs=[smem, smem],
        out_specs=smem,
        out_shape=pltpu.SMEM(kept_rows.shape, jnp.int32),
        name="offsets",
    )(kept_rows, kept_count)
    x_near, x_far = gather_tokens(inputs, n)
    dy_near, dy_far = gather_tokens(cotangent, n)

    padded = pltpu.VMEM((tokens, width + blk), jnp.bfloat16)
    keep_half = pltpu.VMEM((tokens // 2, width), jnp.float32)
    send_half = pltpu.VMEM((tokens // 2, width), jnp.bfloat16)
    params = pltpu.CompilerParams(vmem_limit_bytes=40 * 1024 * 1024)
    scratch = (
        [pltpu.VMEM((tokens, width + blk), jnp.float32)]
        + [pltpu.VMEM(gate_tiles.shape, jnp.bfloat16)] * 3
        + [pltpu.SemaphoreType.DMA((3, blocks))]
    )
    gate, up, hidden, xpad, out_keep, out_send = pl.pallas_call(
        forward_kernel,
        in_specs=[smem, vmem, vmem, hbm, hbm, hbm],
        out_specs=[vmem] * 6,
        out_shape=[pltpu.VMEM((blocks, tokens, blk), jnp.float32)] * 2
        + [pltpu.VMEM((blocks, tokens, blk), jnp.bfloat16), padded, keep_half, send_half],
        scratch_shapes=scratch,
        compiler_params=params,
        cost_estimate=cost(3, 3),
        name="forward",
    )(offs, x_near, x_far, *tiles_in)
    out_parts = exchange(scatter_start(out_keep, out_send, n), n)
    d, dypad, grad_keep, grad_send = pl.pallas_call(
        backward_kernel,
        in_specs=[smem] + [vmem] * 4 + [hbm] * 3,
        out_specs=[vmem] * 4,
        out_shape=[
            pltpu.VMEM((blocks, tokens, 2 * blk), jnp.bfloat16),
            padded,
            keep_half,
            send_half,
        ],
        scratch_shapes=scratch,
        compiler_params=params,
        cost_estimate=cost(3, 3),
        name="backward",
    )(offs, dy_near, dy_far, gate, up, *tiles_in)

    def grads(products, pad, factor, outs, after, name):
        return pl.pallas_call(
            functools.partial(grad_kernel, products, 0, blocks, outs, len(after)),
            in_specs=[smem, vmem, vmem] + [pl.BlockSpec(memory_space=pl.ANY)] * len(after),
            out_specs=[hbm] * outs,
            out_shape=[jax.ShapeDtypeStruct(gate_tiles.shape, jnp.bfloat16)] * outs,
            scratch_shapes=[pltpu.VMEM(gate_tiles.shape, jnp.bfloat16)] * outs
            + [pltpu.SemaphoreType.DMA((outs, blocks))],
            compiler_params=pltpu.CompilerParams(vmem_limit_bytes=24 * 1024 * 1024),
            cost_estimate=cost(outs, outs),
            name=name,
        )(offs, pad, factor, *after)

    (down_grad,) = grads(down_products, dypad, hidden, 1, [d], "down_grad")
    grad_total = scatter_start(grad_keep, grad_send, n)
    grad_parts = exchange(grad_total, n)
    gate_grad, up_grad = grads(gate_up_products, xpad, d, 2, [grad_total], "gate_up_grad")
    return scatter_end(out_parts), scatter_end(grad_parts), gate_grad, up_grad, down_grad


def solution(mesh):
    tiles = P("col", None, None, None)
    tokens = P(("groups", "col"), None)
    grads = P(("groups", "col"), None, None, None)
    return jax.shard_map(
        functools.partial(local, mesh.shape["col"]),
        mesh=mesh,
        in_specs=(tokens, tokens, tiles, tiles, tiles, P("col", None), P("col")),
        out_specs=(tokens, tokens, grads, grads, grads),
        check_vma=False,
    )
```

```python
import functools

import jax
import jax.numpy as jnp
from jax import lax
from jax.experimental import pallas as pl
from jax.experimental.pallas import tpu as pltpu
from jax.sharding import PartitionSpec as P

NT = (((1,), (1,)), ((), ()))
TN = (((0,), (0,)), ((), ()))
CHUNK = 4


def seed_kernel(dead, blk, rows_ref, count_ref, x_ref, dy_ref, offs_ref, x_held, dy_held):
    x_held[0] = x_ref[...]
    dy_held[0] = dy_ref[...]
    blocks, capacity = rows_ref.shape

    def block(c, carry):
        count = count_ref[c]
        for s in range(capacity):
            offs_ref[c, s] = jnp.where(s < count, rows_ref[c, s], dead) * blk
        return carry

    lax.fori_loop(0, blocks, block, 0)


def slot_offsets(offs_ref, c, blk):
    return [pl.multiple_of(offs_ref[c, s], blk) for s in range(offs_ref.shape[1])]


def add_to_rows(acc, offs, parts, blk):
    old = [acc[:, pl.ds(o, blk)] for o in offs]
    for i, o in enumerate(offs):
        acc[:, pl.ds(o, blk)] = old[i] + parts[:, i * blk : (i + 1) * blk]


def tile_copies(sources, targets, sems, c):
    return [
        pltpu.make_async_copy(src.at[c], dst.at[c], sems.at[i, c])
        for i, (src, dst) in enumerate(zip(sources, targets))
    ]


def padded_copy(pad, near, far):
    half, width = near.shape
    pad[:half, :width] = near[...]
    pad[half:, :width] = far[...]
    pad[:, width:] = jnp.zeros((2 * half, pad.shape[1] - width), pad.dtype)


def pipelined(blocks, inward, outward):
    inward(0)

    def step(c, carry):
        outward(c - 1)
        inward(c)
        return carry

    lax.fori_loop(1, blocks, step, 0)
    outward(blocks - 1)


def layer_kernel(
    offs_ref, x_near, x_far, dy_near, dy_far, wg_hbm, wu_hbm, wd_hbm,
    hidden_ref, d_ref, xpad_ref, dypad_ref, keep_ref, send_ref,
    out_acc, grad_acc, wg_ref, wu_ref, wd_ref, sems,
):
    half, width = x_near.shape
    blocks, capacity, blk, _ = wg_ref.shape
    copies = functools.partial(
        tile_copies, (wg_hbm, wu_hbm, wd_hbm), (wg_ref, wu_ref, wd_ref), sems
    )
    for c in range(blocks):
        for copy in copies(c):
            copy.start()
    padded_copy(xpad_ref, x_near, x_far)
    padded_copy(dypad_ref, dy_near, dy_far)
    out_acc[...] = jnp.zeros_like(out_acc)
    grad_acc[...] = jnp.zeros_like(grad_acc)

    def inward(c):
        for copy in copies(c):
            copy.wait()
        offs = slot_offsets(offs_ref, c, blk)
        xg = jnp.concatenate([xpad_ref[:, pl.ds(o, blk)] for o in offs], axis=1)
        w = jnp.concatenate(
            [wg_ref[c].reshape(capacity * blk, blk), wu_ref[c].reshape(capacity * blk, blk)],
            axis=1,
        )
        pre = jnp.dot(xg, w, preferred_element_type=jnp.float32)
        dyg = jnp.concatenate([dypad_ref[:, pl.ds(o, blk)] for o in offs], axis=1)
        wd = jnp.concatenate([wd_ref[c, s] for s in range(capacity)], axis=1)
        d_hidden = lax.dot_general(dyg, wd, NT, preferred_element_type=jnp.float32)
        gate, up = pre[:, :blk], pre[:, blk:]
        sig = 1.0 / (1.0 + jnp.exp(-gate))
        act = gate * sig
        hidden_ref[c] = (act * up).astype(jnp.bfloat16)
        d_ref[c, :, :blk] = (d_hidden * up * sig * (1.0 + gate * (1.0 - sig))).astype(jnp.bfloat16)
        d_ref[c, :, blk:] = (d_hidden * act).astype(jnp.bfloat16)

    def outward(c):
        offs = slot_offsets(offs_ref, c, blk)
        hidden = hidden_ref[c]
        d = d_ref[c]
        for s in range(0, capacity, CHUNK):
            wd = jnp.concatenate([wd_ref[c, s + i] for i in range(CHUNK)], axis=1)
            y = jnp.dot(hidden, wd, preferred_element_type=jnp.float32)
            add_to_rows(out_acc, offs[s : s + CHUNK], y, blk)
            w = jnp.concatenate(
                [
                    wg_ref[c, s : s + CHUNK].reshape(CHUNK * blk, blk),
                    wu_ref[c, s : s + CHUNK].reshape(CHUNK * blk, blk),
                ],
                axis=1,
            )
            x_slots = lax.dot_general(d, w, NT, preferred_element_type=jnp.float32)
            add_to_rows(grad_acc, offs[s : s + CHUNK], x_slots, blk)

    pipelined(blocks, inward, outward)
    for i, acc in enumerate((out_acc, grad_acc)):
        keep_ref[i] = acc[:half, :width]
        send_ref[i] = acc[half:, :width].astype(send_ref.dtype)


def gate_up_products(pad_ref, d, offs, blk, stages, i):
    for s, o in enumerate(offs):
        full = lax.dot_general(
            pad_ref[:, pl.ds(o, blk)], d, TN, preferred_element_type=jnp.float32
        ).astype(jnp.bfloat16)
        stages[0][i, s] = full[:, :blk]
        stages[1][i, s] = full[:, blk:]


def down_products(pad_ref, hidden, offs, blk, stages, i):
    for s in range(0, len(offs), 2):
        dys = jnp.concatenate([pad_ref[:, pl.ds(o, blk)] for o in offs[s : s + 2]], axis=1)
        full = lax.dot_general(hidden, dys, TN, preferred_element_type=jnp.float32)
        full = full.astype(jnp.bfloat16)
        stages[0][i, s] = full[:, :blk]
        stages[0][i, s + 1] = full[:, blk:]


def grad_kernel(products, first, count, outs, behind, *refs):
    offs_ref, pad_ref, factor_ref = refs[:3]
    grad_refs = refs[3 + behind : 3 + behind + outs]
    stages = refs[3 + behind + outs : -1]
    sems = refs[-1]
    blk = stages[0].shape[-1]

    def copies(i):
        return [
            pltpu.make_async_copy(stage.at[i], grad.at[first + i], sems.at[k, i])
            for k, (stage, grad) in enumerate(zip(stages, grad_refs))
        ]

    def step(i, carry):
        offs = slot_offsets(offs_ref, first + i, blk)
        products(pad_ref, factor_ref[first + i], offs, blk, stages, i)
        for copy in copies(i):
            copy.start()
        return carry

    lax.fori_loop(0, count, step, 0)
    for i in range(count):
        for copy in copies(i):
            copy.wait()


def swap(value, bit, n):
    return lax.ppermute(value, "col", [(i, i ^ bit) for i in range(n)])


def gather_hops(held, value, order, n):
    send = value[None]
    for i, bit in enumerate(order):
        if i:
            send = held[: 1 << i]
        held = lax.dynamic_update_slice_in_dim(held, swap(send, bit, n), 1 << i, 0)
    return held


def arrange(held, order, wanted):
    levels = len(order)
    split = held.reshape((2,) * levels + held.shape[1:])
    axis = {bit: levels - 1 - i for i, bit in enumerate(order)}
    perm = [axis[bit] for bit in wanted[::-1]] + [levels, levels + 1]
    moved = split.transpose(perm) if perm != sorted(perm) else split
    return moved.reshape(held.shape[0] * held.shape[1], held.shape[2])


def local(n, inputs, cotangent, gate_tiles, up_tiles, down_tiles, kept_rows, kept_count):
    blocks, capacity, blk, _ = gate_tiles.shape
    mine, width = inputs.shape
    tokens = mine * n
    bits = [1 << i for i in range(n.bit_length() - 1)]
    smem = pl.BlockSpec(memory_space=pltpu.SMEM)
    vmem = pl.BlockSpec(memory_space=pltpu.VMEM)
    hbm = pl.BlockSpec(memory_space=pltpu.HBM)
    tile_bytes = blocks * capacity * blk * blk * 2
    tiles_in = [
        pltpu.with_memory_space_constraint(t, pltpu.HBM) for t in (gate_tiles, up_tiles, down_tiles)
    ]

    def cost(products, tiles, part=1.0):
        return pl.CostEstimate(
            flops=int(products * tokens * tile_bytes * part),
            bytes_accessed=int(tiles * tile_bytes * part),
            transcendentals=0,
        )

    offs, x_held, dy_held = pl.pallas_call(
        functools.partial(seed_kernel, width // blk, blk),
        in_specs=[smem, smem, vmem, vmem],
        out_specs=[smem, vmem, vmem],
        out_shape=[pltpu.SMEM(kept_rows.shape, jnp.int32)]
        + [pltpu.VMEM((n // 2, mine, width), inputs.dtype)] * 2,
        name="seed",
    )(kept_rows, kept_count, inputs, cotangent)
    x_order = bits[:0:-1]
    dy_order = bits[1:2] + bits[:1:-1]
    x_held = gather_hops(x_held, inputs, x_order, n)
    dy_held = gather_hops(dy_held, cotangent, dy_order, n)
    x_near, x_far = [arrange(v, x_order, x_order) for v in (x_held, swap(x_held, 1, n))]
    dy_near, dy_far = [arrange(v, dy_order, x_order) for v in (dy_held, swap(dy_held, 1, n))]

    padded = pltpu.VMEM((tokens, width + blk), jnp.bfloat16)
    acc = pltpu.VMEM((tokens, width + blk), jnp.float32)
    hidden, d, xpad, dypad, keep, send = pl.pallas_call(
        layer_kernel,
        in_specs=[smem] + [vmem] * 4 + [hbm] * 3,
        out_specs=[vmem] * 6,
        out_shape=[
            pltpu.VMEM((blocks, tokens, blk), jnp.bfloat16),
            pltpu.VMEM((blocks, tokens, 2 * blk), jnp.bfloat16),
            padded,
            padded,
            pltpu.VMEM((2, tokens // 2, width), jnp.float32),
            pltpu.VMEM((2, tokens // 2, width), jnp.bfloat16),
        ],
        scratch_shapes=[acc, acc]
        + [pltpu.VMEM(gate_tiles.shape, jnp.bfloat16)] * 3
        + [pltpu.SemaphoreType.DMA((3, blocks))],
        compiler_params=pltpu.CompilerParams(vmem_limit_bytes=40 * 1024 * 1024),
        cost_estimate=cost(6, 3),
        name="layer",
    )(offs, x_near, x_far, dy_near, dy_far, *tiles_in)

    def grads(products, pad, factor, first, count, outs, earlier, after, name):
        behind = len(earlier) + len(after)
        return pl.pallas_call(
            functools.partial(grad_kernel, products, first, count, outs, behind),
            in_specs=[smem, vmem, vmem]
            + [hbm] * len(earlier)
            + [pl.BlockSpec(memory_space=pl.ANY)] * len(after),
            out_specs=[hbm] * outs,
            out_shape=[jax.ShapeDtypeStruct(gate_tiles.shape, jnp.bfloat16)] * outs,
            scratch_shapes=[pltpu.VMEM((count,) + gate_tiles.shape[1:], jnp.bfloat16)] * outs
            + [pltpu.SemaphoreType.DMA((outs, count))],
            input_output_aliases={3 + k: k for k in range(len(earlier))},
            compiler_params=pltpu.CompilerParams(vmem_limit_bytes=24 * 1024 * 1024),
            cost_estimate=cost(outs, outs, count / blocks),
            name=name,
        )(offs, pad, factor, *earlier, *after)

    third = -(-blocks // 3)
    cuts = {0: (0, third), 2: (third, 2 * third), 3: (2 * third, blocks)}
    gate_up, down_grad, after = [], None, []
    for i, bit in enumerate(bits):
        got = swap(send, bit, n)
        done = []
        if i == 1:
            (down_grad,) = grads(
                down_products, dypad, hidden, 0, blocks, 1, [], after, "down_grad"
            )
            done = [down_grad]
        elif i in cuts:
            first, last = cuts[i]
            gate_up = grads(
                gate_up_products, xpad, d, first, last - first, 2, gate_up, after, "gate_up_grad"
            )
            done = gate_up
        total = keep + got.astype(jnp.float32)
        if i + 1 < len(bits):
            half = total.shape[1] // 2
            keep, send = total[:, :half], total[:, half:].astype(jnp.bfloat16)
            send, done = lax.optimization_barrier((send, done))
            after = [send]
            if i == 1:
                (down_grad,) = done
            elif i in cuts:
                gate_up = done
    total = total.astype(jnp.bfloat16)
    return total[0], total[1], gate_up[0], gate_up[1], down_grad


def solution(mesh):
    tiles = P("col", None, None, None)
    tokens = P(("groups", "col"), None)
    grads = P(("groups", "col"), None, None, None)
    return jax.shard_map(
        functools.partial(local, mesh.shape["col"]),
        mesh=mesh,
        in_specs=(tokens, tokens, tiles, tiles, tiles, P("col", None), P("col")),
        out_specs=(tokens, tokens, grads, grads, grads),
        check_vma=False,
    )
```

```python
import functools

import jax
import jax.numpy as jnp
from jax import lax
from jax.experimental import pallas as pl
from jax.experimental.pallas import tpu as pltpu
from jax.sharding import PartitionSpec as P

TN = (((0,), (0,)), ((), ()))
CHUNK = 4


def seed_kernel(dead, blk, rows_ref, count_ref, x_ref, dy_ref, offs_ref, x_held, dy_held):
    x_held[0] = x_ref[...]
    dy_held[0] = dy_ref[...]
    blocks, capacity = rows_ref.shape

    def block(c, carry):
        count = count_ref[c]
        for s in range(capacity):
            offs_ref[c, s] = jnp.where(s < count, rows_ref[c, s], dead) * blk
        return carry

    lax.fori_loop(0, blocks, block, 0)


def slot_offsets(offs_ref, c, blk):
    return [pl.multiple_of(offs_ref[c, s], blk) for s in range(offs_ref.shape[1])]


def add_to_rows(acc, offs, parts, blk):
    old = [acc[:, pl.ds(o, blk)] for o in offs]
    for i, o in enumerate(offs):
        acc[:, pl.ds(o, blk)] = old[i] + parts[:, i * blk : (i + 1) * blk]


def tile_copies(sources, targets, sems, c):
    return [
        pltpu.make_async_copy(src.at[c], dst.at[c], sems.at[i, c])
        for i, (src, dst) in enumerate(zip(sources, targets))
    ]


def padded_copy(pad, near, far):
    half, width = near.shape
    pad[:half, :width] = near[...]
    pad[half:, :width] = far[...]
    pad[:, width:] = jnp.zeros((2 * half, pad.shape[1] - width), pad.dtype)


def pipelined(blocks, inward, outward):
    inward(0)

    def step(c, carry):
        outward(c - 1)
        inward(c)
        return carry

    lax.fori_loop(1, blocks, step, 0)
    outward(blocks - 1)


def layer_kernel(
    offs_ref, x_near, x_far, dy_near, dy_far, wg_hbm, wu_hbm, wd_hbm,
    hidden_ref, d_ref, xpad_ref, dypad_ref, keep_ref, send_ref,
    out_acc, grad_acc_t, dy_t, wg_ref, wu_ref, wd_ref, sems,
):
    half, width = x_near.shape
    blocks, capacity, blk, _ = wg_ref.shape
    copies = functools.partial(
        tile_copies, (wg_hbm, wu_hbm, wd_hbm), (wg_ref, wu_ref, wd_ref), sems
    )
    for c in range(blocks):
        for copy in copies(c):
            copy.start()
    padded_copy(xpad_ref, x_near, x_far)
    padded_copy(dypad_ref, dy_near, dy_far)
    out_acc[...] = jnp.zeros_like(out_acc)
    grad_acc_t[...] = jnp.zeros_like(grad_acc_t)
    for o in range(0, width + blk, blk):
        dy_t[o : o + blk] = dypad_ref[:, o : o + blk].T

    def inward(c):
        for copy in copies(c):
            copy.wait()
        offs = slot_offsets(offs_ref, c, blk)
        xg = jnp.concatenate([xpad_ref[:, pl.ds(o, blk)] for o in offs], axis=1)
        w = jnp.concatenate(
            [wg_ref[c].reshape(capacity * blk, blk), wu_ref[c].reshape(capacity * blk, blk)],
            axis=1,
        )
        pre = jnp.dot(xg, w, preferred_element_type=jnp.float32)
        dyg = jnp.concatenate([dy_t[pl.ds(o, blk)] for o in offs], axis=0)
        wd = jnp.concatenate([wd_ref[c, s] for s in range(capacity)], axis=1)
        d_hidden = jnp.dot(wd, dyg, preferred_element_type=jnp.float32).T
        gate, up = pre[:, :blk], pre[:, blk:]
        sig = 1.0 / (1.0 + jnp.exp(-gate))
        act = gate * sig
        hidden_ref[c] = (act * up).astype(jnp.bfloat16)
        d_ref[c, :, :blk] = (d_hidden * up * sig * (1.0 + gate * (1.0 - sig))).astype(jnp.bfloat16)
        d_ref[c, :, blk:] = (d_hidden * act).astype(jnp.bfloat16)

    def outward(c):
        offs = slot_offsets(offs_ref, c, blk)
        hidden = hidden_ref[c]
        d_t = d_ref[c].T
        for s in range(0, capacity, CHUNK):
            wd = jnp.concatenate([wd_ref[c, s + i] for i in range(CHUNK)], axis=1)
            y = jnp.dot(hidden, wd, preferred_element_type=jnp.float32)
            add_to_rows(out_acc, offs[s : s + CHUNK], y, blk)
            w = jnp.concatenate(
                [
                    wg_ref[c, s : s + CHUNK].reshape(CHUNK * blk, blk),
                    wu_ref[c, s : s + CHUNK].reshape(CHUNK * blk, blk),
                ],
                axis=1,
            )
            x_slots = jnp.dot(w, d_t, preferred_element_type=jnp.float32)
            for i, o in enumerate(offs[s : s + CHUNK]):
                grad_acc_t[pl.ds(o, blk)] += x_slots[i * blk : (i + 1) * blk]

    pipelined(blocks, inward, outward)
    keep_ref[0] = out_acc[:half, :width]
    send_ref[0] = out_acc[half:, :width].astype(send_ref.dtype)
    for o in range(0, width, blk):
        turned = grad_acc_t[o : o + blk].T
        keep_ref[1, :, o : o + blk] = turned[:half]
        send_ref[1, :, o : o + blk] = turned[half:].astype(send_ref.dtype)


def gate_up_products(pad_ref, d, offs, blk, stages, i):
    for s, o in enumerate(offs):
        full = lax.dot_general(
            pad_ref[:, pl.ds(o, blk)], d, TN, preferred_element_type=jnp.float32
        ).astype(jnp.bfloat16)
        stages[0][i, s] = full[:, :blk]
        stages[1][i, s] = full[:, blk:]


def down_products(pad_ref, hidden, offs, blk, stages, i):
    for s in range(0, len(offs), 2):
        dys = jnp.concatenate([pad_ref[:, pl.ds(o, blk)] for o in offs[s : s + 2]], axis=1)
        full = lax.dot_general(hidden, dys, TN, preferred_element_type=jnp.float32)
        full = full.astype(jnp.bfloat16)
        stages[0][i, s] = full[:, :blk]
        stages[0][i, s + 1] = full[:, blk:]


def grad_kernel(products, first, count, outs, behind, *refs):
    offs_ref, pad_ref, factor_ref = refs[:3]
    grad_refs = refs[3 + behind : 3 + behind + outs]
    stages = refs[3 + behind + outs : -1]
    sems = refs[-1]
    blk = stages[0].shape[-1]

    def copies(i):
        return [
            pltpu.make_async_copy(stage.at[i], grad.at[first + i], sems.at[k, i])
            for k, (stage, grad) in enumerate(zip(stages, grad_refs))
        ]

    def step(i, carry):
        offs = slot_offsets(offs_ref, first + i, blk)
        products(pad_ref, factor_ref[first + i], offs, blk, stages, i)
        for copy in copies(i):
            copy.start()
        return carry

    lax.fori_loop(0, count, step, 0)
    for i in range(count):
        for copy in copies(i):
            copy.wait()


def swap(value, bit, n):
    return lax.ppermute(value, "col", [(i, i ^ bit) for i in range(n)])


def gather_hops(held, value, order, n):
    send = value[None]
    for i, bit in enumerate(order):
        if i:
            send = held[: 1 << i]
        held = lax.dynamic_update_slice_in_dim(held, swap(send, bit, n), 1 << i, 0)
    return held


def arrange(held, order, wanted):
    levels = len(order)
    split = held.reshape((2,) * levels + held.shape[1:])
    axis = {bit: levels - 1 - i for i, bit in enumerate(order)}
    perm = [axis[bit] for bit in wanted[::-1]] + [levels, levels + 1]
    moved = split.transpose(perm) if perm != sorted(perm) else split
    return moved.reshape(held.shape[0] * held.shape[1], held.shape[2])


def local(n, inputs, cotangent, gate_tiles, up_tiles, down_tiles, kept_rows, kept_count):
    blocks, capacity, blk, _ = gate_tiles.shape
    mine, width = inputs.shape
    tokens = mine * n
    bits = [1 << i for i in range(n.bit_length() - 1)]
    smem = pl.BlockSpec(memory_space=pltpu.SMEM)
    vmem = pl.BlockSpec(memory_space=pltpu.VMEM)
    hbm = pl.BlockSpec(memory_space=pltpu.HBM)
    tile_bytes = blocks * capacity * blk * blk * 2
    tiles_in = [
        pltpu.with_memory_space_constraint(t, pltpu.HBM) for t in (gate_tiles, up_tiles, down_tiles)
    ]

    def cost(products, tiles, part=1.0):
        return pl.CostEstimate(
            flops=int(products * tokens * tile_bytes * part),
            bytes_accessed=int(tiles * tile_bytes * part),
            transcendentals=0,
        )

    offs, x_held, dy_held = pl.pallas_call(
        functools.partial(seed_kernel, width // blk, blk),
        in_specs=[smem, smem, vmem, vmem],
        out_specs=[smem, vmem, vmem],
        out_shape=[pltpu.SMEM(kept_rows.shape, jnp.int32)]
        + [pltpu.VMEM((n // 2, mine, width), inputs.dtype)] * 2,
        name="seed",
    )(kept_rows, kept_count, inputs, cotangent)
    x_order = bits[:0:-1]
    dy_order = bits[1:2] + bits[:1:-1]
    x_held = gather_hops(x_held, inputs, x_order, n)
    dy_held = gather_hops(dy_held, cotangent, dy_order, n)
    x_near, x_far = [arrange(v, x_order, x_order) for v in (x_held, swap(x_held, 1, n))]
    dy_near, dy_far = [arrange(v, dy_order, x_order) for v in (dy_held, swap(dy_held, 1, n))]

    padded = pltpu.VMEM((tokens, width + blk), jnp.bfloat16)
    acc = pltpu.VMEM((tokens, width + blk), jnp.float32)
    hidden, d, xpad, dypad, keep, send = pl.pallas_call(
        layer_kernel,
        in_specs=[smem] + [vmem] * 4 + [hbm] * 3,
        out_specs=[vmem] * 6,
        out_shape=[
            pltpu.VMEM((blocks, tokens, blk), jnp.bfloat16),
            pltpu.VMEM((blocks, tokens, 2 * blk), jnp.bfloat16),
            padded,
            padded,
            pltpu.VMEM((2, tokens // 2, width), jnp.float32),
            pltpu.VMEM((2, tokens // 2, width), jnp.bfloat16),
        ],
        scratch_shapes=[
            acc,
            pltpu.VMEM((width + blk, tokens), jnp.float32),
            pltpu.VMEM((width + blk, tokens), jnp.bfloat16),
        ]
        + [pltpu.VMEM(gate_tiles.shape, jnp.bfloat16)] * 3
        + [pltpu.SemaphoreType.DMA((3, blocks))],
        compiler_params=pltpu.CompilerParams(vmem_limit_bytes=44 * 1024 * 1024),
        cost_estimate=cost(6, 3),
        name="layer",
    )(offs, x_near, x_far, dy_near, dy_far, *tiles_in)

    def grads(products, pad, factor, first, count, outs, earlier, after, name):
        behind = len(earlier) + len(after)
        return pl.pallas_call(
            functools.partial(grad_kernel, products, first, count, outs, behind),
            in_specs=[smem, vmem, vmem]
            + [hbm] * len(earlier)
            + [pl.BlockSpec(memory_space=pl.ANY)] * len(after),
            out_specs=[hbm] * outs,
            out_shape=[jax.ShapeDtypeStruct(gate_tiles.shape, jnp.bfloat16)] * outs,
            scratch_shapes=[pltpu.VMEM((count,) + gate_tiles.shape[1:], jnp.bfloat16)] * outs
            + [pltpu.SemaphoreType.DMA((outs, count))],
            input_output_aliases={3 + k: k for k in range(len(earlier))},
            compiler_params=pltpu.CompilerParams(vmem_limit_bytes=24 * 1024 * 1024),
            cost_estimate=cost(outs, outs, count / blocks),
            name=name,
        )(offs, pad, factor, *earlier, *after)

    third = -(-blocks // 3)
    cuts = {0: (0, third), 2: (third, 2 * third), 3: (2 * third, blocks)}
    gate_up, down_grad, after = [], None, []
    for i, bit in enumerate(bits):
        got = swap(send, bit, n)
        done = []
        if i == 1:
            (down_grad,) = grads(
                down_products, dypad, hidden, 0, blocks, 1, [], after, "down_grad"
            )
            done = [down_grad]
        elif i in cuts:
            first, last = cuts[i]
            gate_up = grads(
                gate_up_products, xpad, d, first, last - first, 2, gate_up, after, "gate_up_grad"
            )
            done = gate_up
        total = keep + got.astype(jnp.float32)
        if i + 1 < len(bits):
            half = total.shape[1] // 2
            keep, send = total[:, :half], total[:, half:].astype(jnp.bfloat16)
            send, done = lax.optimization_barrier((send, done))
            after = [send]
            if i == 1:
                (down_grad,) = done
            elif i in cuts:
                gate_up = done
    total = total.astype(jnp.bfloat16)
    return total[0], total[1], gate_up[0], gate_up[1], down_grad


def solution(mesh):
    tiles = P("col", None, None, None)
    tokens = P(("groups", "col"), None)
    grads = P(("groups", "col"), None, None, None)
    return jax.shard_map(
        functools.partial(local, mesh.shape["col"]),
        mesh=mesh,
        in_specs=(tokens, tokens, tiles, tiles, tiles, P("col", None), P("col")),
        out_specs=(tokens, tokens, grads, grads, grads),
        check_vma=False,
    )
```

```python
import functools

import jax
import jax.numpy as jnp
from jax import lax
from jax.experimental import pallas as pl
from jax.experimental.pallas import tpu as pltpu
from jax.sharding import PartitionSpec as P

NT = (((1,), (1,)), ((), ()))
TN = (((0,), (0,)), ((), ()))
CHUNK = 4


def seed_kernel(x_ref, dy_ref, held):
    held[0, 0] = x_ref[...]
    held[0, 1] = dy_ref[...]


def offsets_kernel(dead, blk, rows_ref, count_ref, offs_ref):
    blocks, capacity = rows_ref.shape

    def block(c, carry):
        count = count_ref[c]
        for s in range(capacity):
            offs_ref[c, s] = jnp.where(s < count, rows_ref[c, s], dead) * blk
        return carry

    lax.fori_loop(0, blocks, block, 0)


def slot_offsets(offs_ref, c, blk):
    return [pl.multiple_of(offs_ref[c, s], blk) for s in range(offs_ref.shape[1])]


def add_to_rows(acc, offs, parts, blk):
    old = [acc[:, pl.ds(o, blk)] for o in offs]
    for i, o in enumerate(offs):
        acc[:, pl.ds(o, blk)] = old[i] + parts[:, i * blk : (i + 1) * blk]


def tile_copies(sources, targets, sems, c):
    return [
        pltpu.make_async_copy(src.at[c], dst.at[c], sems.at[i, c])
        for i, (src, dst) in enumerate(zip(sources, targets))
    ]


def padded_copy(pad, near, far):
    half, width = near.shape
    pad[:half, :width] = near[...]
    pad[half:, :width] = far[...]
    pad[:, width:] = jnp.zeros((2 * half, pad.shape[1] - width), pad.dtype)


def pipelined(blocks, group, arrived, inward, outward):
    for c in range(group):
        arrived(c)
        inward(c)

    def step(g, carry):
        for i in range(group):
            arrived(g * group + i)
        for i in range(group):
            outward((g - 1) * group + i)
        for i in range(group):
            inward(g * group + i)
        return carry

    lax.fori_loop(1, blocks // group, step, 0)
    for c in range(blocks - group, blocks):
        outward(c)


def layer_kernel(
    offs_ref, x_near, x_far, dy_near, dy_far, wg_hbm, wu_hbm, wd_hbm,
    hidden_ref, d_ref, xpad_ref, dypad_ref, keep_ref, send_ref,
    out_acc, grad_acc, wg_ref, wu_ref, wd_ref, sems,
):
    half, width = x_near.shape
    blocks, capacity, blk, _ = wg_ref.shape
    copies = functools.partial(
        tile_copies, (wg_hbm, wu_hbm, wd_hbm), (wg_ref, wu_ref, wd_ref), sems
    )
    for c in range(blocks):
        for copy in copies(c):
            copy.start()
    padded_copy(xpad_ref, x_near, x_far)
    padded_copy(dypad_ref, dy_near, dy_far)
    out_acc[...] = jnp.zeros_like(out_acc)
    grad_acc[...] = jnp.zeros_like(grad_acc)

    def arrived(c):
        for copy in copies(c):
            copy.wait()

    def inward(c):
        offs = slot_offsets(offs_ref, c, blk)
        xg = jnp.concatenate([xpad_ref[:, pl.ds(o, blk)] for o in offs], axis=1)
        w = jnp.concatenate(
            [wg_ref[c].reshape(capacity * blk, blk), wu_ref[c].reshape(capacity * blk, blk)],
            axis=1,
        )
        pre = jnp.dot(xg, w, preferred_element_type=jnp.float32)
        dyg = jnp.concatenate([dypad_ref[:, pl.ds(o, blk)] for o in offs], axis=1)
        wd = jnp.concatenate([wd_ref[c, s] for s in range(capacity)], axis=1)
        d_hidden = lax.dot_general(dyg, wd, NT, preferred_element_type=jnp.float32)
        gate, up = pre[:, :blk], pre[:, blk:]
        sig = 1.0 / (1.0 + jnp.exp(-gate))
        act = gate * sig
        hidden_ref[c] = (act * up).astype(jnp.bfloat16)
        d_ref[c, :, :blk] = (d_hidden * up * sig * (1.0 + gate * (1.0 - sig))).astype(jnp.bfloat16)
        d_ref[c, :, blk:] = (d_hidden * act).astype(jnp.bfloat16)

    def outward(c):
        offs = slot_offsets(offs_ref, c, blk)
        hidden = hidden_ref[c]
        d = d_ref[c]
        for s in range(0, capacity, CHUNK):
            wd = jnp.concatenate([wd_ref[c, s + i] for i in range(CHUNK)], axis=1)
            y = jnp.dot(hidden, wd, preferred_element_type=jnp.float32)
            add_to_rows(out_acc, offs[s : s + CHUNK], y, blk)
            w = jnp.concatenate(
                [
                    wg_ref[c, s : s + CHUNK].reshape(CHUNK * blk, blk),
                    wu_ref[c, s : s + CHUNK].reshape(CHUNK * blk, blk),
                ],
                axis=1,
            )
            x_slots = lax.dot_general(d, w, NT, preferred_element_type=jnp.float32)
            add_to_rows(grad_acc, offs[s : s + CHUNK], x_slots, blk)

    pipelined(blocks, 2 if blocks % 2 == 0 else 1, arrived, inward, outward)
    for i, acc in enumerate((out_acc, grad_acc)):
        keep_ref[i] = acc[:half, :width]
        send_ref[i] = acc[half:, :width].astype(send_ref.dtype)


def gate_up_products(pad_ref, d, offs, slots, blk, stages, i):
    for s in slots:
        full = lax.dot_general(
            pad_ref[:, pl.ds(offs[s], blk)], d, TN, preferred_element_type=jnp.float32
        ).astype(jnp.bfloat16)
        stages[0][i, s] = full[:, :blk]
        stages[1][i, s] = full[:, blk:]


def down_products(pad_ref, hidden, offs, slots, blk, stages, i):
    for s in slots[::2]:
        dys = jnp.concatenate([pad_ref[:, pl.ds(o, blk)] for o in offs[s : s + 2]], axis=1)
        full = lax.dot_general(hidden, dys, TN, preferred_element_type=jnp.float32)
        full = full.astype(jnp.bfloat16)
        stages[0][i, s] = full[:, :blk]
        stages[0][i, s + 1] = full[:, blk:]


def grad_kernel(products, first, count, outs, behind, *refs):
    offs_ref, pad_ref, factor_ref = refs[:3]
    grad_refs = refs[3 + behind : 3 + behind + outs]
    stages = refs[3 + behind + outs : -1]
    sems = refs[-1]
    capacity, blk = stages[0].shape[1], stages[0].shape[-1]
    half = capacity // 2

    def copies(i, h):
        part = pl.ds(h * half, half)
        return [
            pltpu.make_async_copy(stage.at[i, part], grad.at[first + i, part], sems.at[k, i, h])
            for k, (stage, grad) in enumerate(zip(stages, grad_refs))
        ]

    def step(i, carry):
        offs = slot_offsets(offs_ref, first + i, blk)
        factor = factor_ref[first + i]
        for h in range(2):
            products(pad_ref, factor, offs, range(h * half, (h + 1) * half), blk, stages, i)
            for copy in copies(i, h):
                copy.start()
        return carry

    lax.fori_loop(0, count, step, 0)
    for i in range(count):
        for h in range(2):
            for copy in copies(i, h):
                copy.wait()


def hop_orders(n):
    bits = [1 << i for i in range(1, n.bit_length() - 1)]
    return bits[::-1], bits[:1] + bits[:0:-1]


def hop(value, i, n):
    orders = hop_orders(n)
    return lax.ppermute(value, "col", [(j, j ^ orders[j % 2][i]) for j in range(n)])


def swap_cores(value, n):
    return lax.ppermute(value, "col", [(j, j ^ 1) for j in range(n)])


def local(n, inputs, cotangent, gate_tiles, up_tiles, down_tiles, kept_rows, kept_count):
    blocks, capacity, blk, _ = gate_tiles.shape
    mine, width = inputs.shape
    tokens = mine * n
    hops = n.bit_length() - 2
    smem = pl.BlockSpec(memory_space=pltpu.SMEM)
    vmem = pl.BlockSpec(memory_space=pltpu.VMEM)
    hbm = pl.BlockSpec(memory_space=pltpu.HBM)
    tile_bytes = blocks * capacity * blk * blk * 2
    tiles_in = [
        pltpu.with_memory_space_constraint(t, pltpu.HBM) for t in (gate_tiles, up_tiles, down_tiles)
    ]

    def cost(products, tiles, part=1.0):
        return pl.CostEstimate(
            flops=int(products * tokens * tile_bytes * part),
            bytes_accessed=int(tiles * tile_bytes * part),
            transcendentals=0,
        )

    held = pl.pallas_call(
        seed_kernel,
        in_specs=[vmem, vmem],
        out_specs=vmem,
        out_shape=pltpu.VMEM((n // 2, 2, mine, width), inputs.dtype),
        name="seed",
    )(inputs, cotangent)
    offs = pl.pallas_call(
        functools.partial(offsets_kernel, width // blk, blk),
        in_specs=[smem, smem],
        out_specs=smem,
        out_shape=pltpu.SMEM(kept_rows.shape, jnp.int32),
        name="offsets",
    )(kept_rows, kept_count)
    for i in range(hops):
        if i == 0:
            for k, value in enumerate((inputs, cotangent)):
                held = lax.dynamic_update_slice(held, hop(value, 0, n)[None, None], (1, k, 0, 0))
        else:
            size = 1 << i
            held = lax.dynamic_update_slice_in_dim(held, hop(held[:size], i, n), size, 0)
    other = swap_cores(held, n)
    half = n // 2 * mine
    x_near, dy_near = [held[:, k].reshape(half, width) for k in range(2)]
    x_far, dy_far = [other[:, k].reshape(half, width) for k in range(2)]

    padded = pltpu.VMEM((tokens, width + blk), jnp.bfloat16)
    acc = pltpu.VMEM((tokens, width + blk), jnp.float32)
    hidden, d, xpad, dypad, keep, send = pl.pallas_call(
        layer_kernel,
        in_specs=[smem] + [vmem] * 4 + [hbm] * 3,
        out_specs=[vmem] * 6,
        out_shape=[
            pltpu.VMEM((blocks, tokens, blk), jnp.bfloat16),
            pltpu.VMEM((blocks, tokens, 2 * blk), jnp.bfloat16),
            padded,
            padded,
            pltpu.VMEM((2, tokens // 2, width), jnp.float32),
            pltpu.VMEM((2, tokens // 2, width), jnp.bfloat16),
        ],
        scratch_shapes=[acc, acc]
        + [pltpu.VMEM(gate_tiles.shape, jnp.bfloat16)] * 3
        + [pltpu.SemaphoreType.DMA((3, blocks))],
        compiler_params=pltpu.CompilerParams(vmem_limit_bytes=40 * 1024 * 1024),
        cost_estimate=cost(6, 3),
        name="layer",
    )(offs, x_near, x_far, dy_near, dy_far, *tiles_in)

    def grads(products, pad, factor, first, count, outs, earlier, after, name):
        behind = len(earlier) + len(after)
        return pl.pallas_call(
            functools.partial(grad_kernel, products, first, count, outs, behind),
            in_specs=[smem, vmem, vmem]
            + [hbm] * len(earlier)
            + [pl.BlockSpec(memory_space=pl.ANY)] * len(after),
            out_specs=[hbm] * outs,
            out_shape=[jax.ShapeDtypeStruct(gate_tiles.shape, jnp.bfloat16)] * outs,
            scratch_shapes=[pltpu.VMEM((count,) + gate_tiles.shape[1:], jnp.bfloat16)] * outs
            + [pltpu.SemaphoreType.DMA((outs, count, 2))],
            input_output_aliases={3 + k: k for k in range(len(earlier))},
            compiler_params=pltpu.CompilerParams(vmem_limit_bytes=24 * 1024 * 1024),
            cost_estimate=cost(outs, outs, count / blocks),
            name=name,
        )(offs, pad, factor, *earlier, *after)

    third = -(-blocks // 3)
    cuts = {0: (0, third), 2: (third, 2 * third), 3: (2 * third, blocks)}
    gate_up, down_grad, after = [], None, []
    for i in range(hops + 1):
        got = hop(send, hops - i, n) if i else swap_cores(send, n)
        done = []
        if i == 1:
            (down_grad,) = grads(
                down_products, dypad, hidden, 0, blocks, 1, [], after, "down_grad"
            )
            done = [down_grad]
        elif i in cuts:
            first, last = cuts[i]
            gate_up = grads(
                gate_up_products, xpad, d, first, last - first, 2, gate_up, after, "gate_up_grad"
            )
            done = gate_up
        total = keep + got.astype(jnp.float32)
        if i < hops:
            half = total.shape[1] // 2
            keep, send = total[:, :half], total[:, half:].astype(jnp.bfloat16)
            send, done = lax.optimization_barrier((send, done))
            after = [send]
            if i == 1:
                (down_grad,) = done
            elif i in cuts:
                gate_up = done
    total = total.astype(jnp.bfloat16)
    return total[0], total[1], gate_up[0], gate_up[1], down_grad


def solution(mesh):
    tiles = P("col", None, None, None)
    tokens = P(("groups", "col"), None)
    grads = P(("groups", "col"), None, None, None)
    return jax.shard_map(
        functools.partial(local, mesh.shape["col"]),
        mesh=mesh,
        in_specs=(tokens, tokens, tiles, tiles, tiles, P("col", None), P("col")),
        out_specs=(tokens, tokens, grads, grads, grads),
        check_vma=False,
    )
```

```python
import functools

import jax
import jax.numpy as jnp
from jax import lax
from jax.experimental import pallas as pl
from jax.experimental.pallas import tpu as pltpu
from jax.sharding import PartitionSpec as P

NT = (((1,), (1,)), ((), ()))
TN = (((0,), (0,)), ((), ()))
CHUNK = 4


def seed_kernel(x_ref, dy_ref, x_held, dy_held):
    x_held[0] = x_ref[...]
    dy_held[0] = dy_ref[...]


def offsets_kernel(dead, blk, rows_ref, count_ref, offs_ref):
    blocks, capacity = rows_ref.shape

    def block(c, carry):
        count = count_ref[c]
        for s in range(capacity):
            offs_ref[c, s] = jnp.where(s < count, rows_ref[c, s], dead) * blk
        return carry

    lax.fori_loop(0, blocks, block, 0)


def slot_offsets(offs_ref, c, blk):
    return [pl.multiple_of(offs_ref[c, s], blk) for s in range(offs_ref.shape[1])]


def add_to_rows(acc, offs, parts, blk):
    old = [acc[:, pl.ds(o, blk)] for o in offs]
    for i, o in enumerate(offs):
        acc[:, pl.ds(o, blk)] = old[i] + parts[:, i * blk : (i + 1) * blk]


def tile_copies(sources, targets, sems, c):
    return [
        pltpu.make_async_copy(src.at[c], dst.at[c], sems.at[i, c])
        for i, (src, dst) in enumerate(zip(sources, targets))
    ]


def padded_copy(pad, near, far):
    half, width = near.shape
    pad[:half, :width] = near[...]
    pad[half:, :width] = far[...]
    pad[:, width:] = jnp.zeros((2 * half, pad.shape[1] - width), pad.dtype)


def pipelined(blocks, group, arrived, inward, outward):
    for c in range(group):
        arrived(c)
        inward(c)

    def step(g, carry):
        for i in range(group):
            arrived(g * group + i)
        for i in range(group):
            outward((g - 1) * group + i)
        for i in range(group):
            inward(g * group + i)
        return carry

    lax.fori_loop(1, blocks // group, step, 0)
    for c in range(blocks - group, blocks):
        outward(c)


def layer_kernel(
    offs_ref, x_near, x_far, dy_near, dy_far, wg_hbm, wu_hbm, wd_hbm,
    hidden_ref, d_ref, xpad_ref, dypad_ref, keep_ref, send_ref,
    out_acc, grad_acc, wg_ref, wu_ref, wd_ref, sems,
):
    half, width = x_near.shape
    blocks, capacity, blk, _ = wg_ref.shape
    copies = functools.partial(
        tile_copies, (wg_hbm, wu_hbm, wd_hbm), (wg_ref, wu_ref, wd_ref), sems
    )
    for c in range(blocks):
        for copy in copies(c):
            copy.start()
    padded_copy(xpad_ref, x_near, x_far)
    padded_copy(dypad_ref, dy_near, dy_far)
    out_acc[...] = jnp.zeros_like(out_acc)
    grad_acc[...] = jnp.zeros_like(grad_acc)

    def arrived(c):
        for copy in copies(c):
            copy.wait()

    def inward(c):
        offs = slot_offsets(offs_ref, c, blk)
        xg = jnp.concatenate([xpad_ref[:, pl.ds(o, blk)] for o in offs], axis=1)
        w = jnp.concatenate(
            [wg_ref[c].reshape(capacity * blk, blk), wu_ref[c].reshape(capacity * blk, blk)],
            axis=1,
        )
        cut = capacity // 2 * blk
        pre = jnp.dot(xg[:, :cut], w[:cut], preferred_element_type=jnp.float32) + jnp.dot(
            xg[:, cut:], w[cut:], preferred_element_type=jnp.float32
        )
        dyg = jnp.concatenate([dypad_ref[:, pl.ds(o, blk)] for o in offs], axis=1)
        wd = jnp.concatenate([wd_ref[c, s] for s in range(capacity)], axis=1)
        d_hidden = lax.dot_general(
            dyg[:, :cut], wd[:, :cut], NT, preferred_element_type=jnp.float32
        ) + lax.dot_general(dyg[:, cut:], wd[:, cut:], NT, preferred_element_type=jnp.float32)
        gate, up = pre[:, :blk], pre[:, blk:]
        sig = 1.0 / (1.0 + jnp.exp(-gate))
        act = gate * sig
        hidden_ref[c] = (act * up).astype(jnp.bfloat16)
        d_ref[c, :, :blk] = (d_hidden * up * sig * (1.0 + gate * (1.0 - sig))).astype(jnp.bfloat16)
        d_ref[c, :, blk:] = (d_hidden * act).astype(jnp.bfloat16)

    def outward(c):
        offs = slot_offsets(offs_ref, c, blk)
        hidden = hidden_ref[c]
        d = d_ref[c]
        for s in range(0, capacity, CHUNK):
            wd = jnp.concatenate([wd_ref[c, s + i] for i in range(CHUNK)], axis=1)
            y = jnp.dot(hidden, wd, preferred_element_type=jnp.float32)
            add_to_rows(out_acc, offs[s : s + CHUNK], y, blk)
            w = jnp.concatenate(
                [
                    wg_ref[c, s : s + CHUNK].reshape(CHUNK * blk, blk),
                    wu_ref[c, s : s + CHUNK].reshape(CHUNK * blk, blk),
                ],
                axis=1,
            )
            x_slots = lax.dot_general(d, w, NT, preferred_element_type=jnp.float32)
            add_to_rows(grad_acc, offs[s : s + CHUNK], x_slots, blk)

    pipelined(blocks, 2 if blocks % 2 == 0 else 1, arrived, inward, outward)
    for i, acc in enumerate((out_acc, grad_acc)):
        keep_ref[i] = acc[:half, :width]
        send_ref[i] = acc[half:, :width].astype(send_ref.dtype)


def gate_up_products(pad_ref, d, offs, slots, blk, stages, i):
    for s in slots[::2]:
        xs = jnp.concatenate([pad_ref[:, pl.ds(o, blk)] for o in offs[s : s + 2]], axis=1)
        full = lax.dot_general(xs, d, TN, preferred_element_type=jnp.float32)
        full = full.astype(jnp.bfloat16)
        for k in range(2):
            stages[0][i, s + k] = full[k * blk : (k + 1) * blk, :blk]
            stages[1][i, s + k] = full[k * blk : (k + 1) * blk, blk:]


def down_products(pad_ref, hidden, offs, slots, blk, stages, i):
    for s in slots[::CHUNK]:
        dys = jnp.concatenate([pad_ref[:, pl.ds(o, blk)] for o in offs[s : s + CHUNK]], axis=1)
        full = lax.dot_general(hidden, dys, TN, preferred_element_type=jnp.float32)
        full = full.astype(jnp.bfloat16)
        for k in range(CHUNK):
            stages[0][i, s + k] = full[:, k * blk : (k + 1) * blk]


def grad_kernel(products, first, count, outs, behind, *refs):
    offs_ref, pad_ref, factor_ref = refs[:3]
    grad_refs = refs[3 + behind : 3 + behind + outs]
    stages = refs[3 + behind + outs : -1]
    sems = refs[-1]
    capacity, blk = stages[0].shape[1], stages[0].shape[-1]
    cut = capacity // 2 // CHUNK * CHUNK
    parts = (range(cut), range(cut, capacity))

    def copies(i, h):
        part = pl.ds(parts[h].start, len(parts[h]))
        return [
            pltpu.make_async_copy(stage.at[i, part], grad.at[first + i, part], sems.at[k, i, h])
            for k, (stage, grad) in enumerate(zip(stages, grad_refs))
        ]

    def step(i, carry):
        offs = slot_offsets(offs_ref, first + i, blk)
        factor = factor_ref[first + i]
        for h in range(2):
            products(pad_ref, factor, offs, parts[h], blk, stages, i)
            for copy in copies(i, h):
                copy.start()
        return carry

    lax.fori_loop(0, count, step, 0)
    for i in range(count):
        for h in range(2):
            for copy in copies(i, h):
                copy.wait()


def hop_orders(n):
    bits = [1 << i for i in range(n.bit_length() - 2, 0, -1)]
    return bits, bits[:-2] + bits[:-3:-1]


def swap(value, bits, n):
    return lax.ppermute(value, "col", [(j, j ^ bits[j % 2]) for j in range(n)])


def gather_hops(held, value, hops, n):
    send = value[None]
    for i, bits in enumerate(hops):
        if i:
            send = held[: 1 << i]
        held = lax.dynamic_update_slice_in_dim(held, swap(send, bits, n), 1 << i, 0)
    return held


def rows_of(held, swapped):
    pieces, mine, width = held.shape
    if swapped:
        held = held.reshape(2, 2, pieces // 4, mine, width).transpose(1, 0, 2, 3, 4)
    return held.reshape(pieces * mine, width)


def local(n, inputs, cotangent, gate_tiles, up_tiles, down_tiles, kept_rows, kept_count):
    blocks, capacity, blk, _ = gate_tiles.shape
    mine, width = inputs.shape
    tokens = mine * n
    smem = pl.BlockSpec(memory_space=pltpu.SMEM)
    vmem = pl.BlockSpec(memory_space=pltpu.VMEM)
    hbm = pl.BlockSpec(memory_space=pltpu.HBM)
    tile_bytes = blocks * capacity * blk * blk * 2
    tiles_in = [
        pltpu.with_memory_space_constraint(t, pltpu.HBM) for t in (gate_tiles, up_tiles, down_tiles)
    ]

    def cost(products, tiles, part=1.0):
        return pl.CostEstimate(
            flops=int(products * tokens * tile_bytes * part),
            bytes_accessed=int(tiles * tile_bytes * part),
            transcendentals=0,
        )

    x_held, dy_held = pl.pallas_call(
        seed_kernel,
        in_specs=[vmem, vmem],
        out_specs=[vmem, vmem],
        out_shape=[pltpu.VMEM((n // 2, mine, width), inputs.dtype)] * 2,
        name="seed",
    )(inputs, cotangent)
    offs = pl.pallas_call(
        functools.partial(offsets_kernel, width // blk, blk),
        in_specs=[smem, smem],
        out_specs=smem,
        out_shape=pltpu.SMEM(kept_rows.shape, jnp.int32),
        name="offsets",
    )(kept_rows, kept_count)
    cores = (1, 1)
    first, second = hop_orders(n)
    x_hops, dy_hops = list(zip(first, second)), list(zip(second, first))
    x_held = gather_hops(x_held, inputs, x_hops, n)
    dy_held = gather_hops(dy_held, cotangent, dy_hops, n)
    x_near, x_far = [rows_of(v, False) for v in (x_held, swap(x_held, cores, n))]
    dy_near, dy_far = [rows_of(v, True) for v in (dy_held, swap(dy_held, cores, n))]

    padded = pltpu.VMEM((tokens, width + blk), jnp.bfloat16)
    acc = pltpu.VMEM((tokens, width + blk), jnp.float32)
    hidden, d, xpad, dypad, keep, send = pl.pallas_call(
        layer_kernel,
        in_specs=[smem] + [vmem] * 4 + [hbm] * 3,
        out_specs=[vmem] * 6,
        out_shape=[
            pltpu.VMEM((blocks, tokens, blk), jnp.bfloat16),
            pltpu.VMEM((blocks, tokens, 2 * blk), jnp.bfloat16),
            padded,
            padded,
            pltpu.VMEM((2, tokens // 2, width), jnp.float32),
            pltpu.VMEM((2, tokens // 2, width), jnp.bfloat16),
        ],
        scratch_shapes=[acc, acc]
        + [pltpu.VMEM(gate_tiles.shape, jnp.bfloat16)] * 3
        + [pltpu.SemaphoreType.DMA((3, blocks))],
        compiler_params=pltpu.CompilerParams(vmem_limit_bytes=40 * 1024 * 1024),
        cost_estimate=cost(6, 3),
        name="layer",
    )(offs, x_near, x_far, dy_near, dy_far, *tiles_in)

    def grads(products, pad, factor, first, count, outs, earlier, after, name):
        behind = len(earlier) + len(after)
        return pl.pallas_call(
            functools.partial(grad_kernel, products, first, count, outs, behind),
            in_specs=[smem, vmem, vmem]
            + [hbm] * len(earlier)
            + [pl.BlockSpec(memory_space=pl.ANY)] * len(after),
            out_specs=[hbm] * outs,
            out_shape=[jax.ShapeDtypeStruct(gate_tiles.shape, jnp.bfloat16)] * outs,
            scratch_shapes=[pltpu.VMEM((count,) + gate_tiles.shape[1:], jnp.bfloat16)] * outs
            + [pltpu.SemaphoreType.DMA((outs, count, 2))],
            input_output_aliases={3 + k: k for k in range(len(earlier))},
            compiler_params=pltpu.CompilerParams(vmem_limit_bytes=24 * 1024 * 1024),
            cost_estimate=cost(outs, outs, count / blocks),
            name=name,
        )(offs, pad, factor, *earlier, *after)

    third = -(-blocks // 3)
    cuts = {0: (0, third), 2: (third, 2 * third), 3: (2 * third, blocks)}
    gate_up, down_grad, after = [], None, []
    for i, bits in enumerate([cores] + x_hops[::-1]):
        got = swap(send, bits, n)
        done = []
        if i == 1:
            (down_grad,) = grads(
                down_products, dypad, hidden, 0, blocks, 1, [], after, "down_grad"
            )
            done = [down_grad]
        elif i in cuts:
            first, last = cuts[i]
            gate_up = grads(
                gate_up_products, xpad, d, first, last - first, 2, gate_up, after, "gate_up_grad"
            )
            done = gate_up
        total = keep + got.astype(jnp.float32)
        if i < len(x_hops):
            half = total.shape[1] // 2
            keep, send = total[:, :half], total[:, half:].astype(jnp.bfloat16)
            send, done = lax.optimization_barrier((send, done))
            after = [send]
            if i == 1:
                (down_grad,) = done
            elif i in cuts:
                gate_up = done
    total = total.astype(jnp.bfloat16)
    return total[0], total[1], gate_up[0], gate_up[1], down_grad


def solution(mesh):
    tiles = P("col", None, None, None)
    tokens = P(("groups", "col"), None)
    grads = P(("groups", "col"), None, None, None)
    return jax.shard_map(
        functools.partial(local, mesh.shape["col"]),
        mesh=mesh,
        in_specs=(tokens, tokens, tiles, tiles, tiles, P("col", None), P("col")),
        out_specs=(tokens, tokens, grads, grads, grads),
        check_vma=False,
    )
```

```python
import functools

import jax
import jax.numpy as jnp
from jax import lax
from jax.experimental import pallas as pl
from jax.experimental.pallas import tpu as pltpu
from jax.sharding import PartitionSpec as P

NT = (((1,), (1,)), ((), ()))
TN = (((0,), (0,)), ((), ()))
CHUNK = 4
STEP = 4
LAG = 2


def seed_kernel(dead, rows_ref, count_ref, x_ref, dy_ref, live_ref, items_ref, total_ref, x_held, dy_held):
    x_held[0] = x_ref[...]
    dy_held[0] = dy_ref[...]
    blocks, capacity = rows_ref.shape
    chunks = capacity // CHUNK

    def block(c, position):
        count = count_ref[c]
        for s in range(capacity):
            live_ref[c, s] = jnp.where(s < count, rows_ref[c, s], dead)
        for q in range(chunks):
            items_ref[position + q] = c * chunks + q
        return position + jnp.clip((count + CHUNK - 1) // CHUNK, 1, chunks)

    total = lax.fori_loop(0, blocks, block, 0)
    total_ref[0] = total
    for s in range(capacity):
        live_ref[blocks, s] = dead
    for i in range(STEP):
        items_ref[total + i] = blocks * chunks


def add_to_rows(acc, rows, parts, blk):
    old = [acc[r] for r in rows]
    for i, r in enumerate(rows):
        acc[r] = old[i] + parts[:, i * blk : (i + 1) * blk]


def tile_copies(sources, targets, sems, c):
    return [
        pltpu.make_async_copy(src.at[c], dst.at[c], sems.at[i, c])
        for i, (src, dst) in enumerate(zip(sources, targets))
    ]


def row_blocks(pad, near, far):
    half = near.shape[0]
    count, _, blk = pad.shape
    for r in range(count - 1):
        pad[r, :half] = near[:, r * blk : (r + 1) * blk]
        pad[r, half:] = far[:, r * blk : (r + 1) * blk]
    pad[count - 1] = jnp.zeros(pad.shape[1:], pad.dtype)


def layer_kernel(
    live_ref, items_ref, total_ref, x_near, x_far, dy_near, dy_far, wg_hbm, wu_hbm, wd_hbm,
    hidden_ref, d_ref, xpad_ref, dypad_ref, keep_ref, send_ref,
    out_acc, grad_acc, pre_acc, wg_ref, wu_ref, wd_ref, sems,
):
    half = x_near.shape[0]
    blocks, capacity, blk, _ = wg_ref.shape
    chunks = capacity // CHUNK
    copies = functools.partial(
        tile_copies, (wg_hbm, wu_hbm, wd_hbm), (wg_ref, wu_ref, wd_ref), sems
    )
    for c in range(blocks):
        for copy in copies(c):
            copy.start()
    row_blocks(xpad_ref, x_near, x_far)
    row_blocks(dypad_ref, dy_near, dy_far)
    out_acc[...] = jnp.zeros_like(out_acc)
    grad_acc[...] = jnp.zeros_like(grad_acc)
    pre_acc[...] = jnp.zeros_like(pre_acc)

    def item(position):
        code = items_ref[position]
        c = code // chunks
        s = (code - c * chunks) * CHUNK
        rows = [live_ref[c, s + i] for i in range(CHUNK)]
        tiles = jnp.where(c < blocks, c, 0)
        return c, s, rows, tiles

    def arrived(position):
        code = items_ref[position]
        c = code // chunks

        @pl.when((code == c * chunks) & (c < blocks))
        def _():
            for copy in copies(c):
                copy.wait()

    def gate_up_tiles(tiles, s):
        return jnp.concatenate(
            [ref[tiles, pl.ds(s, CHUNK)].reshape(CHUNK * blk, blk) for ref in (wg_ref, wu_ref)],
            axis=1,
        )

    def down_tiles(tiles, s):
        return jnp.concatenate([wd_ref[tiles, s + i] for i in range(CHUNK)], axis=1)

    def inward(position):
        c, s, rows, tiles = item(position)
        xg = jnp.concatenate([xpad_ref[r] for r in rows], axis=1)
        dyg = jnp.concatenate([dypad_ref[r] for r in rows], axis=1)
        pre = jnp.dot(xg, gate_up_tiles(tiles, s), preferred_element_type=jnp.float32)
        d_hidden = lax.dot_general(
            dyg, down_tiles(tiles, s), NT, preferred_element_type=jnp.float32
        )
        pre_acc[c, :, : 2 * blk] += pre
        pre_acc[c, :, 2 * blk :] += d_hidden

    def outward(position):
        c, s, rows, tiles = item(position)
        gate, up, d_hidden = [pre_acc[c, :, i * blk : (i + 1) * blk] for i in range(3)]
        sig = 1.0 / (1.0 + jnp.exp(-gate))
        act = gate * sig
        hidden = (act * up).astype(jnp.bfloat16)
        d_gate = (d_hidden * up * sig * (1.0 + gate * (1.0 - sig))).astype(jnp.bfloat16)
        d = jnp.concatenate([d_gate, (d_hidden * act).astype(jnp.bfloat16)], axis=1)
        hidden_ref[c] = hidden
        d_ref[c] = d
        y = jnp.dot(hidden, down_tiles(tiles, s), preferred_element_type=jnp.float32)
        x_slots = lax.dot_general(
            d, gate_up_tiles(tiles, s), NT, preferred_element_type=jnp.float32
        )
        add_to_rows(out_acc, rows, y, blk)
        add_to_rows(grad_acc, rows, x_slots, blk)

    def step(g, do_inward, do_outward):
        if do_inward:
            for i in range(STEP):
                arrived(g * STEP + i)
        if do_outward:
            for i in range(STEP):
                outward((g - LAG) * STEP + i)
        if do_inward:
            for i in range(STEP):
                inward(g * STEP + i)

    steps = (total_ref[0] + STEP - 1) // STEP
    lag = jnp.minimum(steps, LAG)

    def loop(first, last, *parts):
        def body(g, carry):
            step(g, *parts)
            return carry

        lax.fori_loop(first, last, body, 0)

    loop(0, lag, True, False)
    loop(LAG, steps, True, True)
    loop(steps - lag + LAG, steps + LAG, False, True)
    for r in range(out_acc.shape[0] - 1):
        columns = slice(r * blk, (r + 1) * blk)
        for i, acc in enumerate((out_acc, grad_acc)):
            keep_ref[i, :, columns] = acc[r, :half]
            send_ref[i, :, columns] = acc[r, half:].astype(send_ref.dtype)


def gate_up_products(pad_ref, d, rows, slots, blk, stages, i):
    for s in slots[::2]:
        xs = jnp.concatenate([pad_ref[r] for r in rows[s : s + 2]], axis=1)
        full = lax.dot_general(xs, d, TN, preferred_element_type=jnp.float32)
        full = full.astype(jnp.bfloat16)
        for k in range(2):
            stages[0][i, s + k] = full[k * blk : (k + 1) * blk, :blk]
            stages[1][i, s + k] = full[k * blk : (k + 1) * blk, blk:]


def down_products(pad_ref, hidden, rows, slots, blk, stages, i):
    for s in slots[::CHUNK]:
        dys = jnp.concatenate([pad_ref[r] for r in rows[s : s + CHUNK]], axis=1)
        full = lax.dot_general(hidden, dys, TN, preferred_element_type=jnp.float32)
        full = full.astype(jnp.bfloat16)
        for k in range(CHUNK):
            stages[0][i, s + k] = full[:, k * blk : (k + 1) * blk]


def grad_kernel(products, first, count, outs, behind, *refs):
    live_ref, pad_ref, factor_ref = refs[:3]
    grad_refs = refs[3 + behind : 3 + behind + outs]
    stages = refs[3 + behind + outs : -1]
    sems = refs[-1]
    capacity, blk = stages[0].shape[1], stages[0].shape[-1]
    cut = capacity // 2 // CHUNK * CHUNK
    parts = (range(cut), range(cut, capacity))

    def copies(i, h):
        part = pl.ds(parts[h].start, len(parts[h]))
        return [
            pltpu.make_async_copy(stage.at[i, part], grad.at[first + i, part], sems.at[k, i, h])
            for k, (stage, grad) in enumerate(zip(stages, grad_refs))
        ]

    def step(i, carry):
        rows = [live_ref[first + i, s] for s in range(capacity)]
        factor = factor_ref[first + i]
        for h in range(2):
            products(pad_ref, factor, rows, parts[h], blk, stages, i)
            for copy in copies(i, h):
                copy.start()
        return carry

    lax.fori_loop(0, count, step, 0)
    for i in range(count):
        for h in range(2):
            for copy in copies(i, h):
                copy.wait()


def hop_orders(n):
    bits = [1 << i for i in range(n.bit_length() - 2, 0, -1)]
    return bits, bits[:-2] + bits[:-3:-1]


def swap(value, bits, n):
    return lax.ppermute(value, "col", [(j, j ^ bits[j % 2]) for j in range(n)])


def gather_hops(held, value, hops, n):
    send = value[None]
    for i, bits in enumerate(hops):
        if i:
            send = held[: 1 << i]
        held = lax.dynamic_update_slice_in_dim(held, swap(send, bits, n), 1 << i, 0)
    return held


def rows_of(held, swapped):
    pieces, mine, width = held.shape
    if swapped:
        held = held.reshape(2, 2, pieces // 4, mine, width).transpose(1, 0, 2, 3, 4)
    return held.reshape(pieces * mine, width)


def local(n, inputs, cotangent, gate_tiles, up_tiles, down_tiles, kept_rows, kept_count):
    blocks, capacity, blk, _ = gate_tiles.shape
    mine, width = inputs.shape
    tokens = mine * n
    smem = pl.BlockSpec(memory_space=pltpu.SMEM)
    vmem = pl.BlockSpec(memory_space=pltpu.VMEM)
    hbm = pl.BlockSpec(memory_space=pltpu.HBM)
    tile_bytes = blocks * capacity * blk * blk * 2
    tiles_in = [
        pltpu.with_memory_space_constraint(t, pltpu.HBM) for t in (gate_tiles, up_tiles, down_tiles)
    ]

    def cost(products, tiles, part=1.0):
        return pl.CostEstimate(
            flops=int(products * tokens * tile_bytes * part),
            bytes_accessed=int(tiles * tile_bytes * part),
            transcendentals=0,
        )

    live, items, total, x_held, dy_held = pl.pallas_call(
        functools.partial(seed_kernel, width // blk),
        in_specs=[smem, smem, vmem, vmem],
        out_specs=[smem, smem, smem, vmem, vmem],
        out_shape=[
            pltpu.SMEM((blocks + 1, capacity), jnp.int32),
            pltpu.SMEM((blocks * (capacity // CHUNK) + capacity // CHUNK + STEP,), jnp.int32),
            pltpu.SMEM((1,), jnp.int32),
        ]
        + [pltpu.VMEM((n // 2, mine, width), inputs.dtype)] * 2,
        name="seed",
    )(kept_rows, kept_count, inputs, cotangent)
    cores = (1, 1)
    first, second = hop_orders(n)
    x_hops, dy_hops = list(zip(first, second)), list(zip(second, first))
    x_held = gather_hops(x_held, inputs, x_hops, n)
    dy_held = gather_hops(dy_held, cotangent, dy_hops, n)
    x_near, x_far = [rows_of(v, False) for v in (x_held, swap(x_held, cores, n))]
    dy_near, dy_far = [rows_of(v, True) for v in (dy_held, swap(dy_held, cores, n))]

    padded = pltpu.VMEM((width // blk + 1, tokens, blk), jnp.bfloat16)
    acc = pltpu.VMEM((width // blk + 1, tokens, blk), jnp.float32)
    hidden, d, xpad, dypad, keep, send = pl.pallas_call(
        layer_kernel,
        in_specs=[smem] * 3 + [vmem] * 4 + [hbm] * 3,
        out_specs=[vmem] * 6,
        out_shape=[
            pltpu.VMEM((blocks + 1, tokens, blk), jnp.bfloat16),
            pltpu.VMEM((blocks + 1, tokens, 2 * blk), jnp.bfloat16),
            padded,
            padded,
            pltpu.VMEM((2, tokens // 2, width), jnp.float32),
            pltpu.VMEM((2, tokens // 2, width), jnp.bfloat16),
        ],
        scratch_shapes=[acc, acc, pltpu.VMEM((blocks + 1, tokens, 3 * blk), jnp.float32)]
        + [pltpu.VMEM(gate_tiles.shape, jnp.bfloat16)] * 3
        + [pltpu.SemaphoreType.DMA((3, blocks))],
        compiler_params=pltpu.CompilerParams(vmem_limit_bytes=40 * 1024 * 1024),
        cost_estimate=cost(6, 3),
        name="layer",
    )(live, items, total, x_near, x_far, dy_near, dy_far, *tiles_in)

    def grads(products, pad, factor, first, count, outs, earlier, after, name):
        behind = len(earlier) + len(after)
        return pl.pallas_call(
            functools.partial(grad_kernel, products, first, count, outs, behind),
            in_specs=[smem, vmem, vmem]
            + [hbm] * len(earlier)
            + [pl.BlockSpec(memory_space=pl.ANY)] * len(after),
            out_specs=[hbm] * outs,
            out_shape=[jax.ShapeDtypeStruct(gate_tiles.shape, jnp.bfloat16)] * outs,
            scratch_shapes=[pltpu.VMEM((count,) + gate_tiles.shape[1:], jnp.bfloat16)] * outs
            + [pltpu.SemaphoreType.DMA((outs, count, 2))],
            input_output_aliases={3 + k: k for k in range(len(earlier))},
            compiler_params=pltpu.CompilerParams(vmem_limit_bytes=24 * 1024 * 1024),
            cost_estimate=cost(outs, outs, count / blocks),
            name=name,
        )(live, pad, factor, *earlier, *after)

    third = -(-blocks // 3)
    cuts = {0: (0, third), 2: (third, 2 * third), 3: (2 * third, blocks)}
    gate_up, down_grad, after = [], None, []
    for i, bits in enumerate([cores] + x_hops[::-1]):
        got = swap(send, bits, n)
        done = []
        if i == 1:
            (down_grad,) = grads(
                down_products, dypad, hidden, 0, blocks, 1, [], after, "down_grad"
            )
            done = [down_grad]
        elif i in cuts:
            first, last = cuts[i]
            gate_up = grads(
                gate_up_products, xpad, d, first, last - first, 2, gate_up, after, "gate_up_grad"
            )
            done = gate_up
        total = keep + got.astype(jnp.float32)
        if i < len(x_hops):
            half = total.shape[1] // 2
            keep, send = total[:, :half], total[:, half:].astype(jnp.bfloat16)
            send, done = lax.optimization_barrier((send, done))
            after = [send]
            if i == 1:
                (down_grad,) = done
            elif i in cuts:
                gate_up = done
    total = total.astype(jnp.bfloat16)
    return total[0], total[1], gate_up[0], gate_up[1], down_grad


def solution(mesh):
    tiles = P("col", None, None, None)
    tokens = P(("groups", "col"), None)
    grads = P(("groups", "col"), None, None, None)
    return jax.shard_map(
        functools.partial(local, mesh.shape["col"]),
        mesh=mesh,
        in_specs=(tokens, tokens, tiles, tiles, tiles, P("col", None), P("col")),
        out_specs=(tokens, tokens, grads, grads, grads),
        check_vma=False,
    )
```

```python
import functools

import jax
import jax.numpy as jnp
from jax import lax
from jax.experimental import pallas as pl
from jax.experimental.pallas import tpu as pltpu
from jax.sharding import PartitionSpec as P

NT = (((1,), (1,)), ((), ()))
TN = (((0,), (0,)), ((), ()))
CHUNK = 4
STEP = 4
LAG = 2


def seed_kernel(dead, rows_ref, count_ref, x_ref, dy_ref, live_ref, items_ref, total_ref, held):
    held[0, 0] = x_ref[...]
    held[1, 0] = dy_ref[...]
    blocks, capacity = rows_ref.shape
    chunks = capacity // CHUNK

    def block(c, position):
        count = count_ref[c]
        for s in range(capacity):
            live_ref[c, s] = jnp.where(s < count, rows_ref[c, s], dead)
        for q in range(chunks):
            items_ref[position + q] = c * chunks + q
        return position + jnp.clip((count + CHUNK - 1) // CHUNK, 1, chunks)

    total = lax.fori_loop(0, blocks, block, 0)
    total_ref[0] = total
    for s in range(capacity):
        live_ref[blocks, s] = dead
    for i in range(STEP):
        items_ref[total + i] = blocks * chunks


def add_to_rows(acc, rows, parts, blk):
    old = [acc[r] for r in rows]
    for i, r in enumerate(rows):
        acc[r] = old[i] + parts[:, i * blk : (i + 1) * blk]


def tile_copies(sources, targets, sems, c):
    return [
        pltpu.make_async_copy(src.at[c], dst.at[c], sems.at[i, c])
        for i, (src, dst) in enumerate(zip(sources, targets))
    ]


def row_blocks(pad, near, far):
    half = near.shape[0]
    count, _, blk = pad.shape
    for r in range(count - 1):
        pad[r, :half] = near[:, r * blk : (r + 1) * blk]
        pad[r, half:] = far[:, r * blk : (r + 1) * blk]
    pad[count - 1] = jnp.zeros(pad.shape[1:], pad.dtype)


def layer_kernel(
    live_ref, items_ref, total_ref, near_ref, far_ref, wg_hbm, wu_hbm, wd_hbm,
    hidden_ref, d_ref, xpad_ref, dypad_ref, keep_ref, send_ref,
    out_acc, grad_acc, pre_acc, wg_ref, wu_ref, wd_ref, sems,
):
    half = near_ref.shape[1]
    blocks, capacity, blk, _ = wg_ref.shape
    chunks = capacity // CHUNK
    copies = functools.partial(
        tile_copies, (wg_hbm, wu_hbm, wd_hbm), (wg_ref, wu_ref, wd_ref), sems
    )
    for c in range(blocks):
        for copy in copies(c):
            copy.start()
    row_blocks(xpad_ref, near_ref.at[0], far_ref.at[0])
    row_blocks(dypad_ref, near_ref.at[1], far_ref.at[1])
    out_acc[...] = jnp.zeros_like(out_acc)
    grad_acc[...] = jnp.zeros_like(grad_acc)
    pre_acc[...] = jnp.zeros_like(pre_acc)

    def item(position):
        code = items_ref[position]
        c = code // chunks
        s = (code - c * chunks) * CHUNK
        rows = [live_ref[c, s + i] for i in range(CHUNK)]
        tiles = jnp.where(c < blocks, c, 0)
        return c, s, rows, tiles

    def arrived(position):
        code = items_ref[position]
        c = code // chunks

        @pl.when((code == c * chunks) & (c < blocks))
        def _():
            for copy in copies(c):
                copy.wait()

    def gate_up_tiles(tiles, s):
        return jnp.concatenate(
            [ref[tiles, pl.ds(s, CHUNK)].reshape(CHUNK * blk, blk) for ref in (wg_ref, wu_ref)],
            axis=1,
        )

    def down_tiles(tiles, s):
        return jnp.concatenate([wd_ref[tiles, s + i] for i in range(CHUNK)], axis=1)

    def inward(position):
        c, s, rows, tiles = item(position)
        xg = jnp.concatenate([xpad_ref[r] for r in rows], axis=1)
        dyg = jnp.concatenate([dypad_ref[r] for r in rows], axis=1)
        pre = jnp.dot(xg, gate_up_tiles(tiles, s), preferred_element_type=jnp.float32)
        d_hidden = lax.dot_general(
            dyg, down_tiles(tiles, s), NT, preferred_element_type=jnp.float32
        )
        pre_acc[c, :, : 2 * blk] += pre
        pre_acc[c, :, 2 * blk :] += d_hidden

    def outward(position):
        c, s, rows, tiles = item(position)
        gate, up, d_hidden = [pre_acc[c, :, i * blk : (i + 1) * blk] for i in range(3)]
        sig = 1.0 / (1.0 + jnp.exp(-gate))
        act = gate * sig
        hidden = (act * up).astype(jnp.bfloat16)
        d_gate = (d_hidden * up * sig * (1.0 + gate * (1.0 - sig))).astype(jnp.bfloat16)
        d = jnp.concatenate([d_gate, (d_hidden * act).astype(jnp.bfloat16)], axis=1)
        hidden_ref[c] = hidden
        d_ref[c] = d
        y = jnp.dot(hidden, down_tiles(tiles, s), preferred_element_type=jnp.float32)
        x_slots = lax.dot_general(
            d, gate_up_tiles(tiles, s), NT, preferred_element_type=jnp.float32
        )
        add_to_rows(out_acc, rows, y, blk)
        add_to_rows(grad_acc, rows, x_slots, blk)

    def step(g, do_inward, do_outward):
        if do_inward:
            for i in range(STEP):
                arrived(g * STEP + i)
        if do_outward:
            for i in range(STEP):
                outward((g - LAG) * STEP + i)
        if do_inward:
            for i in range(STEP):
                inward(g * STEP + i)

    steps = (total_ref[0] + STEP - 1) // STEP
    lag = jnp.minimum(steps, LAG)

    def loop(first, last, *parts):
        def body(g, carry):
            step(g, *parts)
            return carry

        lax.fori_loop(first, last, body, 0)

    loop(0, lag, True, False)
    loop(LAG, steps, True, True)
    loop(steps - lag + LAG, steps + LAG, False, True)
    for r in range(out_acc.shape[0] - 1):
        columns = slice(r * blk, (r + 1) * blk)
        for i, acc in enumerate((out_acc, grad_acc)):
            keep_ref[i, :, columns] = acc[r, :half]
            send_ref[i, :, columns] = acc[r, half:].astype(send_ref.dtype)


def gate_up_products(pad_ref, d, rows, slots, blk, stages, i):
    for s in slots[::2]:
        xs = jnp.concatenate([pad_ref[r] for r in rows[s : s + 2]], axis=1)
        full = lax.dot_general(xs, d, TN, preferred_element_type=jnp.float32)
        full = full.astype(jnp.bfloat16)
        for k in range(2):
            stages[0][i, s + k] = full[k * blk : (k + 1) * blk, :blk]
            stages[1][i, s + k] = full[k * blk : (k + 1) * blk, blk:]


def down_products(pad_ref, hidden, rows, slots, blk, stages, i):
    tokens = hidden.shape[0]
    groups = len(slots) // CHUNK
    zero = jnp.zeros((tokens, blk), hidden.dtype)
    spread = jnp.concatenate(
        [
            jnp.concatenate([hidden if j == k else zero for k in range(groups)], axis=1)
            for j in range(groups)
        ],
        axis=0,
    )
    for s in range(0, CHUNK, 2):
        dys = jnp.concatenate(
            [
                jnp.concatenate([pad_ref[rows[j * CHUNK + s + k]] for k in range(2)], axis=1)
                for j in range(groups)
            ],
            axis=0,
        )
        full = lax.dot_general(spread, dys, TN, preferred_element_type=jnp.float32)
        full = full.astype(jnp.bfloat16)
        for j in range(groups):
            for k in range(2):
                stages[0][i, j * CHUNK + s + k] = full[
                    j * blk : (j + 1) * blk, k * blk : (k + 1) * blk
                ]


def grad_kernel(products, first, count, outs, behind, per_part, *refs):
    live_ref, pad_ref, factor_ref = refs[:3]
    grad_refs = refs[3 + behind : 3 + behind + outs]
    stages = refs[3 + behind + outs : -1]
    sems = refs[-1]
    capacity, blk = stages[0].shape[1], stages[0].shape[-1]
    parts = capacity // per_part

    def copies(i, h):
        part = pl.ds(h * per_part, per_part)
        return [
            pltpu.make_async_copy(stage.at[i, part], grad.at[first + i, part], sems.at[k, i, h])
            for k, (stage, grad) in enumerate(zip(stages, grad_refs))
        ]

    def step(i, carry):
        rows = [live_ref[first + i, s] for s in range(capacity)]
        factor = factor_ref[first + i]
        for h in range(parts):
            slots = range(h * per_part, (h + 1) * per_part)
            products(pad_ref, factor, rows, slots, blk, stages, i)
            for copy in copies(i, h):
                copy.start()
        return carry

    lax.fori_loop(0, count, step, 0)
    for i in range(count):
        for h in range(parts):
            for copy in copies(i, h):
                copy.wait()


def hop_orders(n):
    bits = [1 << i for i in range(n.bit_length() - 2, 0, -1)]
    return bits, bits[:-2] + bits[:-3:-1]


def swap(value, bits, n):
    return lax.ppermute(value, "col", [(j, j ^ bits[j % 2]) for j in range(n)])


def local(n, inputs, cotangent, gate_tiles, up_tiles, down_tiles, kept_rows, kept_count):
    blocks, capacity, blk, _ = gate_tiles.shape
    mine, width = inputs.shape
    tokens = mine * n
    smem = pl.BlockSpec(memory_space=pltpu.SMEM)
    vmem = pl.BlockSpec(memory_space=pltpu.VMEM)
    hbm = pl.BlockSpec(memory_space=pltpu.HBM)
    tile_bytes = blocks * capacity * blk * blk * 2
    tiles_in = [
        pltpu.with_memory_space_constraint(t, pltpu.HBM) for t in (gate_tiles, up_tiles, down_tiles)
    ]

    def cost(products, tiles, part=1.0):
        return pl.CostEstimate(
            flops=int(products * tokens * tile_bytes * part),
            bytes_accessed=int(tiles * tile_bytes * part),
            transcendentals=0,
        )

    live, items, total, held = pl.pallas_call(
        functools.partial(seed_kernel, width // blk),
        in_specs=[smem, smem, vmem, vmem],
        out_specs=[smem, smem, smem, vmem],
        out_shape=[
            pltpu.SMEM((blocks + 1, capacity), jnp.int32),
            pltpu.SMEM((blocks * (capacity // CHUNK) + capacity // CHUNK + STEP,), jnp.int32),
            pltpu.SMEM((1,), jnp.int32),
            pltpu.VMEM((2, n // 2, mine, width), inputs.dtype),
        ],
        name="seed",
    )(kept_rows, kept_count, inputs, cotangent)
    cores = (1, 1)
    hops = list(zip(*hop_orders(n)))
    for i, bits in enumerate(hops):
        if i:
            got = swap(held[:, : 1 << i], bits, n)
            held = lax.dynamic_update_slice(held, got, (0, 1 << i, 0, 0))
        else:
            for k, value in enumerate((inputs, cotangent)):
                held = lax.dynamic_update_slice(held, swap(value, bits, n)[None, None], (k, 1, 0, 0))
    near, far = [v.reshape(2, n // 2 * mine, width) for v in (held, swap(held, cores, n))]

    padded = pltpu.VMEM((width // blk + 1, tokens, blk), jnp.bfloat16)
    acc = pltpu.VMEM((width // blk + 1, tokens, blk), jnp.float32)
    hidden, d, xpad, dypad, keep, send = pl.pallas_call(
        layer_kernel,
        in_specs=[smem] * 3 + [vmem] * 2 + [hbm] * 3,
        out_specs=[vmem] * 6,
        out_shape=[
            pltpu.VMEM((blocks + 1, tokens, blk), jnp.bfloat16),
            pltpu.VMEM((blocks + 1, tokens, 2 * blk), jnp.bfloat16),
            padded,
            padded,
            pltpu.VMEM((2, tokens // 2, width), jnp.float32),
            pltpu.VMEM((2, tokens // 2, width), jnp.bfloat16),
        ],
        scratch_shapes=[acc, acc, pltpu.VMEM((blocks + 1, tokens, 3 * blk), jnp.float32)]
        + [pltpu.VMEM(gate_tiles.shape, jnp.bfloat16)] * 3
        + [pltpu.SemaphoreType.DMA((3, blocks))],
        compiler_params=pltpu.CompilerParams(vmem_limit_bytes=40 * 1024 * 1024),
        cost_estimate=cost(6, 3),
        name="layer",
    )(live, items, total, near, far, *tiles_in)

    def grads(products, pad, factor, first, count, outs, per_part, earlier, after, name):
        behind = len(earlier) + len(after)
        return pl.pallas_call(
            functools.partial(grad_kernel, products, first, count, outs, behind, per_part),
            in_specs=[smem, vmem, vmem]
            + [hbm] * len(earlier)
            + [pl.BlockSpec(memory_space=pl.ANY)] * len(after),
            out_specs=[hbm] * outs,
            out_shape=[jax.ShapeDtypeStruct(gate_tiles.shape, jnp.bfloat16)] * outs,
            scratch_shapes=[pltpu.VMEM((count,) + gate_tiles.shape[1:], jnp.bfloat16)] * outs
            + [pltpu.SemaphoreType.DMA((outs, count, capacity // per_part))],
            input_output_aliases={3 + k: k for k in range(len(earlier))},
            compiler_params=pltpu.CompilerParams(vmem_limit_bytes=24 * 1024 * 1024),
            cost_estimate=cost(outs, outs, count / blocks),
            name=name,
        )(live, pad, factor, *earlier, *after)

    third = -(-blocks // 3)
    cuts = {0: (0, third), 2: (third, 2 * third), 3: (2 * third, blocks)}
    gate_up, down_grad, after = [], None, []
    for i, bits in enumerate([cores] + hops[::-1]):
        got = swap(send, bits, n)
        done = []
        if i == 1:
            (down_grad,) = grads(
                down_products, dypad, hidden, 0, blocks, 1, capacity, [], after, "down_grad"
            )
            done = [down_grad]
        elif i in cuts:
            first, last = cuts[i]
            gate_up = grads(
                gate_up_products, xpad, d, first, last - first, 2, CHUNK, gate_up, after, "gate_up_grad"
            )
            done = gate_up
        total = keep + got.astype(jnp.float32)
        if i < len(hops):
            half = total.shape[1] // 2
            keep, send = total[:, :half], total[:, half:].astype(jnp.bfloat16)
            send, done = lax.optimization_barrier((send, done))
            after = [send]
            if i == 1:
                (down_grad,) = done
            elif i in cuts:
                gate_up = done
    total = total.astype(jnp.bfloat16)
    return total[0], total[1], gate_up[0], gate_up[1], down_grad


def solution(mesh):
    tiles = P("col", None, None, None)
    tokens = P(("groups", "col"), None)
    grads = P(("groups", "col"), None, None, None)
    return jax.shard_map(
        functools.partial(local, mesh.shape["col"]),
        mesh=mesh,
        in_specs=(tokens, tokens, tiles, tiles, tiles, P("col", None), P("col")),
        out_specs=(tokens, tokens, grads, grads, grads),
        check_vma=False,
    )
```

```python
import functools

import jax
import jax.numpy as jnp
from jax import lax
from jax.experimental import pallas as pl
from jax.experimental.pallas import tpu as pltpu
from jax.sharding import PartitionSpec as P

NT = (((1,), (1,)), ((), ()))
TN = (((0,), (0,)), ((), ()))
CHUNK = 4
STEP = 4
LAG = 2


def seed_kernel(dead, rows_ref, count_ref, x_ref, dy_ref, live_ref, block_ref, slot_ref, total_ref, x_held, dy_held):
    x_held[0] = x_ref[...]
    dy_held[0] = dy_ref[...]
    blocks, capacity = rows_ref.shape
    chunks = capacity // CHUNK

    def block(c, position):
        count = count_ref[c]
        for s in range(capacity):
            live_ref[c, s] = jnp.where(s < count, rows_ref[c, s], dead)
        for q in range(chunks):
            block_ref[position + q] = c
            slot_ref[position + q] = q * CHUNK
        return position + jnp.clip((count + CHUNK - 1) // CHUNK, 1, chunks)

    total = lax.fori_loop(0, blocks, block, 0)
    total_ref[0] = total
    for s in range(capacity):
        live_ref[blocks, s] = dead
    for i in range(STEP):
        block_ref[total + i] = blocks
        slot_ref[total + i] = 0


def add_to_rows(acc, rows, parts, blk):
    old = [acc[r] for r in rows]
    for i, r in enumerate(rows):
        acc[r] = old[i] + parts[:, i * blk : (i + 1) * blk]


def tile_copies(sources, targets, sems, c):
    return [
        pltpu.make_async_copy(src.at[c], dst.at[c], sems.at[i, c])
        for i, (src, dst) in enumerate(zip(sources, targets))
    ]


def row_blocks(pad, near, far):
    half = near.shape[0]
    count, _, blk = pad.shape
    for r in range(count - 1):
        pad[r, :half] = near[:, r * blk : (r + 1) * blk]
        pad[r, half:] = far[:, r * blk : (r + 1) * blk]
    pad[count - 1] = jnp.zeros(pad.shape[1:], pad.dtype)


def layer_kernel(
    live_ref, block_ref, slot_ref, total_ref, x_near, x_far, dy_near, dy_far, wg_hbm, wu_hbm, wd_hbm,
    hidden_ref, d_ref, xpad_ref, dypad_ref, keep_ref, send_ref,
    out_acc, grad_acc, pre_acc, wg_ref, wu_ref, wd_ref, sems,
):
    half = x_near.shape[0]
    blocks, capacity, blk, _ = wg_ref.shape
    copies = functools.partial(
        tile_copies, (wg_hbm, wu_hbm, wd_hbm), (wg_ref, wu_ref, wd_ref), sems
    )
    for c in range(blocks):
        for copy in copies(c):
            copy.start()
    row_blocks(xpad_ref, x_near, x_far)
    row_blocks(dypad_ref, dy_near, dy_far)
    out_acc[...] = jnp.zeros_like(out_acc)
    grad_acc[...] = jnp.zeros_like(grad_acc)
    pre_acc[...] = jnp.zeros_like(pre_acc)

    def item(position):
        c, s = block_ref[position], slot_ref[position]
        rows = [live_ref[c, s + i] for i in range(CHUNK)]
        return c, s, rows, jnp.where(c < blocks, c, 0)

    def arrived(g):
        before = jnp.where(g > 0, block_ref[jnp.maximum(g * STEP - 1, 0)] + 1, 0)
        after = jnp.minimum(block_ref[g * STEP + STEP - 1] + 1, blocks)

        def wait(c, carry):
            for copy in copies(c):
                copy.wait()
            return carry

        lax.fori_loop(before, after, wait, 0)

    def gate_up_tiles(tiles, s):
        return jnp.concatenate(
            [ref[tiles, pl.ds(s, CHUNK)].reshape(CHUNK * blk, blk) for ref in (wg_ref, wu_ref)],
            axis=1,
        )

    def down_tiles(tiles, s):
        return jnp.concatenate([wd_ref[tiles, s + i] for i in range(CHUNK)], axis=1)

    def inward(position):
        c, s, rows, tiles = item(position)
        xg = jnp.concatenate([xpad_ref[r] for r in rows], axis=1)
        dyg = jnp.concatenate([dypad_ref[r] for r in rows], axis=1)
        pre = jnp.dot(xg, gate_up_tiles(tiles, s), preferred_element_type=jnp.float32)
        d_hidden = lax.dot_general(
            dyg, down_tiles(tiles, s), NT, preferred_element_type=jnp.float32
        )
        pre_acc[c, :, : 2 * blk] += pre
        pre_acc[c, :, 2 * blk :] += d_hidden

    def outward(position):
        c, s, rows, tiles = item(position)
        gate, up, d_hidden = [pre_acc[c, :, i * blk : (i + 1) * blk] for i in range(3)]
        sig = 1.0 / (1.0 + jnp.exp(-gate))
        act = gate * sig
        hidden = (act * up).astype(jnp.bfloat16)
        d_gate = (d_hidden * up * sig * (1.0 + gate * (1.0 - sig))).astype(jnp.bfloat16)
        d = jnp.concatenate([d_gate, (d_hidden * act).astype(jnp.bfloat16)], axis=1)
        hidden_ref[c] = hidden
        d_ref[c] = d
        y = jnp.dot(hidden, down_tiles(tiles, s), preferred_element_type=jnp.float32)
        x_slots = lax.dot_general(
            d, gate_up_tiles(tiles, s), NT, preferred_element_type=jnp.float32
        )
        add_to_rows(out_acc, rows, y, blk)
        add_to_rows(grad_acc, rows, x_slots, blk)

    def step(g, do_inward, do_outward):
        if do_inward:
            arrived(g)
        if do_outward:
            for i in range(STEP):
                outward((g - LAG) * STEP + i)
        if do_inward:
            for i in range(STEP):
                inward(g * STEP + i)

    steps = (total_ref[0] + STEP - 1) // STEP
    lag = jnp.minimum(steps, LAG)

    def loop(first, last, *parts):
        def body(g, carry):
            step(g, *parts)
            return carry

        lax.fori_loop(first, last, body, 0)

    loop(0, lag, True, False)
    loop(LAG, steps, True, True)
    loop(steps - lag + LAG, steps + LAG, False, True)
    for r in range(out_acc.shape[0] - 1):
        columns = slice(r * blk, (r + 1) * blk)
        for i, acc in enumerate((out_acc, grad_acc)):
            keep_ref[i, :, columns] = acc[r, :half]
            send_ref[i, :, columns] = acc[r, half:].astype(send_ref.dtype)


def gate_up_products(pad_ref, d, rows, slots, blk, stages, i):
    for s in slots[::2]:
        xs = jnp.concatenate([pad_ref[r] for r in rows[s : s + 2]], axis=1)
        full = lax.dot_general(xs, d, TN, preferred_element_type=jnp.float32)
        full = full.astype(jnp.bfloat16)
        for k in range(2):
            stages[0][i, s + k] = full[k * blk : (k + 1) * blk, :blk]
            stages[1][i, s + k] = full[k * blk : (k + 1) * blk, blk:]


def down_products(pad_ref, hidden, rows, slots, blk, stages, i):
    for s in slots[::CHUNK]:
        dys = jnp.concatenate([pad_ref[r] for r in rows[s : s + CHUNK]], axis=1)
        full = lax.dot_general(hidden, dys, TN, preferred_element_type=jnp.float32)
        full = full.astype(jnp.bfloat16)
        for k in range(CHUNK):
            stages[0][i, s + k] = full[:, k * blk : (k + 1) * blk]


def grad_kernel(products, first, count, outs, behind, *refs):
    live_ref, pad_ref, factor_ref = refs[:3]
    grad_refs = refs[3 + behind : 3 + behind + outs]
    stages = refs[3 + behind + outs : -1]
    sems = refs[-1]
    capacity, blk = stages[0].shape[1], stages[0].shape[-1]
    cut = capacity // 2 // CHUNK * CHUNK
    parts = (range(cut), range(cut, capacity))

    def copies(i, h):
        part = pl.ds(parts[h].start, len(parts[h]))
        return [
            pltpu.make_async_copy(stage.at[i, part], grad.at[first + i, part], sems.at[k, i, h])
            for k, (stage, grad) in enumerate(zip(stages, grad_refs))
        ]

    def step(i, carry):
        rows = [live_ref[first + i, s] for s in range(capacity)]
        factor = factor_ref[first + i]
        for h in range(2):
            products(pad_ref, factor, rows, parts[h], blk, stages, i)
            for copy in copies(i, h):
                copy.start()
        return carry

    lax.fori_loop(0, count, step, 0)
    for i in range(count):
        for h in range(2):
            for copy in copies(i, h):
                copy.wait()


def hop_orders(n):
    bits = [1 << i for i in range(n.bit_length() - 2, 0, -1)]
    return bits, bits[:-2] + bits[:-3:-1]


def swap(value, bits, n):
    return lax.ppermute(value, "col", [(j, j ^ bits[j % 2]) for j in range(n)])


def gather_hops(held, value, hops, n):
    send = value[None]
    for i, bits in enumerate(hops):
        if i:
            send = held[: 1 << i]
        held = lax.dynamic_update_slice_in_dim(held, swap(send, bits, n), 1 << i, 0)
    return held


def rows_of(held, swapped):
    pieces, mine, width = held.shape
    if swapped:
        held = held.reshape(2, 2, pieces // 4, mine, width).transpose(1, 0, 2, 3, 4)
    return held.reshape(pieces * mine, width)


def local(n, inputs, cotangent, gate_tiles, up_tiles, down_tiles, kept_rows, kept_count):
    blocks, capacity, blk, _ = gate_tiles.shape
    mine, width = inputs.shape
    tokens = mine * n
    smem = pl.BlockSpec(memory_space=pltpu.SMEM)
    vmem = pl.BlockSpec(memory_space=pltpu.VMEM)
    hbm = pl.BlockSpec(memory_space=pltpu.HBM)
    tile_bytes = blocks * capacity * blk * blk * 2
    tiles_in = [
        pltpu.with_memory_space_constraint(t, pltpu.HBM) for t in (gate_tiles, up_tiles, down_tiles)
    ]

    def cost(products, tiles, part=1.0):
        return pl.CostEstimate(
            flops=int(products * tokens * tile_bytes * part),
            bytes_accessed=int(tiles * tile_bytes * part),
            transcendentals=0,
        )

    listed = pltpu.SMEM((blocks * (capacity // CHUNK) + capacity // CHUNK + STEP,), jnp.int32)
    live, item_block, item_slot, total, x_held, dy_held = pl.pallas_call(
        functools.partial(seed_kernel, width // blk),
        in_specs=[smem, smem, vmem, vmem],
        out_specs=[smem] * 4 + [vmem] * 2,
        out_shape=[
            pltpu.SMEM((blocks + 1, capacity), jnp.int32),
            listed,
            listed,
            pltpu.SMEM((1,), jnp.int32),
        ]
        + [pltpu.VMEM((n // 2, mine, width), inputs.dtype)] * 2,
        name="seed",
    )(kept_rows, kept_count, inputs, cotangent)
    cores = (1, 1)
    first, second = hop_orders(n)
    x_hops, dy_hops = list(zip(first, second)), list(zip(second, first))
    x_held = gather_hops(x_held, inputs, x_hops, n)
    dy_held = gather_hops(dy_held, cotangent, dy_hops, n)
    x_near, x_far = [rows_of(v, False) for v in (x_held, swap(x_held, cores, n))]
    dy_near, dy_far = [rows_of(v, True) for v in (dy_held, swap(dy_held, cores, n))]

    padded = pltpu.VMEM((width // blk + 1, tokens, blk), jnp.bfloat16)
    acc = pltpu.VMEM((width // blk + 1, tokens, blk), jnp.float32)
    hidden, d, xpad, dypad, keep, send = pl.pallas_call(
        layer_kernel,
        in_specs=[smem] * 4 + [vmem] * 4 + [hbm] * 3,
        out_specs=[vmem] * 6,
        out_shape=[
            pltpu.VMEM((blocks + 1, tokens, blk), jnp.bfloat16),
            pltpu.VMEM((blocks + 1, tokens, 2 * blk), jnp.bfloat16),
            padded,
            padded,
            pltpu.VMEM((2, tokens // 2, width), jnp.float32),
            pltpu.VMEM((2, tokens // 2, width), jnp.bfloat16),
        ],
        scratch_shapes=[acc, acc, pltpu.VMEM((blocks + 1, tokens, 3 * blk), jnp.float32)]
        + [pltpu.VMEM(gate_tiles.shape, jnp.bfloat16)] * 3
        + [pltpu.SemaphoreType.DMA((3, blocks))],
        compiler_params=pltpu.CompilerParams(vmem_limit_bytes=40 * 1024 * 1024),
        cost_estimate=cost(6, 3),
        name="layer",
    )(live, item_block, item_slot, total, x_near, x_far, dy_near, dy_far, *tiles_in)

    def grads(products, pad, factor, first, count, outs, earlier, after, name):
        behind = len(earlier) + len(after)
        return pl.pallas_call(
            functools.partial(grad_kernel, products, first, count, outs, behind),
            in_specs=[smem, vmem, vmem]
            + [hbm] * len(earlier)
            + [pl.BlockSpec(memory_space=pl.ANY)] * len(after),
            out_specs=[hbm] * outs,
            out_shape=[jax.ShapeDtypeStruct(gate_tiles.shape, jnp.bfloat16)] * outs,
            scratch_shapes=[pltpu.VMEM((count,) + gate_tiles.shape[1:], jnp.bfloat16)] * outs
            + [pltpu.SemaphoreType.DMA((outs, count, 2))],
            input_output_aliases={3 + k: k for k in range(len(earlier))},
            compiler_params=pltpu.CompilerParams(vmem_limit_bytes=24 * 1024 * 1024),
            cost_estimate=cost(outs, outs, count / blocks),
            name=name,
        )(live, pad, factor, *earlier, *after)

    third = -(-blocks // 3)
    cuts = {0: (0, third), 2: (third, 2 * third), 3: (2 * third, blocks)}
    gate_up, down_grad, after = [], None, []
    for i, bits in enumerate([cores] + x_hops[::-1]):
        got = swap(send, bits, n)
        done = []
        if i == 1:
            (down_grad,) = grads(
                down_products, dypad, hidden, 0, blocks, 1, [], after, "down_grad"
            )
            done = [down_grad]
        elif i in cuts:
            first, last = cuts[i]
            gate_up = grads(
                gate_up_products, xpad, d, first, last - first, 2, gate_up, after, "gate_up_grad"
            )
            done = gate_up
        total = keep + got.astype(jnp.float32)
        if i < len(x_hops):
            half = total.shape[1] // 2
            keep, send = total[:, :half], total[:, half:].astype(jnp.bfloat16)
            send, done = lax.optimization_barrier((send, done))
            after = [send]
            if i == 1:
                (down_grad,) = done
            elif i in cuts:
                gate_up = done
    total = total.astype(jnp.bfloat16)
    return total[0], total[1], gate_up[0], gate_up[1], down_grad


def solution(mesh):
    tiles = P("col", None, None, None)
    tokens = P(("groups", "col"), None)
    grads = P(("groups", "col"), None, None, None)
    return jax.shard_map(
        functools.partial(local, mesh.shape["col"]),
        mesh=mesh,
        in_specs=(tokens, tokens, tiles, tiles, tiles, P("col", None), P("col")),
        out_specs=(tokens, tokens, grads, grads, grads),
        check_vma=False,
    )
```

```python
import functools

import jax
import jax.numpy as jnp
from jax import lax
from jax.experimental import pallas as pl
from jax.experimental.pallas import tpu as pltpu
from jax.sharding import PartitionSpec as P

NT = (((1,), (1,)), ((), ()))
TN = (((0,), (0,)), ((), ()))
CHUNK = 4
STEP = 4
LAG = 2


def seed_kernel(dead, rows_ref, count_ref, x_ref, dy_ref, live_ref, block_ref, slot_ref, full_ref, total_ref, x_held, dy_held):
    x_held[0] = x_ref[...]
    dy_held[0] = dy_ref[...]
    blocks, capacity = rows_ref.shape
    chunks = capacity // CHUNK

    def block(c, position):
        count = count_ref[c]
        for s in range(capacity):
            live_ref[c, s] = jnp.where(s < count, rows_ref[c, s], dead)
        for q in range(chunks):
            block_ref[position + q] = c
            slot_ref[position + q] = q * CHUNK
        full = jnp.clip((count + CHUNK - 1) // CHUNK, 1, chunks)
        full_ref[c] = full
        return position + full

    total = lax.fori_loop(0, blocks, block, 0)
    total_ref[0] = total
    for s in range(capacity):
        live_ref[blocks, s] = dead
    for i in range(STEP):
        block_ref[total + i] = blocks
        slot_ref[total + i] = 0


def add_to_rows(acc, rows, parts, blk):
    old = [acc[r] for r in rows]
    for i, r in enumerate(rows):
        acc[r] = old[i] + parts[:, i * blk : (i + 1) * blk]


def tile_copies(sources, targets, sems, c):
    return [
        pltpu.make_async_copy(src.at[c], dst.at[c], sems.at[i, c])
        for i, (src, dst) in enumerate(zip(sources, targets))
    ]


def row_blocks(pad, near, far):
    half = near.shape[0]
    count, _, blk = pad.shape
    for r in range(count - 1):
        pad[r, :half] = near[:, r * blk : (r + 1) * blk]
        pad[r, half:] = far[:, r * blk : (r + 1) * blk]
    pad[count - 1] = jnp.zeros(pad.shape[1:], pad.dtype)


def layer_kernel(
    live_ref, block_ref, slot_ref, full_ref, total_ref, x_near, x_far, dy_near, dy_far, wg_hbm, wu_hbm, wd_hbm,
    hidden_ref, d_ref, xpad_ref, dypad_ref, keep_ref, send_ref, gate_grad, up_grad, down_grad,
    out_acc, grad_acc, pre_acc, wg_ref, wu_ref, wd_ref, sems, zeros, zero_sems,
):
    half = x_near.shape[0]
    blocks, capacity, blk, _ = wg_ref.shape
    copies = functools.partial(
        tile_copies, (wg_hbm, wu_hbm, wd_hbm), (wg_ref, wu_ref, wd_ref), sems
    )
    for c in range(blocks):
        for copy in copies(c):
            copy.start()
    row_blocks(xpad_ref, x_near, x_far)
    row_blocks(dypad_ref, dy_near, dy_far)
    out_acc[...] = jnp.zeros_like(out_acc)
    grad_acc[...] = jnp.zeros_like(grad_acc)
    pre_acc[...] = jnp.zeros_like(pre_acc)

    def item(position):
        c, s = block_ref[position], slot_ref[position]
        rows = [live_ref[c, s + i] for i in range(CHUNK)]
        return c, s, rows, jnp.where(c < blocks, c, 0)

    def arrived(g):
        before = jnp.where(g > 0, block_ref[jnp.maximum(g * STEP - 1, 0)] + 1, 0)
        after = jnp.minimum(block_ref[g * STEP + STEP - 1] + 1, blocks)

        def wait(c, carry):
            for copy in copies(c):
                copy.wait()
            return carry

        lax.fori_loop(before, after, wait, 0)

    def gate_up_tiles(tiles, s):
        return jnp.concatenate(
            [ref[tiles, pl.ds(s, CHUNK)].reshape(CHUNK * blk, blk) for ref in (wg_ref, wu_ref)],
            axis=1,
        )

    def down_tiles(tiles, s):
        return jnp.concatenate([wd_ref[tiles, s + i] for i in range(CHUNK)], axis=1)

    def inward(position):
        c, s, rows, tiles = item(position)
        xg = jnp.concatenate([xpad_ref[r] for r in rows], axis=1)
        dyg = jnp.concatenate([dypad_ref[r] for r in rows], axis=1)
        pre = jnp.dot(xg, gate_up_tiles(tiles, s), preferred_element_type=jnp.float32)
        d_hidden = lax.dot_general(
            dyg, down_tiles(tiles, s), NT, preferred_element_type=jnp.float32
        )
        pre_acc[c, :, : 2 * blk] += pre
        pre_acc[c, :, 2 * blk :] += d_hidden

    def outward(position):
        c, s, rows, tiles = item(position)
        gate, up, d_hidden = [pre_acc[c, :, i * blk : (i + 1) * blk] for i in range(3)]
        sig = 1.0 / (1.0 + jnp.exp(-gate))
        act = gate * sig
        hidden = (act * up).astype(jnp.bfloat16)
        d_gate = (d_hidden * up * sig * (1.0 + gate * (1.0 - sig))).astype(jnp.bfloat16)
        d = jnp.concatenate([d_gate, (d_hidden * act).astype(jnp.bfloat16)], axis=1)
        hidden_ref[c] = hidden
        d_ref[c] = d
        y = jnp.dot(hidden, down_tiles(tiles, s), preferred_element_type=jnp.float32)
        x_slots = lax.dot_general(
            d, gate_up_tiles(tiles, s), NT, preferred_element_type=jnp.float32
        )
        add_to_rows(out_acc, rows, y, blk)
        add_to_rows(grad_acc, rows, x_slots, blk)

    def step(g, do_inward, do_outward):
        if do_inward:
            arrived(g)
        if do_outward:
            for i in range(STEP):
                outward((g - LAG) * STEP + i)
        if do_inward:
            for i in range(STEP):
                inward(g * STEP + i)

    def dead_chunks(act):
        def block(c, carry):
            def chunk(q, inner):
                part = pl.ds(q * CHUNK, CHUNK)
                for k, grad in enumerate((gate_grad, up_grad, down_grad)):
                    act(pltpu.make_async_copy(zeros, grad.at[c, part], zero_sems.at[k, c, q]))
                return inner

            return lax.fori_loop(full_ref[c], capacity // CHUNK, chunk, carry)

        lax.fori_loop(0, blocks, block, 0)

    zeros[...] = jnp.zeros_like(zeros)
    steps = (total_ref[0] + STEP - 1) // STEP
    lag = jnp.minimum(steps, LAG)

    def loop(first, last, *parts):
        def body(g, carry):
            step(g, *parts)
            return carry

        lax.fori_loop(first, last, body, 0)

    loop(0, lag, True, False)
    dead_chunks(lambda copy: copy.start())
    loop(LAG, steps, True, True)
    loop(steps - lag + LAG, steps + LAG, False, True)
    for r in range(out_acc.shape[0] - 1):
        columns = slice(r * blk, (r + 1) * blk)
        for i, acc in enumerate((out_acc, grad_acc)):
            keep_ref[i, :, columns] = acc[r, :half]
            send_ref[i, :, columns] = acc[r, half:].astype(send_ref.dtype)
    dead_chunks(lambda copy: copy.wait())


def gate_up_products(pad_ref, d, rows, blk, stages, i):
    for s in range(0, CHUNK, 2):
        xs = jnp.concatenate([pad_ref[r] for r in rows[s : s + 2]], axis=1)
        full = lax.dot_general(xs, d, TN, preferred_element_type=jnp.float32)
        full = full.astype(jnp.bfloat16)
        for k in range(2):
            stages[0][i, s + k] = full[k * blk : (k + 1) * blk, :blk]
            stages[1][i, s + k] = full[k * blk : (k + 1) * blk, blk:]


def down_products(pad_ref, hidden, rows, blk, stages, i):
    dys = jnp.concatenate([pad_ref[r] for r in rows], axis=1)
    full = lax.dot_general(hidden, dys, TN, preferred_element_type=jnp.float32)
    full = full.astype(jnp.bfloat16)
    for k in range(CHUNK):
        stages[0][i, k] = full[:, k * blk : (k + 1) * blk]


def grad_kernel(products, first, last, cuts, outs, after, *refs):
    live_ref, block_ref, slot_ref, total_ref, pad_ref, factor_ref = refs[:6]
    grad_refs = refs[6 + outs + after : 6 + 2 * outs + after]
    stages = refs[6 + 2 * outs + after : -1]
    sems = refs[-1]
    blk = stages[0].shape[-1]
    begin = total_ref[0] * first // cuts
    end = total_ref[0] * last // cuts

    def copies(i):
        c, part = block_ref[begin + i], pl.ds(slot_ref[begin + i], CHUNK)
        return [
            pltpu.make_async_copy(stage.at[i], grad.at[c, part], sems.at[k, i])
            for k, (stage, grad) in enumerate(zip(stages, grad_refs))
        ]

    def step(g, carry):
        for k in range(STEP):
            i = g * STEP + k
            c, s = block_ref[begin + i], slot_ref[begin + i]
            rows = [live_ref[c, s + j] for j in range(CHUNK)]
            products(pad_ref, factor_ref[c], rows, blk, stages, i)
        for k in range(STEP):
            i = g * STEP + k

            @pl.when(begin + i < end)
            def _():
                for copy in copies(i):
                    copy.start()

        return carry

    def finish(i, carry):
        for copy in copies(i):
            copy.wait()
        return carry

    lax.fori_loop(0, (end - begin + STEP - 1) // STEP, step, 0)
    lax.fori_loop(0, end - begin, finish, 0)


def hop_orders(n):
    bits = [1 << i for i in range(n.bit_length() - 2, 0, -1)]
    return bits, bits[:-2] + bits[:-3:-1]


def swap(value, bits, n):
    return lax.ppermute(value, "col", [(j, j ^ bits[j % 2]) for j in range(n)])


def gather_hops(held, value, hops, n):
    send = value[None]
    for i, bits in enumerate(hops):
        if i:
            send = held[: 1 << i]
        held = lax.dynamic_update_slice_in_dim(held, swap(send, bits, n), 1 << i, 0)
    return held


def rows_of(held, swapped):
    pieces, mine, width = held.shape
    if swapped:
        held = held.reshape(2, 2, pieces // 4, mine, width).transpose(1, 0, 2, 3, 4)
    return held.reshape(pieces * mine, width)


def local(n, inputs, cotangent, gate_tiles, up_tiles, down_tiles, kept_rows, kept_count):
    blocks, capacity, blk, _ = gate_tiles.shape
    mine, width = inputs.shape
    tokens = mine * n
    smem = pl.BlockSpec(memory_space=pltpu.SMEM)
    vmem = pl.BlockSpec(memory_space=pltpu.VMEM)
    hbm = pl.BlockSpec(memory_space=pltpu.HBM)
    tile_bytes = blocks * capacity * blk * blk * 2
    tiles_in = [
        pltpu.with_memory_space_constraint(t, pltpu.HBM) for t in (gate_tiles, up_tiles, down_tiles)
    ]

    def cost(products, tiles, part=1.0):
        return pl.CostEstimate(
            flops=int(products * tokens * tile_bytes * part),
            bytes_accessed=int(tiles * tile_bytes * part),
            transcendentals=0,
        )

    listed = pltpu.SMEM((blocks * (capacity // CHUNK) + capacity // CHUNK + STEP,), jnp.int32)
    live, item_block, item_slot, full, total, x_held, dy_held = pl.pallas_call(
        functools.partial(seed_kernel, width // blk),
        in_specs=[smem, smem, vmem, vmem],
        out_specs=[smem] * 5 + [vmem] * 2,
        out_shape=[
            pltpu.SMEM((blocks + 1, capacity), jnp.int32),
            listed,
            listed,
            pltpu.SMEM((blocks,), jnp.int32),
            pltpu.SMEM((1,), jnp.int32),
        ]
        + [pltpu.VMEM((n // 2, mine, width), inputs.dtype)] * 2,
        name="seed",
    )(kept_rows, kept_count, inputs, cotangent)
    cores = (1, 1)
    first, second = hop_orders(n)
    x_hops, dy_hops = list(zip(first, second)), list(zip(second, first))
    x_held = gather_hops(x_held, inputs, x_hops, n)
    dy_held = gather_hops(dy_held, cotangent, dy_hops, n)
    x_near, x_far = [rows_of(v, False) for v in (x_held, swap(x_held, cores, n))]
    dy_near, dy_far = [rows_of(v, True) for v in (dy_held, swap(dy_held, cores, n))]

    padded = pltpu.VMEM((width // blk + 1, tokens, blk), jnp.bfloat16)
    acc = pltpu.VMEM((width // blk + 1, tokens, blk), jnp.float32)
    hidden, d, xpad, dypad, keep, send, gate_grad, up_grad, down_grad = pl.pallas_call(
        layer_kernel,
        in_specs=[smem] * 5 + [vmem] * 4 + [hbm] * 3,
        out_specs=[vmem] * 6 + [hbm] * 3,
        out_shape=[
            pltpu.VMEM((blocks + 1, tokens, blk), jnp.bfloat16),
            pltpu.VMEM((blocks + 1, tokens, 2 * blk), jnp.bfloat16),
            padded,
            padded,
            pltpu.VMEM((2, tokens // 2, width), jnp.float32),
            pltpu.VMEM((2, tokens // 2, width), jnp.bfloat16),
        ]
        + [jax.ShapeDtypeStruct(gate_tiles.shape, jnp.bfloat16)] * 3,
        scratch_shapes=[acc, acc, pltpu.VMEM((blocks + 1, tokens, 3 * blk), jnp.float32)]
        + [pltpu.VMEM(gate_tiles.shape, jnp.bfloat16)] * 3
        + [
            pltpu.SemaphoreType.DMA((3, blocks)),
            pltpu.VMEM((CHUNK, blk, blk), jnp.bfloat16),
            pltpu.SemaphoreType.DMA((3, blocks, capacity // CHUNK)),
        ],
        compiler_params=pltpu.CompilerParams(vmem_limit_bytes=40 * 1024 * 1024),
        cost_estimate=cost(6, 3),
        name="layer",
    )(live, item_block, item_slot, full, total, x_near, x_far, dy_near, dy_far, *tiles_in)

    def grads(products, pad, factor, first, last, cuts, earlier, after, name):
        outs = len(earlier)
        most = -(-blocks * (capacity // CHUNK) * (last - first) // cuts) + STEP
        return pl.pallas_call(
            functools.partial(grad_kernel, products, first, last, cuts, outs, len(after)),
            in_specs=[smem] * 4
            + [vmem] * 2
            + [hbm] * outs
            + [pl.BlockSpec(memory_space=pl.ANY)] * len(after),
            out_specs=[hbm] * outs,
            out_shape=[jax.ShapeDtypeStruct(gate_tiles.shape, jnp.bfloat16)] * outs,
            scratch_shapes=[pltpu.VMEM((most, CHUNK, blk, blk), jnp.bfloat16)] * outs
            + [pltpu.SemaphoreType.DMA((outs, most))],
            input_output_aliases={6 + k: k for k in range(outs)},
            compiler_params=pltpu.CompilerParams(vmem_limit_bytes=24 * 1024 * 1024),
            cost_estimate=cost(outs, outs, (last - first) / cuts),
            name=name,
        )(live, item_block, item_slot, total_chunks, pad, factor, *earlier, *after)

    total_chunks = total
    cuts = {0: (0, 1), 2: (1, 2), 3: (2, 3)}
    gate_up, after = [gate_grad, up_grad], []
    for i, bits in enumerate([cores] + x_hops[::-1]):
        got = swap(send, bits, n)
        done = []
        if i == 1:
            done = grads(down_products, dypad, hidden, 0, 1, 1, [down_grad], after, "down_grad")
        elif i in cuts:
            first, last = cuts[i]
            done = gate_up = grads(
                gate_up_products, xpad, d, first, last, 3, gate_up, after, "gate_up_grad"
            )
        total = keep + got.astype(jnp.float32)
        if i < len(x_hops):
            half = total.shape[1] // 2
            keep, send = total[:, :half], total[:, half:].astype(jnp.bfloat16)
            send, done = lax.optimization_barrier((send, done))
            after = [send]
            if i == 1:
                (down_grad,) = done
            elif i in cuts:
                gate_up = done
    total = total.astype(jnp.bfloat16)
    return total[0], total[1], gate_up[0], gate_up[1], down_grad


def solution(mesh):
    tiles = P("col", None, None, None)
    tokens = P(("groups", "col"), None)
    grads = P(("groups", "col"), None, None, None)
    return jax.shard_map(
        functools.partial(local, mesh.shape["col"]),
        mesh=mesh,
        in_specs=(tokens, tokens, tiles, tiles, tiles, P("col", None), P("col")),
        out_specs=(tokens, tokens, grads, grads, grads),
        check_vma=False,
    )
```

```python
import functools

import jax
import jax.numpy as jnp
from jax import lax
from jax.experimental import pallas as pl
from jax.experimental.pallas import tpu as pltpu
from jax.sharding import PartitionSpec as P

NT = (((1,), (1,)), ((), ()))
TN = (((0,), (0,)), ((), ()))
CHUNK = 4
STEP = 4
LAG = 2


def seed_kernel(dead, rows_ref, count_ref, x_ref, dy_ref, live_ref, block_ref, slot_ref, total_ref, x_held, dy_held):
    x_held[0] = x_ref[...]
    dy_held[0] = dy_ref[...]
    blocks, capacity = rows_ref.shape
    chunks = capacity // CHUNK

    def block(c, position):
        count = count_ref[c]
        for s in range(capacity):
            live_ref[c, s] = jnp.where(s < count, rows_ref[c, s], dead)
        for q in range(chunks):
            block_ref[position + q] = c
            slot_ref[position + q] = q * CHUNK
        return position + jnp.clip((count + CHUNK - 1) // CHUNK, 1, chunks)

    total = lax.fori_loop(0, blocks, block, 0)
    total_ref[0] = total
    for s in range(capacity):
        live_ref[blocks, s] = dead
    for i in range(STEP):
        block_ref[total + i] = blocks
        slot_ref[total + i] = 0


def add_to_rows(acc, rows, parts, blk):
    old = [acc[r] for r in rows]
    for i, r in enumerate(rows):
        acc[r] = old[i] + parts[:, i * blk : (i + 1) * blk]


def row_blocks(pad, near, far):
    half = near.shape[0]
    count, _, blk = pad.shape
    for r in range(count - 1):
        pad[r, :half] = near[:, r * blk : (r + 1) * blk]
        pad[r, half:] = far[:, r * blk : (r + 1) * blk]
    pad[count - 1] = jnp.zeros(pad.shape[1:], pad.dtype)


def layer_kernel(
    live_ref, block_ref, slot_ref, total_ref, x_near, x_far, dy_near, dy_far, wg_hbm, wu_hbm, wd_hbm,
    hidden_ref, d_ref, xpad_ref, dypad_ref, keep_ref, send_ref,
    out_acc, grad_acc, pre_acc, tiles_ref, sems,
):
    half = x_near.shape[0]
    blocks, _, capacity, blk, _ = tiles_ref.shape
    for c in range(blocks):
        for k, source in enumerate((wg_hbm, wu_hbm, wd_hbm)):
            pltpu.make_async_copy(source.at[c], tiles_ref.at[c, k], sems.at[c]).start()
    row_blocks(xpad_ref, x_near, x_far)
    row_blocks(dypad_ref, dy_near, dy_far)
    out_acc[...] = jnp.zeros_like(out_acc)
    grad_acc[...] = jnp.zeros_like(grad_acc)
    pre_acc[...] = jnp.zeros_like(pre_acc)

    def item(position):
        c, s = block_ref[position], slot_ref[position]
        rows = [live_ref[c, s + i] for i in range(CHUNK)]
        return c, s, rows, jnp.where(c < blocks, c, 0)

    def arrived(g):
        before = jnp.where(g > 0, block_ref[jnp.maximum(g * STEP - 1, 0)] + 1, 0)
        after = jnp.minimum(block_ref[g * STEP + STEP - 1] + 1, blocks)

        def wait(c, carry):
            pltpu.make_async_copy(tiles_ref.at[c], tiles_ref.at[c], sems.at[c]).wait()
            return carry

        lax.fori_loop(before, after, wait, 0)

    def gate_up_tiles(tiles, s):
        return jnp.concatenate(
            [tiles_ref[tiles, k, pl.ds(s, CHUNK)].reshape(CHUNK * blk, blk) for k in range(2)],
            axis=1,
        )

    def down_tiles(tiles, s):
        return jnp.concatenate([tiles_ref[tiles, 2, s + i] for i in range(CHUNK)], axis=1)

    def inward(position):
        c, s, rows, tiles = item(position)
        xg = jnp.concatenate([xpad_ref[r] for r in rows], axis=1)
        dyg = jnp.concatenate([dypad_ref[r] for r in rows], axis=1)
        pre = jnp.dot(xg, gate_up_tiles(tiles, s), preferred_element_type=jnp.float32)
        d_hidden = lax.dot_general(
            dyg, down_tiles(tiles, s), NT, preferred_element_type=jnp.float32
        )
        pre_acc[c, :, : 2 * blk] += pre
        pre_acc[c, :, 2 * blk :] += d_hidden

    def outward(position):
        c, s, rows, tiles = item(position)
        gate, up, d_hidden = [pre_acc[c, :, i * blk : (i + 1) * blk] for i in range(3)]
        sig = 1.0 / (1.0 + jnp.exp(-gate))
        act = gate * sig
        hidden = (act * up).astype(jnp.bfloat16)
        d_gate = (d_hidden * up * sig * (1.0 + gate * (1.0 - sig))).astype(jnp.bfloat16)
        d = jnp.concatenate([d_gate, (d_hidden * act).astype(jnp.bfloat16)], axis=1)
        hidden_ref[c] = hidden
        d_ref[c] = d
        y = jnp.dot(hidden, down_tiles(tiles, s), preferred_element_type=jnp.float32)
        x_slots = lax.dot_general(
            d, gate_up_tiles(tiles, s), NT, preferred_element_type=jnp.float32
        )
        add_to_rows(out_acc, rows, y, blk)
        add_to_rows(grad_acc, rows, x_slots, blk)

    def step(g, do_inward, do_outward):
        if do_inward:
            arrived(g)
        if do_outward:
            for i in range(STEP):
                outward((g - LAG) * STEP + i)
        if do_inward:
            for i in range(STEP):
                inward(g * STEP + i)

    steps = (total_ref[0] + STEP - 1) // STEP
    lag = jnp.minimum(steps, LAG)

    def loop(first, last, *parts):
        def body(g, carry):
            step(g, *parts)
            return carry

        lax.fori_loop(first, last, body, 0)

    loop(0, lag, True, False)
    loop(LAG, steps, True, True)
    loop(steps - lag + LAG, steps + LAG, False, True)
    for r in range(out_acc.shape[0] - 1):
        columns = slice(r * blk, (r + 1) * blk)
        for i, acc in enumerate((out_acc, grad_acc)):
            keep_ref[i, :, columns] = acc[r, :half]
            send_ref[i, :, columns] = acc[r, half:].astype(send_ref.dtype)


def gate_up_products(pad_ref, d, rows, slots, blk, stages, i):
    for s in slots[::2]:
        xs = jnp.concatenate([pad_ref[r] for r in rows[s : s + 2]], axis=1)
        full = lax.dot_general(xs, d, TN, preferred_element_type=jnp.float32)
        full = full.astype(jnp.bfloat16)
        for k in range(2):
            stages[0][i, s + k] = full[k * blk : (k + 1) * blk, :blk]
            stages[1][i, s + k] = full[k * blk : (k + 1) * blk, blk:]


def down_products(pad_ref, hidden, rows, slots, blk, stages, i):
    for s in slots[::CHUNK]:
        dys = jnp.concatenate([pad_ref[r] for r in rows[s : s + CHUNK]], axis=1)
        full = lax.dot_general(hidden, dys, TN, preferred_element_type=jnp.float32)
        full = full.astype(jnp.bfloat16)
        for k in range(CHUNK):
            stages[0][i, s + k] = full[:, k * blk : (k + 1) * blk]


def grad_kernel(products, first, count, outs, behind, *refs):
    live_ref, pad_ref, factor_ref = refs[:3]
    grad_refs = refs[3 + behind : 3 + behind + outs]
    stages = refs[3 + behind + outs : -1]
    sems = refs[-1]
    capacity, blk = stages[0].shape[1], stages[0].shape[-1]
    cut = capacity // 2 // CHUNK * CHUNK
    parts = (range(cut), range(cut, capacity))

    def copies(i, h):
        part = pl.ds(parts[h].start, len(parts[h]))
        return [
            pltpu.make_async_copy(stage.at[i, part], grad.at[first + i, part], sems.at[k, i, h])
            for k, (stage, grad) in enumerate(zip(stages, grad_refs))
        ]

    group = 2 if count % 2 == 0 else 1

    def step(g, carry):
        some = [g * group + k for k in range(group)]
        rows = [[live_ref[first + i, s] for s in range(capacity)] for i in some]
        for i, names in zip(some, rows):
            for h in range(2):
                products(pad_ref, factor_ref[first + i], names, parts[h], blk, stages, i)
                for copy in copies(i, h):
                    copy.start()
        return carry

    lax.fori_loop(0, count // group, step, 0)
    for i in range(count):
        for h in range(2):
            for copy in copies(i, h):
                copy.wait()


def hop_orders(n):
    bits = [1 << i for i in range(n.bit_length() - 2, 0, -1)]
    return bits, bits[:-2] + bits[:-3:-1]


def swap(value, bits, n):
    return lax.ppermute(value, "col", [(j, j ^ bits[j % 2]) for j in range(n)])


def gather_hops(held, value, hops, n):
    send = value[None]
    for i, bits in enumerate(hops):
        if i:
            send = held[: 1 << i]
        held = lax.dynamic_update_slice_in_dim(held, swap(send, bits, n), 1 << i, 0)
    return held


def rows_of(held, swapped):
    pieces, mine, width = held.shape
    if swapped:
        held = held.reshape(2, 2, pieces // 4, mine, width).transpose(1, 0, 2, 3, 4)
    return held.reshape(pieces * mine, width)


def local(n, inputs, cotangent, gate_tiles, up_tiles, down_tiles, kept_rows, kept_count):
    blocks, capacity, blk, _ = gate_tiles.shape
    mine, width = inputs.shape
    tokens = mine * n
    smem = pl.BlockSpec(memory_space=pltpu.SMEM)
    vmem = pl.BlockSpec(memory_space=pltpu.VMEM)
    hbm = pl.BlockSpec(memory_space=pltpu.HBM)
    tile_bytes = blocks * capacity * blk * blk * 2
    tiles_in = [
        pltpu.with_memory_space_constraint(t, pltpu.HBM) for t in (gate_tiles, up_tiles, down_tiles)
    ]

    def cost(products, tiles, part=1.0):
        return pl.CostEstimate(
            flops=int(products * tokens * tile_bytes * part),
            bytes_accessed=int(tiles * tile_bytes * part),
            transcendentals=0,
        )

    listed = pltpu.SMEM((blocks * (capacity // CHUNK) + capacity // CHUNK + STEP,), jnp.int32)
    live, item_block, item_slot, total, x_held, dy_held = pl.pallas_call(
        functools.partial(seed_kernel, width // blk),
        in_specs=[smem, smem, vmem, vmem],
        out_specs=[smem] * 4 + [vmem] * 2,
        out_shape=[
            pltpu.SMEM((blocks + 1, capacity), jnp.int32),
            listed,
            listed,
            pltpu.SMEM((1,), jnp.int32),
        ]
        + [pltpu.VMEM((n // 2, mine, width), inputs.dtype)] * 2,
        name="seed",
    )(kept_rows, kept_count, inputs, cotangent)
    cores = (1, 1)
    first, second = hop_orders(n)
    x_hops, dy_hops = list(zip(first, second)), list(zip(second, first))
    x_held = gather_hops(x_held, inputs, x_hops, n)
    dy_held = gather_hops(dy_held, cotangent, dy_hops, n)
    x_near, x_far = [rows_of(v, False) for v in (x_held, swap(x_held, cores, n))]
    dy_near, dy_far = [rows_of(v, True) for v in (dy_held, swap(dy_held, cores, n))]

    padded = pltpu.VMEM((width // blk + 1, tokens, blk), jnp.bfloat16)
    acc = pltpu.VMEM((width // blk + 1, tokens, blk), jnp.float32)
    hidden, d, xpad, dypad, keep, send = pl.pallas_call(
        layer_kernel,
        in_specs=[smem] * 4 + [vmem] * 4 + [hbm] * 3,
        out_specs=[vmem] * 6,
        out_shape=[
            pltpu.VMEM((blocks + 1, tokens, blk), jnp.bfloat16),
            pltpu.VMEM((blocks + 1, tokens, 2 * blk), jnp.bfloat16),
            padded,
            padded,
            pltpu.VMEM((2, tokens // 2, width), jnp.float32),
            pltpu.VMEM((2, tokens // 2, width), jnp.bfloat16),
        ],
        scratch_shapes=[acc, acc, pltpu.VMEM((blocks + 1, tokens, 3 * blk), jnp.float32)]
        + [
            pltpu.VMEM((blocks, 3) + gate_tiles.shape[1:], jnp.bfloat16),
            pltpu.SemaphoreType.DMA((blocks,)),
        ],
        compiler_params=pltpu.CompilerParams(vmem_limit_bytes=40 * 1024 * 1024),
        cost_estimate=cost(6, 3),
        name="layer",
    )(live, item_block, item_slot, total, x_near, x_far, dy_near, dy_far, *tiles_in)

    def grads(products, pad, factor, first, count, outs, earlier, after, name):
        behind = len(earlier) + len(after)
        return pl.pallas_call(
            functools.partial(grad_kernel, products, first, count, outs, behind),
            in_specs=[smem, vmem, vmem]
            + [hbm] * len(earlier)
            + [pl.BlockSpec(memory_space=pl.ANY)] * len(after),
            out_specs=[hbm] * outs,
            out_shape=[jax.ShapeDtypeStruct(gate_tiles.shape, jnp.bfloat16)] * outs,
            scratch_shapes=[pltpu.VMEM((count,) + gate_tiles.shape[1:], jnp.bfloat16)] * outs
            + [pltpu.SemaphoreType.DMA((outs, count, 2))],
            input_output_aliases={3 + k: k for k in range(len(earlier))},
            compiler_params=pltpu.CompilerParams(vmem_limit_bytes=24 * 1024 * 1024),
            cost_estimate=cost(outs, outs, count / blocks),
            name=name,
        )(live, pad, factor, *earlier, *after)

    third = -(-blocks // 3)
    cuts = {0: (0, third), 2: (third, 2 * third), 3: (2 * third, blocks)}
    gate_up, down_grad, after = [], None, []
    for i, bits in enumerate([cores] + x_hops[::-1]):
        got = swap(send, bits, n)
        done = []
        if i == 1:
            (down_grad,) = grads(
                down_products, dypad, hidden, 0, blocks, 1, [], after, "down_grad"
            )
            done = [down_grad]
        elif i in cuts:
            first, last = cuts[i]
            gate_up = grads(
                gate_up_products, xpad, d, first, last - first, 2, gate_up, after, "gate_up_grad"
            )
            done = gate_up
        total = keep + got.astype(jnp.float32)
        if i < len(x_hops):
            half = total.shape[1] // 2
            keep, send = total[:, :half], total[:, half:].astype(jnp.bfloat16)
            send, done = lax.optimization_barrier((send, done))
            after = [send]
            if i == 1:
                (down_grad,) = done
            elif i in cuts:
                gate_up = done
    total = total.astype(jnp.bfloat16)
    return total[0], total[1], gate_up[0], gate_up[1], down_grad


def solution(mesh):
    tiles = P("col", None, None, None)
    tokens = P(("groups", "col"), None)
    grads = P(("groups", "col"), None, None, None)
    return jax.shard_map(
        functools.partial(local, mesh.shape["col"]),
        mesh=mesh,
        in_specs=(tokens, tokens, tiles, tiles, tiles, P("col", None), P("col")),
        out_specs=(tokens, tokens, grads, grads, grads),
        check_vma=False,
    )
```

```python
import functools

import jax
import jax.numpy as jnp
from jax import lax
from jax.experimental import pallas as pl
from jax.experimental.pallas import tpu as pltpu
from jax.sharding import PartitionSpec as P

NT = (((1,), (1,)), ((), ()))
TN = (((0,), (0,)), ((), ()))
CHUNK = 4
STEP = 6
LAG = 2


def seed_kernel(dead, rows_ref, count_ref, x_ref, dy_ref, live_ref, block_ref, slot_ref, total_ref, x_held, dy_held):
    x_held[0] = x_ref[...]
    dy_held[0] = dy_ref[...]
    blocks, capacity = rows_ref.shape
    chunks = capacity // CHUNK

    def block(c, position):
        count = count_ref[c]
        for s in range(capacity):
            live_ref[c, s] = jnp.where(s < count, rows_ref[c, s], dead)
        for q in range(chunks):
            block_ref[position + q] = c
            slot_ref[position + q] = q * CHUNK
        return position + jnp.clip((count + CHUNK - 1) // CHUNK, 1, chunks)

    total = lax.fori_loop(0, blocks, block, 0)
    total_ref[0] = total
    for s in range(capacity):
        live_ref[blocks, s] = dead
    for i in range(STEP):
        block_ref[total + i] = blocks
        slot_ref[total + i] = 0


def add_to_rows(acc, rows, parts, blk):
    old = [acc[r] for r in rows]
    for i, r in enumerate(rows):
        acc[r] = old[i] + parts[:, i * blk : (i + 1) * blk]


def row_blocks(pad, near, far):
    half = near.shape[0]
    count, _, blk = pad.shape
    for r in range(count - 1):
        pad[r, :half] = near[:, r * blk : (r + 1) * blk]
        pad[r, half:] = far[:, r * blk : (r + 1) * blk]
    pad[count - 1] = jnp.zeros(pad.shape[1:], pad.dtype)


def layer_kernel(
    live_ref, block_ref, slot_ref, total_ref, x_near, x_far, dy_near, dy_far, wg_hbm, wu_hbm, wd_hbm,
    hidden_ref, d_ref, xpad_ref, dypad_ref, keep_ref, send_ref,
    out_acc, grad_acc, pre_acc, tiles_ref, sems,
):
    half = x_near.shape[0]
    blocks, _, capacity, blk, _ = tiles_ref.shape
    for c in range(blocks):
        for k, source in enumerate((wg_hbm, wu_hbm, wd_hbm)):
            pltpu.make_async_copy(source.at[c], tiles_ref.at[c, k], sems.at[c]).start()
    row_blocks(xpad_ref, x_near, x_far)
    row_blocks(dypad_ref, dy_near, dy_far)
    out_acc[...] = jnp.zeros_like(out_acc)
    grad_acc[...] = jnp.zeros_like(grad_acc)
    pre_acc[...] = jnp.zeros_like(pre_acc)

    def item(position):
        c, s = block_ref[position], slot_ref[position]
        rows = [live_ref[c, s + i] for i in range(CHUNK)]
        return c, s, rows, jnp.where(c < blocks, c, 0)

    def arrived(g):
        before = jnp.where(g > 0, block_ref[jnp.maximum(g * STEP - 1, 0)] + 1, 0)
        after = jnp.minimum(block_ref[g * STEP + STEP - 1] + 1, blocks)

        def wait(c, carry):
            pltpu.make_async_copy(tiles_ref.at[c], tiles_ref.at[c], sems.at[c]).wait()
            return carry

        lax.fori_loop(before, after, wait, 0)

    def gate_up_tiles(tiles, s):
        return jnp.concatenate(
            [tiles_ref[tiles, k, pl.ds(s, CHUNK)].reshape(CHUNK * blk, blk) for k in range(2)],
            axis=1,
        )

    def down_tiles(tiles, s):
        return jnp.concatenate([tiles_ref[tiles, 2, s + i] for i in range(CHUNK)], axis=1)

    def inward(position):
        c, s, rows, tiles = item(position)
        xg = jnp.concatenate([xpad_ref[r] for r in rows], axis=1)
        dyg = jnp.concatenate([dypad_ref[r] for r in rows], axis=1)
        pre = jnp.dot(xg, gate_up_tiles(tiles, s), preferred_element_type=jnp.float32)
        d_hidden = lax.dot_general(
            dyg, down_tiles(tiles, s), NT, preferred_element_type=jnp.float32
        )
        pre_acc[c, :, : 2 * blk] += pre
        pre_acc[c, :, 2 * blk :] += d_hidden

    def outward(position):
        c, s, rows, tiles = item(position)
        gate, up, d_hidden = [pre_acc[c, :, i * blk : (i + 1) * blk] for i in range(3)]
        sig = 1.0 / (1.0 + jnp.exp(-gate))
        act = gate * sig
        hidden = (act * up).astype(jnp.bfloat16)
        d_gate = (d_hidden * up * sig * (1.0 + gate * (1.0 - sig))).astype(jnp.bfloat16)
        d = jnp.concatenate([d_gate, (d_hidden * act).astype(jnp.bfloat16)], axis=1)
        hidden_ref[c] = hidden
        d_ref[c] = d
        y = jnp.dot(hidden, down_tiles(tiles, s), preferred_element_type=jnp.float32)
        x_slots = lax.dot_general(
            d, gate_up_tiles(tiles, s), NT, preferred_element_type=jnp.float32
        )
        add_to_rows(out_acc, rows, y, blk)
        add_to_rows(grad_acc, rows, x_slots, blk)

    def step(g, do_inward, do_outward):
        if do_inward:
            arrived(g)
        if do_outward:
            for i in range(STEP):
                outward((g - LAG) * STEP + i)
        if do_inward:
            for i in range(STEP):
                inward(g * STEP + i)

    steps = (total_ref[0] + STEP - 1) // STEP
    lag = jnp.minimum(steps, LAG)

    def loop(first, last, *parts):
        def body(g, carry):
            step(g, *parts)
            return carry

        lax.fori_loop(first, last, body, 0)

    loop(0, lag, True, False)
    loop(LAG, steps, True, True)
    loop(steps - lag + LAG, steps + LAG, False, True)
    for r in range(out_acc.shape[0] - 1):
        columns = slice(r * blk, (r + 1) * blk)
        for i, acc in enumerate((out_acc, grad_acc)):
            keep_ref[i, :, columns] = acc[r, :half]
            send_ref[i, :, columns] = acc[r, half:].astype(send_ref.dtype)


def gate_up_products(pad_ref, d, rows, slots, blk, stages, i):
    for s in slots[::2]:
        xs = jnp.concatenate([pad_ref[r] for r in rows[s : s + 2]], axis=1)
        full = lax.dot_general(xs, d, TN, preferred_element_type=jnp.float32)
        full = full.astype(jnp.bfloat16)
        for k in range(2):
            stages[0][i, s + k] = full[k * blk : (k + 1) * blk, :blk]
            stages[1][i, s + k] = full[k * blk : (k + 1) * blk, blk:]


def down_products(pad_ref, hidden, rows, slots, blk, stages, i):
    for s in slots[::CHUNK]:
        dys = jnp.concatenate([pad_ref[r] for r in rows[s : s + CHUNK]], axis=1)
        full = lax.dot_general(hidden, dys, TN, preferred_element_type=jnp.float32)
        full = full.astype(jnp.bfloat16)
        for k in range(CHUNK):
            stages[0][i, s + k] = full[:, k * blk : (k + 1) * blk]


def grad_kernel(products, first, count, outs, behind, *refs):
    live_ref, pad_ref, factor_ref = refs[:3]
    grad_refs = refs[3 + behind : 3 + behind + outs]
    stages = refs[3 + behind + outs : -1]
    sems = refs[-1]
    capacity, blk = stages[0].shape[1], stages[0].shape[-1]
    cut = capacity // 2 // CHUNK * CHUNK
    parts = (range(cut), range(cut, capacity))

    def copies(i, h):
        part = pl.ds(parts[h].start, len(parts[h]))
        return [
            pltpu.make_async_copy(stage.at[i, part], grad.at[first + i, part], sems.at[k, i, h])
            for k, (stage, grad) in enumerate(zip(stages, grad_refs))
        ]

    group = max(k for k in range(1, 5) if count % k == 0)

    def step(g, carry):
        some = [g * group + k for k in range(group)]
        rows = [[live_ref[first + i, s] for s in range(capacity)] for i in some]
        for i, names in zip(some, rows):
            for h in range(2):
                products(pad_ref, factor_ref[first + i], names, parts[h], blk, stages, i)
                for copy in copies(i, h):
                    copy.start()
        return carry

    lax.fori_loop(0, count // group, step, 0)
    for i in range(count):
        for h in range(2):
            for copy in copies(i, h):
                copy.wait()


def hop_orders(n):
    bits = [1 << i for i in range(n.bit_length() - 2, 0, -1)]
    return bits, bits[:-2] + bits[:-3:-1]


def swap(value, bits, n):
    return lax.ppermute(value, "col", [(j, j ^ bits[j % 2]) for j in range(n)])


def gather_hops(held, value, hops, n):
    send = value[None]
    for i, bits in enumerate(hops):
        if i:
            send = held[: 1 << i]
        held = lax.dynamic_update_slice_in_dim(held, swap(send, bits, n), 1 << i, 0)
    return held


def rows_of(held, swapped):
    pieces, mine, width = held.shape
    if swapped:
        held = held.reshape(2, 2, pieces // 4, mine, width).transpose(1, 0, 2, 3, 4)
    return held.reshape(pieces * mine, width)


def local(n, inputs, cotangent, gate_tiles, up_tiles, down_tiles, kept_rows, kept_count):
    blocks, capacity, blk, _ = gate_tiles.shape
    mine, width = inputs.shape
    tokens = mine * n
    smem = pl.BlockSpec(memory_space=pltpu.SMEM)
    vmem = pl.BlockSpec(memory_space=pltpu.VMEM)
    hbm = pl.BlockSpec(memory_space=pltpu.HBM)
    tile_bytes = blocks * capacity * blk * blk * 2
    tiles_in = [
        pltpu.with_memory_space_constraint(t, pltpu.HBM) for t in (gate_tiles, up_tiles, down_tiles)
    ]

    def cost(products, tiles, part=1.0):
        return pl.CostEstimate(
            flops=int(products * tokens * tile_bytes * part),
            bytes_accessed=int(tiles * tile_bytes * part),
            transcendentals=0,
        )

    listed = pltpu.SMEM((blocks * (capacity // CHUNK) + capacity // CHUNK + STEP,), jnp.int32)
    live, item_block, item_slot, total, x_held, dy_held = pl.pallas_call(
        functools.partial(seed_kernel, width // blk),
        in_specs=[smem, smem, vmem, vmem],
        out_specs=[smem] * 4 + [vmem] * 2,
        out_shape=[
            pltpu.SMEM((blocks + 1, capacity), jnp.int32),
            listed,
            listed,
            pltpu.SMEM((1,), jnp.int32),
        ]
        + [pltpu.VMEM((n // 2, mine, width), inputs.dtype)] * 2,
        name="seed",
    )(kept_rows, kept_count, inputs, cotangent)
    cores = (1, 1)
    first, second = hop_orders(n)
    x_hops, dy_hops = list(zip(first, second)), list(zip(second, first))
    x_held = gather_hops(x_held, inputs, x_hops, n)
    dy_held = gather_hops(dy_held, cotangent, dy_hops, n)
    x_near, x_far = [rows_of(v, False) for v in (x_held, swap(x_held, cores, n))]
    dy_near, dy_far = [rows_of(v, True) for v in (dy_held, swap(dy_held, cores, n))]

    padded = pltpu.VMEM((width // blk + 1, tokens, blk), jnp.bfloat16)
    acc = pltpu.VMEM((width // blk + 1, tokens, blk), jnp.float32)
    hidden, d, xpad, dypad, keep, send = pl.pallas_call(
        layer_kernel,
        in_specs=[smem] * 4 + [vmem] * 4 + [hbm] * 3,
        out_specs=[vmem] * 6,
        out_shape=[
            pltpu.VMEM((blocks + 1, tokens, blk), jnp.bfloat16),
            pltpu.VMEM((blocks + 1, tokens, 2 * blk), jnp.bfloat16),
            padded,
            padded,
            pltpu.VMEM((2, tokens // 2, width), jnp.float32),
            pltpu.VMEM((2, tokens // 2, width), jnp.bfloat16),
        ],
        scratch_shapes=[acc, acc, pltpu.VMEM((blocks + 1, tokens, 3 * blk), jnp.float32)]
        + [
            pltpu.VMEM((blocks, 3) + gate_tiles.shape[1:], jnp.bfloat16),
            pltpu.SemaphoreType.DMA((blocks,)),
        ],
        compiler_params=pltpu.CompilerParams(vmem_limit_bytes=40 * 1024 * 1024),
        cost_estimate=cost(6, 3),
        name="layer",
    )(live, item_block, item_slot, total, x_near, x_far, dy_near, dy_far, *tiles_in)

    def grads(products, pad, factor, first, count, outs, earlier, after, name):
        behind = len(earlier) + len(after)
        return pl.pallas_call(
            functools.partial(grad_kernel, products, first, count, outs, behind),
            in_specs=[smem, vmem, vmem]
            + [hbm] * len(earlier)
            + [pl.BlockSpec(memory_space=pl.ANY)] * len(after),
            out_specs=[hbm] * outs,
            out_shape=[jax.ShapeDtypeStruct(gate_tiles.shape, jnp.bfloat16)] * outs,
            scratch_shapes=[pltpu.VMEM((count,) + gate_tiles.shape[1:], jnp.bfloat16)] * outs
            + [pltpu.SemaphoreType.DMA((outs, count, 2))],
            input_output_aliases={3 + k: k for k in range(len(earlier))},
            compiler_params=pltpu.CompilerParams(vmem_limit_bytes=24 * 1024 * 1024),
            cost_estimate=cost(outs, outs, count / blocks),
            name=name,
        )(live, pad, factor, *earlier, *after)

    third = -(-blocks // 3)
    cuts = {0: (0, third), 2: (third, 2 * third), 3: (2 * third, blocks)}
    gate_up, down_grad, after = [], None, []
    for i, bits in enumerate([cores] + x_hops[::-1]):
        got = swap(send, bits, n)
        done = []
        if i == 1:
            (down_grad,) = grads(
                down_products, dypad, hidden, 0, blocks, 1, [], after, "down_grad"
            )
            done = [down_grad]
        elif i in cuts:
            first, last = cuts[i]
            gate_up = grads(
                gate_up_products, xpad, d, first, last - first, 2, gate_up, after, "gate_up_grad"
            )
            done = gate_up
        total = keep + got.astype(jnp.float32)
        if i < len(x_hops):
            half = total.shape[1] // 2
            keep, send = total[:, :half], total[:, half:].astype(jnp.bfloat16)
            send, done = lax.optimization_barrier((send, done))
            after = [send]
            if i == 1:
                (down_grad,) = done
            elif i in cuts:
                gate_up = done
    total = total.astype(jnp.bfloat16)
    return total[0], total[1], gate_up[0], gate_up[1], down_grad


def solution(mesh):
    tiles = P("col", None, None, None)
    tokens = P(("groups", "col"), None)
    grads = P(("groups", "col"), None, None, None)
    return jax.shard_map(
        functools.partial(local, mesh.shape["col"]),
        mesh=mesh,
        in_specs=(tokens, tokens, tiles, tiles, tiles, P("col", None), P("col")),
        out_specs=(tokens, tokens, grads, grads, grads),
        check_vma=False,
    )
```

```python
import functools

import jax
import jax.numpy as jnp
from jax import lax
from jax.experimental import pallas as pl
from jax.experimental.pallas import tpu as pltpu
from jax.sharding import PartitionSpec as P

NT = (((1,), (1,)), ((), ()))
TN = (((0,), (0,)), ((), ()))
CHUNK = 4
STEP = 4
LAG = 2


def seed_kernel(dead, rows_ref, count_ref, x_ref, dy_ref, live_ref, block_ref, slot_ref, total_ref, x_held, dy_held):
    x_held[0] = x_ref[...]
    dy_held[0] = dy_ref[...]
    blocks, capacity = rows_ref.shape
    chunks = capacity // CHUNK

    def block(c, position):
        count = count_ref[c]
        for s in range(capacity):
            live_ref[c, s] = jnp.where(s < count, rows_ref[c, s], dead)
        for q in range(chunks):
            block_ref[position + q] = c
            slot_ref[position + q] = q * CHUNK
        return position + jnp.clip((count + CHUNK - 1) // CHUNK, 1, chunks)

    total = lax.fori_loop(0, blocks, block, 0)
    total_ref[0] = total
    for s in range(capacity):
        live_ref[blocks, s] = dead
    for i in range(STEP):
        block_ref[total + i] = blocks
        slot_ref[total + i] = 0


def add_to_rows(acc, rows, parts, blk):
    old = [acc[r] for r in rows]
    for i, r in enumerate(rows):
        acc[r] = old[i] + parts[:, i * blk : (i + 1) * blk]


def row_blocks(pad, near, far):
    half = near.shape[0]
    count, _, blk = pad.shape
    for r in range(count - 1):
        pad[r, :half] = near[:, r * blk : (r + 1) * blk]
        pad[r, half:] = far[:, r * blk : (r + 1) * blk]
    pad[count - 1] = jnp.zeros(pad.shape[1:], pad.dtype)


def layer_kernel(
    live_ref, block_ref, slot_ref, total_ref, x_near, x_far, dy_near, dy_far, wg_hbm, wu_hbm, wd_hbm,
    hidden_ref, d_ref, xpad_ref, dypad_ref, keep_ref, send_ref,
    out_acc, grad_acc, pre_acc, tiles_ref, sems,
):
    half = x_near.shape[0]
    blocks, _, capacity, blk, _ = tiles_ref.shape
    for c in range(blocks):
        for k, source in enumerate((wg_hbm, wu_hbm, wd_hbm)):
            pltpu.make_async_copy(source.at[c], tiles_ref.at[c, k], sems.at[c]).start()
    row_blocks(xpad_ref, x_near, x_far)
    row_blocks(dypad_ref, dy_near, dy_far)
    out_acc[...] = jnp.zeros_like(out_acc)
    grad_acc[...] = jnp.zeros_like(grad_acc)
    pre_acc[...] = jnp.zeros_like(pre_acc)

    def item(position):
        c, s = block_ref[position], slot_ref[position]
        rows = [live_ref[c, s + i] for i in range(CHUNK)]
        return c, s, rows, jnp.where(c < blocks, c, 0)

    def arrived(g):
        before = jnp.where(g > 0, block_ref[jnp.maximum(g * STEP - 1, 0)] + 1, 0)
        after = jnp.minimum(block_ref[g * STEP + STEP - 1] + 1, blocks)

        def wait(c, carry):
            pltpu.make_async_copy(tiles_ref.at[c], tiles_ref.at[c], sems.at[c]).wait()
            return carry

        lax.fori_loop(before, after, wait, 0)

    def gate_up_tiles(tiles, s):
        return jnp.concatenate(
            [tiles_ref[tiles, k, pl.ds(s, CHUNK)].reshape(CHUNK * blk, blk) for k in range(2)],
            axis=1,
        )

    def down_tiles(tiles, s):
        return jnp.concatenate([tiles_ref[tiles, 2, s + i] for i in range(CHUNK)], axis=1)

    def inward(position):
        c, s, rows, tiles = item(position)
        xg = jnp.concatenate([xpad_ref[r] for r in rows], axis=1)
        dyg = jnp.concatenate([dypad_ref[r] for r in rows], axis=1)
        pre = jnp.dot(xg, gate_up_tiles(tiles, s), preferred_element_type=jnp.float32)
        d_hidden = lax.dot_general(
            dyg, down_tiles(tiles, s), NT, preferred_element_type=jnp.float32
        )
        pre_acc[c, :, : 2 * blk] += pre
        pre_acc[c, :, 2 * blk :] += d_hidden

    def outward(position):
        c, s, rows, tiles = item(position)
        gate, up, d_hidden = [pre_acc[c, :, i * blk : (i + 1) * blk] for i in range(3)]
        sig = 1.0 / (1.0 + jnp.exp(-gate))
        act = gate * sig
        hidden = (act * up).astype(jnp.bfloat16)
        d_gate = (d_hidden * up * sig * (1.0 + gate * (1.0 - sig))).astype(jnp.bfloat16)
        d = jnp.concatenate([d_gate, (d_hidden * act).astype(jnp.bfloat16)], axis=1)
        hidden_ref[c] = hidden
        d_ref[c] = d
        y = jnp.dot(hidden, down_tiles(tiles, s), preferred_element_type=jnp.float32)
        turned = jnp.dot(gate_up_tiles(tiles, s), d.T, preferred_element_type=jnp.float32)
        x_slots = turned.T
        add_to_rows(out_acc, rows, y, blk)
        add_to_rows(grad_acc, rows, x_slots, blk)

    def step(g, do_inward, do_outward):
        if do_inward:
            arrived(g)
        if do_outward:
            for i in range(STEP):
                outward((g - LAG) * STEP + i)
        if do_inward:
            for i in range(STEP):
                inward(g * STEP + i)

    steps = (total_ref[0] + STEP - 1) // STEP
    lag = jnp.minimum(steps, LAG)

    def loop(first, last, *parts):
        def body(g, carry):
            step(g, *parts)
            return carry

        lax.fori_loop(first, last, body, 0)

    loop(0, lag, True, False)
    loop(LAG, steps, True, True)
    loop(steps - lag + LAG, steps + LAG, False, True)
    for r in range(out_acc.shape[0] - 1):
        columns = slice(r * blk, (r + 1) * blk)
        for i, acc in enumerate((out_acc, grad_acc)):
            keep_ref[i, :, columns] = acc[r, :half]
            send_ref[i, :, columns] = acc[r, half:].astype(send_ref.dtype)


def gate_up_products(pad_ref, d, rows, slots, blk, stages, i):
    for s in slots[::2]:
        xs = jnp.concatenate([pad_ref[r] for r in rows[s : s + 2]], axis=1)
        full = lax.dot_general(xs, d, TN, preferred_element_type=jnp.float32)
        full = full.astype(jnp.bfloat16)
        for k in range(2):
            stages[0][i, s + k] = full[k * blk : (k + 1) * blk, :blk]
            stages[1][i, s + k] = full[k * blk : (k + 1) * blk, blk:]


def down_products(pad_ref, hidden, rows, slots, blk, stages, i):
    for s in slots[::CHUNK]:
        dys = jnp.concatenate([pad_ref[r] for r in rows[s : s + CHUNK]], axis=1)
        full = lax.dot_general(hidden, dys, TN, preferred_element_type=jnp.float32)
        full = full.astype(jnp.bfloat16)
        for k in range(CHUNK):
            stages[0][i, s + k] = full[:, k * blk : (k + 1) * blk]


def grad_kernel(products, first, count, outs, behind, *refs):
    live_ref, pad_ref, factor_ref = refs[:3]
    grad_refs = refs[3 + behind : 3 + behind + outs]
    stages = refs[3 + behind + outs : -1]
    sems = refs[-1]
    capacity, blk = stages[0].shape[1], stages[0].shape[-1]
    cut = capacity // 2 // CHUNK * CHUNK
    parts = (range(cut), range(cut, capacity))

    def copies(i, h):
        part = pl.ds(parts[h].start, len(parts[h]))
        return [
            pltpu.make_async_copy(stage.at[i, part], grad.at[first + i, part], sems.at[k, i, h])
            for k, (stage, grad) in enumerate(zip(stages, grad_refs))
        ]

    group = max(k for k in range(1, 5) if count % k == 0)

    def step(g, carry):
        some = [g * group + k for k in range(group)]
        rows = [[live_ref[first + i, s] for s in range(capacity)] for i in some]
        for i, names in zip(some, rows):
            for h in range(2):
                products(pad_ref, factor_ref[first + i], names, parts[h], blk, stages, i)
                for copy in copies(i, h):
                    copy.start()
        return carry

    lax.fori_loop(0, count // group, step, 0)
    for i in range(count):
        for h in range(2):
            for copy in copies(i, h):
                copy.wait()


def hop_orders(n):
    bits = [1 << i for i in range(n.bit_length() - 2, 0, -1)]
    return bits, bits[:-2] + bits[:-3:-1]


def swap(value, bits, n):
    return lax.ppermute(value, "col", [(j, j ^ bits[j % 2]) for j in range(n)])


def gather_hops(held, value, hops, n):
    send = value[None]
    for i, bits in enumerate(hops):
        if i:
            send = held[: 1 << i]
        held = lax.dynamic_update_slice_in_dim(held, swap(send, bits, n), 1 << i, 0)
    return held


def rows_of(held, swapped):
    pieces, mine, width = held.shape
    if swapped:
        held = held.reshape(2, 2, pieces // 4, mine, width).transpose(1, 0, 2, 3, 4)
    return held.reshape(pieces * mine, width)


def local(n, inputs, cotangent, gate_tiles, up_tiles, down_tiles, kept_rows, kept_count):
    blocks, capacity, blk, _ = gate_tiles.shape
    mine, width = inputs.shape
    tokens = mine * n
    smem = pl.BlockSpec(memory_space=pltpu.SMEM)
    vmem = pl.BlockSpec(memory_space=pltpu.VMEM)
    hbm = pl.BlockSpec(memory_space=pltpu.HBM)
    tile_bytes = blocks * capacity * blk * blk * 2
    tiles_in = [
        pltpu.with_memory_space_constraint(t, pltpu.HBM) for t in (gate_tiles, up_tiles, down_tiles)
    ]

    def cost(products, tiles, part=1.0):
        return pl.CostEstimate(
            flops=int(products * tokens * tile_bytes * part),
            bytes_accessed=int(tiles * tile_bytes * part),
            transcendentals=0,
        )

    listed = pltpu.SMEM((blocks * (capacity // CHUNK) + capacity // CHUNK + STEP,), jnp.int32)
    live, item_block, item_slot, total, x_held, dy_held = pl.pallas_call(
        functools.partial(seed_kernel, width // blk),
        in_specs=[smem, smem, vmem, vmem],
        out_specs=[smem] * 4 + [vmem] * 2,
        out_shape=[
            pltpu.SMEM((blocks + 1, capacity), jnp.int32),
            listed,
            listed,
            pltpu.SMEM((1,), jnp.int32),
        ]
        + [pltpu.VMEM((n // 2, mine, width), inputs.dtype)] * 2,
        name="seed",
    )(kept_rows, kept_count, inputs, cotangent)
    cores = (1, 1)
    first, second = hop_orders(n)
    x_hops, dy_hops = list(zip(first, second)), list(zip(second, first))
    x_held = gather_hops(x_held, inputs, x_hops, n)
    dy_held = gather_hops(dy_held, cotangent, dy_hops, n)
    x_near, x_far = [rows_of(v, False) for v in (x_held, swap(x_held, cores, n))]
    dy_near, dy_far = [rows_of(v, True) for v in (dy_held, swap(dy_held, cores, n))]

    padded = pltpu.VMEM((width // blk + 1, tokens, blk), jnp.bfloat16)
    acc = pltpu.VMEM((width // blk + 1, tokens, blk), jnp.float32)
    hidden, d, xpad, dypad, keep, send = pl.pallas_call(
        layer_kernel,
        in_specs=[smem] * 4 + [vmem] * 4 + [hbm] * 3,
        out_specs=[vmem] * 6,
        out_shape=[
            pltpu.VMEM((blocks + 1, tokens, blk), jnp.bfloat16),
            pltpu.VMEM((blocks + 1, tokens, 2 * blk), jnp.bfloat16),
            padded,
            padded,
            pltpu.VMEM((2, tokens // 2, width), jnp.float32),
            pltpu.VMEM((2, tokens // 2, width), jnp.bfloat16),
        ],
        scratch_shapes=[acc, acc, pltpu.VMEM((blocks + 1, tokens, 3 * blk), jnp.float32)]
        + [
            pltpu.VMEM((blocks, 3) + gate_tiles.shape[1:], jnp.bfloat16),
            pltpu.SemaphoreType.DMA((blocks,)),
        ],
        compiler_params=pltpu.CompilerParams(vmem_limit_bytes=40 * 1024 * 1024),
        cost_estimate=cost(6, 3),
        name="layer",
    )(live, item_block, item_slot, total, x_near, x_far, dy_near, dy_far, *tiles_in)

    def grads(products, pad, factor, first, count, outs, earlier, after, name):
        behind = len(earlier) + len(after)
        return pl.pallas_call(
            functools.partial(grad_kernel, products, first, count, outs, behind),
            in_specs=[smem, vmem, vmem]
            + [hbm] * len(earlier)
            + [pl.BlockSpec(memory_space=pl.ANY)] * len(after),
            out_specs=[hbm] * outs,
            out_shape=[jax.ShapeDtypeStruct(gate_tiles.shape, jnp.bfloat16)] * outs,
            scratch_shapes=[pltpu.VMEM((count,) + gate_tiles.shape[1:], jnp.bfloat16)] * outs
            + [pltpu.SemaphoreType.DMA((outs, count, 2))],
            input_output_aliases={3 + k: k for k in range(len(earlier))},
            compiler_params=pltpu.CompilerParams(vmem_limit_bytes=24 * 1024 * 1024),
            cost_estimate=cost(outs, outs, count / blocks),
            name=name,
        )(live, pad, factor, *earlier, *after)

    third = -(-blocks // 3)
    cuts = {0: (0, third), 2: (third, 2 * third), 3: (2 * third, blocks)}
    gate_up, down_grad, after = [], None, []
    for i, bits in enumerate([cores] + x_hops[::-1]):
        got = swap(send, bits, n)
        done = []
        if i == 1:
            (down_grad,) = grads(
                down_products, dypad, hidden, 0, blocks, 1, [], after, "down_grad"
            )
            done = [down_grad]
        elif i in cuts:
            first, last = cuts[i]
            gate_up = grads(
                gate_up_products, xpad, d, first, last - first, 2, gate_up, after, "gate_up_grad"
            )
            done = gate_up
        total = keep + got.astype(jnp.float32)
        if i < len(x_hops):
            half = total.shape[1] // 2
            keep, send = total[:, :half], total[:, half:].astype(jnp.bfloat16)
            send, done = lax.optimization_barrier((send, done))
            after = [send]
            if i == 1:
                (down_grad,) = done
            elif i in cuts:
                gate_up = done
    total = total.astype(jnp.bfloat16)
    return total[0], total[1], gate_up[0], gate_up[1], down_grad


def solution(mesh):
    tiles = P("col", None, None, None)
    tokens = P(("groups", "col"), None)
    grads = P(("groups", "col"), None, None, None)
    return jax.shard_map(
        functools.partial(local, mesh.shape["col"]),
        mesh=mesh,
        in_specs=(tokens, tokens, tiles, tiles, tiles, P("col", None), P("col")),
        out_specs=(tokens, tokens, grads, grads, grads),
        check_vma=False,
    )
```

```python
import functools

import jax
import jax.numpy as jnp
from jax import lax
from jax.experimental import pallas as pl
from jax.experimental.pallas import tpu as pltpu
from jax.sharding import PartitionSpec as P

TN = (((0,), (0,)), ((), ()))
CHUNK = 4
STEP = 4
LAG = 2


def seed_kernel(dead, rows_ref, count_ref, x_ref, dy_ref, live_ref, block_ref, slot_ref, total_ref, x_held, dy_held):
    x_held[0] = x_ref[...]
    dy_held[0] = dy_ref[...]
    blocks, capacity = rows_ref.shape
    chunks = capacity // CHUNK

    def block(c, position):
        count = count_ref[c]
        for s in range(capacity):
            live_ref[c, s] = jnp.where(s < count, rows_ref[c, s], dead)
        for q in range(chunks):
            block_ref[position + q] = c
            slot_ref[position + q] = q * CHUNK
        return position + jnp.clip((count + CHUNK - 1) // CHUNK, 1, chunks)

    total = lax.fori_loop(0, blocks, block, 0)
    total_ref[0] = total
    for s in range(capacity):
        live_ref[blocks, s] = dead
    for i in range(STEP):
        block_ref[total + i] = blocks
        slot_ref[total + i] = 0


def add_to_rows(acc, rows, parts, blk):
    old = [acc[r] for r in rows]
    for i, r in enumerate(rows):
        acc[r] = old[i] + parts[:, i * blk : (i + 1) * blk]


def row_blocks(pad, near, far):
    half = near.shape[0]
    count, _, blk = pad.shape
    for r in range(count - 1):
        pad[r, :half] = near[:, r * blk : (r + 1) * blk]
        pad[r, half:] = far[:, r * blk : (r + 1) * blk]
    pad[count - 1] = jnp.zeros(pad.shape[1:], pad.dtype)


def layer_kernel(
    live_ref, block_ref, slot_ref, total_ref, x_near, x_far, dy_near, dy_far, wg_hbm, wu_hbm, wd_hbm,
    hidden_ref, d_ref, xpad_ref, dypad_ref, keep_ref, send_ref,
    out_acc, grad_acc, pre_acc, tiles_ref, sems,
):
    half = x_near.shape[0]
    blocks, _, capacity, blk, _ = tiles_ref.shape
    for c in range(blocks):
        for k, source in enumerate((wg_hbm, wu_hbm, wd_hbm)):
            pltpu.make_async_copy(source.at[c], tiles_ref.at[c, k], sems.at[c]).start()
    row_blocks(xpad_ref, x_near, x_far)
    row_blocks(dypad_ref, dy_near, dy_far)
    out_acc[...] = jnp.zeros_like(out_acc)
    grad_acc[...] = jnp.zeros_like(grad_acc)
    pre_acc[...] = jnp.zeros_like(pre_acc)

    def item(position):
        c, s = block_ref[position], slot_ref[position]
        rows = [live_ref[c, s + i] for i in range(CHUNK)]
        return c, s, rows, jnp.where(c < blocks, c, 0)

    def arrived(g):
        before = jnp.where(g > 0, block_ref[jnp.maximum(g * STEP - 1, 0)] + 1, 0)
        after = jnp.minimum(block_ref[g * STEP + STEP - 1] + 1, blocks)

        def wait(c, carry):
            pltpu.make_async_copy(tiles_ref.at[c], tiles_ref.at[c], sems.at[c]).wait()
            return carry

        lax.fori_loop(before, after, wait, 0)

    def gate_up_tiles(tiles, s):
        return jnp.concatenate(
            [tiles_ref[tiles, k, pl.ds(s, CHUNK)].reshape(CHUNK * blk, blk) for k in range(2)],
            axis=1,
        )

    def down_tiles(tiles, s):
        return jnp.concatenate([tiles_ref[tiles, 2, s + i] for i in range(CHUNK)], axis=1)

    def inward(position):
        c, s, rows, tiles = item(position)
        xg = jnp.concatenate([xpad_ref[r] for r in rows], axis=1)
        dyg = jnp.concatenate([dypad_ref[r] for r in rows], axis=1)
        pre = jnp.dot(xg, gate_up_tiles(tiles, s), preferred_element_type=jnp.float32)
        turned = jnp.dot(down_tiles(tiles, s), dyg.T, preferred_element_type=jnp.float32)
        d_hidden = turned.T
        pre_acc[c, :, : 2 * blk] += pre
        pre_acc[c, :, 2 * blk :] += d_hidden

    def outward(position):
        c, s, rows, tiles = item(position)
        gate, up, d_hidden = [pre_acc[c, :, i * blk : (i + 1) * blk] for i in range(3)]
        sig = 1.0 / (1.0 + jnp.exp(-gate))
        act = gate * sig
        hidden = (act * up).astype(jnp.bfloat16)
        d_gate = (d_hidden * up * sig * (1.0 + gate * (1.0 - sig))).astype(jnp.bfloat16)
        d = jnp.concatenate([d_gate, (d_hidden * act).astype(jnp.bfloat16)], axis=1)
        hidden_ref[c] = hidden
        d_ref[c] = d
        y = jnp.dot(hidden, down_tiles(tiles, s), preferred_element_type=jnp.float32)
        turned = jnp.dot(gate_up_tiles(tiles, s), d.T, preferred_element_type=jnp.float32)
        x_slots = turned.T
        add_to_rows(out_acc, rows, y, blk)
        add_to_rows(grad_acc, rows, x_slots, blk)

    def step(g, do_inward, do_outward):
        if do_inward:
            arrived(g)
        if do_outward:
            for i in range(STEP):
                outward((g - LAG) * STEP + i)
        if do_inward:
            for i in range(STEP):
                inward(g * STEP + i)

    steps = (total_ref[0] + STEP - 1) // STEP
    lag = jnp.minimum(steps, LAG)

    def loop(first, last, *parts):
        def body(g, carry):
            step(g, *parts)
            return carry

        lax.fori_loop(first, last, body, 0)

    loop(0, lag, True, False)
    loop(LAG, steps, True, True)
    loop(steps - lag + LAG, steps + LAG, False, True)
    for r in range(out_acc.shape[0] - 1):
        columns = slice(r * blk, (r + 1) * blk)
        for i, acc in enumerate((out_acc, grad_acc)):
            keep_ref[i, :, columns] = acc[r, :half]
            send_ref[i, :, columns] = acc[r, half:].astype(send_ref.dtype)


def gate_up_products(pad_ref, d, rows, slots, blk, stages, i):
    for s in slots[::2]:
        xs = jnp.concatenate([pad_ref[r] for r in rows[s : s + 2]], axis=1)
        full = lax.dot_general(xs, d, TN, preferred_element_type=jnp.float32)
        full = full.astype(jnp.bfloat16)
        for k in range(2):
            stages[0][i, s + k] = full[k * blk : (k + 1) * blk, :blk]
            stages[1][i, s + k] = full[k * blk : (k + 1) * blk, blk:]


def down_products(pad_ref, hidden, rows, slots, blk, stages, i):
    for s in slots[::CHUNK]:
        dys = jnp.concatenate([pad_ref[r] for r in rows[s : s + CHUNK]], axis=1)
        full = lax.dot_general(hidden, dys, TN, preferred_element_type=jnp.float32)
        full = full.astype(jnp.bfloat16)
        for k in range(CHUNK):
            stages[0][i, s + k] = full[:, k * blk : (k + 1) * blk]


def grad_kernel(products, first, count, outs, behind, *refs):
    live_ref, pad_ref, factor_ref = refs[:3]
    grad_refs = refs[3 + behind : 3 + behind + outs]
    stages = refs[3 + behind + outs : -1]
    sems = refs[-1]
    capacity, blk = stages[0].shape[1], stages[0].shape[-1]
    cut = capacity // 2 // CHUNK * CHUNK
    parts = (range(cut), range(cut, capacity))

    def copies(i, h):
        part = pl.ds(parts[h].start, len(parts[h]))
        return [
            pltpu.make_async_copy(stage.at[i, part], grad.at[first + i, part], sems.at[k, i, h])
            for k, (stage, grad) in enumerate(zip(stages, grad_refs))
        ]

    group = max(k for k in range(1, 6) if count % k == 0)

    def step(g, carry):
        some = [g * group + k for k in range(group)]
        rows = [[live_ref[first + i, s] for s in range(capacity)] for i in some]
        for i, names in zip(some, rows):
            for h in range(2):
                products(pad_ref, factor_ref[first + i], names, parts[h], blk, stages, i)
                for copy in copies(i, h):
                    copy.start()
        return carry

    lax.fori_loop(0, count // group, step, 0)
    for i in range(count):
        for h in range(2):
            for copy in copies(i, h):
                copy.wait()


def hop_orders(n):
    bits = [1 << i for i in range(n.bit_length() - 2, 0, -1)]
    return bits, bits[:-2] + bits[:-3:-1]


def swap(value, bits, n):
    return lax.ppermute(value, "col", [(j, j ^ bits[j % 2]) for j in range(n)])


def gather_hops(held, value, hops, n):
    send = value[None]
    for i, bits in enumerate(hops):
        if i:
            send = held[: 1 << i]
        held = lax.dynamic_update_slice_in_dim(held, swap(send, bits, n), 1 << i, 0)
    return held


def rows_of(held, swapped):
    pieces, mine, width = held.shape
    if swapped:
        held = held.reshape(2, 2, pieces // 4, mine, width).transpose(1, 0, 2, 3, 4)
    return held.reshape(pieces * mine, width)


def local(n, inputs, cotangent, gate_tiles, up_tiles, down_tiles, kept_rows, kept_count):
    blocks, capacity, blk, _ = gate_tiles.shape
    mine, width = inputs.shape
    tokens = mine * n
    smem = pl.BlockSpec(memory_space=pltpu.SMEM)
    vmem = pl.BlockSpec(memory_space=pltpu.VMEM)
    hbm = pl.BlockSpec(memory_space=pltpu.HBM)
    tile_bytes = blocks * capacity * blk * blk * 2
    tiles_in = [
        pltpu.with_memory_space_constraint(t, pltpu.HBM) for t in (gate_tiles, up_tiles, down_tiles)
    ]

    def cost(products, tiles, part=1.0):
        return pl.CostEstimate(
            flops=int(products * tokens * tile_bytes * part),
            bytes_accessed=int(tiles * tile_bytes * part),
            transcendentals=0,
        )

    listed = pltpu.SMEM((blocks * (capacity // CHUNK) + capacity // CHUNK + STEP,), jnp.int32)
    live, item_block, item_slot, total, x_held, dy_held = pl.pallas_call(
        functools.partial(seed_kernel, width // blk),
        in_specs=[smem, smem, vmem, vmem],
        out_specs=[smem] * 4 + [vmem] * 2,
        out_shape=[
            pltpu.SMEM((blocks + 1, capacity), jnp.int32),
            listed,
            listed,
            pltpu.SMEM((1,), jnp.int32),
        ]
        + [pltpu.VMEM((n // 2, mine, width), inputs.dtype)] * 2,
        name="seed",
    )(kept_rows, kept_count, inputs, cotangent)
    cores = (1, 1)
    first, second = hop_orders(n)
    x_hops, dy_hops = list(zip(first, second)), list(zip(second, first))
    x_held = gather_hops(x_held, inputs, x_hops, n)
    dy_held = gather_hops(dy_held, cotangent, dy_hops, n)
    x_near, x_far = [rows_of(v, False) for v in (x_held, swap(x_held, cores, n))]
    dy_near, dy_far = [rows_of(v, True) for v in (dy_held, swap(dy_held, cores, n))]

    padded = pltpu.VMEM((width // blk + 1, tokens, blk), jnp.bfloat16)
    acc = pltpu.VMEM((width // blk + 1, tokens, blk), jnp.float32)
    hidden, d, xpad, dypad, keep, send = pl.pallas_call(
        layer_kernel,
        in_specs=[smem] * 4 + [vmem] * 4 + [hbm] * 3,
        out_specs=[vmem] * 6,
        out_shape=[
            pltpu.VMEM((blocks + 1, tokens, blk), jnp.bfloat16),
            pltpu.VMEM((blocks + 1, tokens, 2 * blk), jnp.bfloat16),
            padded,
            padded,
            pltpu.VMEM((2, tokens // 2, width), jnp.float32),
            pltpu.VMEM((2, tokens // 2, width), jnp.bfloat16),
        ],
        scratch_shapes=[acc, acc, pltpu.VMEM((blocks + 1, tokens, 3 * blk), jnp.float32)]
        + [
            pltpu.VMEM((blocks, 3) + gate_tiles.shape[1:], jnp.bfloat16),
            pltpu.SemaphoreType.DMA((blocks,)),
        ],
        compiler_params=pltpu.CompilerParams(vmem_limit_bytes=40 * 1024 * 1024),
        cost_estimate=cost(6, 3),
        name="layer",
    )(live, item_block, item_slot, total, x_near, x_far, dy_near, dy_far, *tiles_in)

    def grads(products, pad, factor, first, count, outs, earlier, after, name):
        behind = len(earlier) + len(after)
        return pl.pallas_call(
            functools.partial(grad_kernel, products, first, count, outs, behind),
            in_specs=[smem, vmem, vmem]
            + [hbm] * len(earlier)
            + [pl.BlockSpec(memory_space=pl.ANY)] * len(after),
            out_specs=[hbm] * outs,
            out_shape=[jax.ShapeDtypeStruct(gate_tiles.shape, jnp.bfloat16)] * outs,
            scratch_shapes=[pltpu.VMEM((count,) + gate_tiles.shape[1:], jnp.bfloat16)] * outs
            + [pltpu.SemaphoreType.DMA((outs, count, 2))],
            input_output_aliases={3 + k: k for k in range(len(earlier))},
            compiler_params=pltpu.CompilerParams(vmem_limit_bytes=24 * 1024 * 1024),
            cost_estimate=cost(outs, outs, count / blocks),
            name=name,
        )(live, pad, factor, *earlier, *after)

    near = max(1, blocks // 6)
    middle = near + (blocks - near + 1) // 2
    cuts = {0: (0, near), 2: (near, middle), 3: (middle, blocks)}
    gate_up, down_grad, after = [], None, []
    for i, bits in enumerate([cores] + x_hops[::-1]):
        got = swap(send, bits, n)
        done = []
        if i == 1:
            (down_grad,) = grads(
                down_products, dypad, hidden, 0, blocks, 1, [], after, "down_grad"
            )
            done = [down_grad]
        elif i in cuts:
            first, last = cuts[i]
            gate_up = grads(
                gate_up_products, xpad, d, first, last - first, 2, gate_up, after, "gate_up_grad"
            )
            done = gate_up
        total = keep + got.astype(jnp.float32)
        if i < len(x_hops):
            half = total.shape[1] // 2
            keep, send = total[:, :half], total[:, half:].astype(jnp.bfloat16)
            send, done = lax.optimization_barrier((send, done))
            after = [send]
            if i == 1:
                (down_grad,) = done
            elif i in cuts:
                gate_up = done
    total = total.astype(jnp.bfloat16)
    return total[0], total[1], gate_up[0], gate_up[1], down_grad


def solution(mesh):
    tiles = P("col", None, None, None)
    tokens = P(("groups", "col"), None)
    grads = P(("groups", "col"), None, None, None)
    return jax.shard_map(
        functools.partial(local, mesh.shape["col"]),
        mesh=mesh,
        in_specs=(tokens, tokens, tiles, tiles, tiles, P("col", None), P("col")),
        out_specs=(tokens, tokens, grads, grads, grads),
        check_vma=False,
    )
```

```python
import functools

import jax
import jax.numpy as jnp
from jax import lax
from jax.experimental import pallas as pl
from jax.experimental.pallas import tpu as pltpu
from jax.sharding import PartitionSpec as P

TN = (((0,), (0,)), ((), ()))
CHUNK = 4
STEP = 4
LAG = 2


def seed_kernel(dead, rows_ref, count_ref, x_ref, dy_ref, live_ref, block_ref, slot_ref, total_ref, x_held, dy_held):
    x_held[0] = x_ref[...]
    dy_held[0] = dy_ref[...]
    blocks, capacity = rows_ref.shape
    chunks = capacity // CHUNK

    def block(c, position):
        count = count_ref[c]
        for s in range(capacity):
            live_ref[c, s] = jnp.where(s < count, rows_ref[c, s], dead)
        for q in range(chunks):
            block_ref[position + q] = c
            slot_ref[position + q] = q * CHUNK
        return position + jnp.clip((count + CHUNK - 1) // CHUNK, 1, chunks)

    total = lax.fori_loop(0, blocks, block, 0)
    total_ref[0] = total
    for s in range(capacity):
        live_ref[blocks, s] = dead
    for i in range(STEP):
        block_ref[total + i] = blocks
        slot_ref[total + i] = 0


def add_to_rows(acc, rows, parts, blk):
    old = [acc[r] for r in rows]
    for i, r in enumerate(rows):
        acc[r] = old[i] + parts[:, i * blk : (i + 1) * blk]


def row_blocks(pad, near, far):
    half = near.shape[0]
    count, _, blk = pad.shape
    for r in range(count - 1):
        pad[r, :half] = near[:, r * blk : (r + 1) * blk]
        pad[r, half:] = far[:, r * blk : (r + 1) * blk]
    pad[count - 1] = jnp.zeros(pad.shape[1:], pad.dtype)


def layer_kernel(
    live_ref, block_ref, slot_ref, total_ref, x_near, x_far, dy_near, dy_far, wg_hbm, wu_hbm, wd_hbm,
    hidden_ref, d_ref, xpad_ref, dypad_ref, keep_ref, send_ref,
    out_acc, grad_acc, pre_acc, tiles_ref, sems,
):
    half = x_near.shape[0]
    blocks, _, capacity, blk, _ = tiles_ref.shape
    for c in range(blocks):
        for k, source in enumerate((wg_hbm, wu_hbm, wd_hbm)):
            pltpu.make_async_copy(source.at[c], tiles_ref.at[c, k], sems.at[c]).start()
    row_blocks(xpad_ref, x_near, x_far)
    row_blocks(dypad_ref, dy_near, dy_far)
    out_acc[...] = jnp.zeros_like(out_acc)
    grad_acc[...] = jnp.zeros_like(grad_acc)
    pre_acc[...] = jnp.zeros_like(pre_acc)

    def item(position):
        c, s = block_ref[position], slot_ref[position]
        rows = [live_ref[c, s + i] for i in range(CHUNK)]
        return c, s, rows, jnp.where(c < blocks, c, 0)

    def arrived(g):
        before = jnp.where(g > 0, block_ref[jnp.maximum(g * STEP - 1, 0)] + 1, 0)
        after = jnp.minimum(block_ref[g * STEP + STEP - 1] + 1, blocks)

        def wait(c, carry):
            pltpu.make_async_copy(tiles_ref.at[c], tiles_ref.at[c], sems.at[c]).wait()
            return carry

        lax.fori_loop(before, after, wait, 0)

    def gate_up_tiles(tiles, s):
        return jnp.concatenate(
            [tiles_ref[tiles, k, pl.ds(s, CHUNK)].reshape(CHUNK * blk, blk) for k in range(2)],
            axis=1,
        )

    def down_tiles(tiles, s):
        return jnp.concatenate([tiles_ref[tiles, 2, s + i] for i in range(CHUNK)], axis=1)

    def inward(position):
        c, s, rows, tiles = item(position)
        xg = jnp.concatenate([xpad_ref[r] for r in rows], axis=1)
        dyg = jnp.concatenate([dypad_ref[r] for r in rows], axis=1)
        pre = jnp.dot(xg, gate_up_tiles(tiles, s), preferred_element_type=jnp.float32)
        turned = jnp.dot(down_tiles(tiles, s), dyg.T, preferred_element_type=jnp.float32)
        d_hidden = turned.T
        pre_acc[c, :, : 2 * blk] += pre
        pre_acc[c, :, 2 * blk :] += d_hidden

    def outward(position):
        c, s, rows, tiles = item(position)
        gate, up, d_hidden = [pre_acc[c, :, i * blk : (i + 1) * blk] for i in range(3)]
        sig = 1.0 / (1.0 + jnp.exp(-gate))
        act = gate * sig
        hidden = (act * up).astype(jnp.bfloat16)
        d_gate = (d_hidden * up * sig * (1.0 + gate * (1.0 - sig))).astype(jnp.bfloat16)
        d = jnp.concatenate([d_gate, (d_hidden * act).astype(jnp.bfloat16)], axis=1)
        hidden_ref[c] = hidden
        d_ref[c] = d
        y = jnp.dot(hidden, down_tiles(tiles, s), preferred_element_type=jnp.float32)
        turned = jnp.dot(gate_up_tiles(tiles, s), d.T, preferred_element_type=jnp.float32)
        x_slots = turned.T
        add_to_rows(out_acc, rows, y, blk)
        add_to_rows(grad_acc, rows, x_slots, blk)

    def step(g, do_inward, do_outward):
        if do_inward:
            arrived(g)
        if do_outward:
            for i in range(STEP):
                outward((g - LAG) * STEP + i)
        if do_inward:
            for i in range(STEP):
                inward(g * STEP + i)

    steps = (total_ref[0] + STEP - 1) // STEP
    lag = jnp.minimum(steps, LAG)

    def loop(first, last, *parts):
        def body(g, carry):
            step(g, *parts)
            return carry

        lax.fori_loop(first, last, body, 0)

    loop(0, lag, True, False)
    loop(LAG, steps, True, True)
    loop(steps - lag + LAG, steps + LAG, False, True)
    for r in range(out_acc.shape[0] - 1):
        columns = slice(r * blk, (r + 1) * blk)
        for i, acc in enumerate((out_acc, grad_acc)):
            keep_ref[i, :, columns] = acc[r, :half]
            send_ref[i, :, columns] = acc[r, half:].astype(send_ref.dtype)


def gate_up_products(pad_ref, d, rows, slots, blk, stages, i):
    for s in slots[::2]:
        xs = jnp.concatenate([pad_ref[r] for r in rows[s : s + 2]], axis=1)
        full = lax.dot_general(xs, d, TN, preferred_element_type=jnp.float32)
        full = full.astype(jnp.bfloat16)
        for k in range(2):
            stages[0][i, s + k] = full[k * blk : (k + 1) * blk, :blk]
            stages[1][i, s + k] = full[k * blk : (k + 1) * blk, blk:]


def down_products(pad_ref, hidden, rows, slots, blk, stages, i):
    for s in slots[::CHUNK]:
        dys = jnp.concatenate([pad_ref[r] for r in rows[s : s + CHUNK]], axis=1)
        full = lax.dot_general(hidden, dys, TN, preferred_element_type=jnp.float32)
        full = full.astype(jnp.bfloat16)
        for k in range(CHUNK):
            stages[0][i, s + k] = full[:, k * blk : (k + 1) * blk]


def grad_kernel(products, first, count, outs, behind, *refs):
    live_ref, pad_ref, factor_ref = refs[:3]
    grad_refs = refs[3 + behind : 3 + behind + outs]
    stages = refs[3 + behind + outs : -1]
    sems = refs[-1]
    capacity, blk = stages[0].shape[1], stages[0].shape[-1]
    cut = capacity // 2 // CHUNK * CHUNK
    parts = (range(cut), range(cut, capacity))

    def copies(i, h):
        part = pl.ds(parts[h].start, len(parts[h]))
        return [
            pltpu.make_async_copy(stage.at[i, part], grad.at[first + i, part], sems.at[k, i, h])
            for k, (stage, grad) in enumerate(zip(stages, grad_refs))
        ]

    group = max(k for k in range(1, 5) if count % k == 0)

    def step(g, carry):
        some = [g * group + k for k in range(group)]
        rows = [[live_ref[first + i, s] for s in range(capacity)] for i in some]
        for i, names in zip(some, rows):
            for h in range(2):
                products(pad_ref, factor_ref[first + i], names, parts[h], blk, stages, i)
                for copy in copies(i, h):
                    copy.start()
        return carry

    lax.fori_loop(0, count // group, step, 0)
    for i in range(count):
        for h in range(2):
            for copy in copies(i, h):
                copy.wait()


def hop_orders(n):
    bits = [1 << i for i in range(n.bit_length() - 2, 0, -1)]
    return bits, bits[:-2] + bits[:-3:-1]


def swap(value, bits, n):
    return lax.ppermute(value, "col", [(j, j ^ bits[j % 2]) for j in range(n)])


def gather_hops(held, value, hops, n):
    send = value[None]
    for i, bits in enumerate(hops):
        if i:
            send = held[: 1 << i]
        held = lax.dynamic_update_slice_in_dim(held, swap(send, bits, n), 1 << i, 0)
    return held


def rows_of(held, swapped):
    pieces, mine, width = held.shape
    if swapped:
        held = held.reshape(2, 2, pieces // 4, mine, width).transpose(1, 0, 2, 3, 4)
    return held.reshape(pieces * mine, width)


def local(n, inputs, cotangent, gate_tiles, up_tiles, down_tiles, kept_rows, kept_count):
    blocks, capacity, blk, _ = gate_tiles.shape
    mine, width = inputs.shape
    tokens = mine * n
    smem = pl.BlockSpec(memory_space=pltpu.SMEM)
    vmem = pl.BlockSpec(memory_space=pltpu.VMEM)
    hbm = pl.BlockSpec(memory_space=pltpu.HBM)
    tile_bytes = blocks * capacity * blk * blk * 2
    tiles_in = [
        pltpu.with_memory_space_constraint(t, pltpu.HBM) for t in (gate_tiles, up_tiles, down_tiles)
    ]

    def cost(products, tiles, part=1.0):
        return pl.CostEstimate(
            flops=int(products * tokens * tile_bytes * part),
            bytes_accessed=int(tiles * tile_bytes * part),
            transcendentals=0,
        )

    listed = pltpu.SMEM((blocks * (capacity // CHUNK) + capacity // CHUNK + STEP,), jnp.int32)
    live, item_block, item_slot, total, x_held, dy_held = pl.pallas_call(
        functools.partial(seed_kernel, width // blk),
        in_specs=[smem, smem, vmem, vmem],
        out_specs=[smem] * 4 + [vmem] * 2,
        out_shape=[
            pltpu.SMEM((blocks + 1, capacity), jnp.int32),
            listed,
            listed,
            pltpu.SMEM((1,), jnp.int32),
        ]
        + [pltpu.VMEM((n // 2, mine, width), inputs.dtype)] * 2,
        name="seed",
    )(kept_rows, kept_count, inputs, cotangent)
    cores = (1, 1)
    first, second = hop_orders(n)
    x_hops, dy_hops = list(zip(first, second)), list(zip(second, first))
    x_held = gather_hops(x_held, inputs, x_hops, n)
    dy_held = gather_hops(dy_held, cotangent, dy_hops, n)
    x_near, x_far = [rows_of(v, False) for v in (x_held, swap(x_held, cores, n))]
    dy_near, dy_far = [rows_of(v, True) for v in (dy_held, swap(dy_held, cores, n))]

    padded = pltpu.VMEM((width // blk + 1, tokens, blk), jnp.bfloat16)
    acc = pltpu.VMEM((width // blk + 1, tokens, blk), jnp.float32)
    hidden, d, xpad, dypad, keep, send = pl.pallas_call(
        layer_kernel,
        in_specs=[smem] * 4 + [vmem] * 4 + [hbm] * 3,
        out_specs=[vmem] * 6,
        out_shape=[
            pltpu.VMEM((blocks + 1, tokens, blk), jnp.bfloat16),
            pltpu.VMEM((blocks + 1, tokens, 2 * blk), jnp.bfloat16),
            padded,
            padded,
            pltpu.VMEM((2, tokens // 2, width), jnp.float32),
            pltpu.VMEM((2, tokens // 2, width), jnp.bfloat16),
        ],
        scratch_shapes=[acc, acc, pltpu.VMEM((blocks + 1, tokens, 3 * blk), jnp.float32)]
        + [
            pltpu.VMEM((blocks, 3) + gate_tiles.shape[1:], jnp.bfloat16),
            pltpu.SemaphoreType.DMA((blocks,)),
        ],
        compiler_params=pltpu.CompilerParams(vmem_limit_bytes=40 * 1024 * 1024),
        cost_estimate=cost(6, 3),
        name="layer",
    )(live, item_block, item_slot, total, x_near, x_far, dy_near, dy_far, *tiles_in)

    def grads(products, pad, factor, first, count, outs, earlier, after, name):
        behind = len(earlier) + len(after)
        return pl.pallas_call(
            functools.partial(grad_kernel, products, first, count, outs, behind),
            in_specs=[smem, vmem, vmem]
            + [hbm] * len(earlier)
            + [pl.BlockSpec(memory_space=pl.ANY)] * len(after),
            out_specs=[hbm] * outs,
            out_shape=[jax.ShapeDtypeStruct(gate_tiles.shape, jnp.bfloat16)] * outs,
            scratch_shapes=[pltpu.VMEM((count,) + gate_tiles.shape[1:], jnp.bfloat16)] * outs
            + [pltpu.SemaphoreType.DMA((outs, count, 2))],
            input_output_aliases={3 + k: k for k in range(len(earlier))},
            compiler_params=pltpu.CompilerParams(vmem_limit_bytes=24 * 1024 * 1024),
            cost_estimate=cost(outs, outs, count / blocks),
            name=name,
        )(live, pad, factor, *earlier, *after)

    near = max(1, blocks // 6)
    middle = min(blocks - 1, near + (3 * (blocks - near) + 4) // 5)
    cuts = {0: (0, near), 2: (near, middle), 3: (middle, blocks)}
    gate_up, down_grad, after = [], None, []
    for i, bits in enumerate([cores] + x_hops[::-1]):
        got = swap(send, bits, n)
        done = []
        if i == 1:
            (down_grad,) = grads(
                down_products, dypad, hidden, 0, blocks, 1, [], after, "down_grad"
            )
            done = [down_grad]
        elif i in cuts:
            first, last = cuts[i]
            gate_up = grads(
                gate_up_products, xpad, d, first, last - first, 2, gate_up, after, "gate_up_grad"
            )
            done = gate_up
        total = keep + got.astype(jnp.float32)
        if i < len(x_hops):
            half = total.shape[1] // 2
            keep, send = total[:, :half], total[:, half:].astype(jnp.bfloat16)
            send, done = lax.optimization_barrier((send, done))
            after = [send]
            if i == 1:
                (down_grad,) = done
            elif i in cuts:
                gate_up = done
    total = total.astype(jnp.bfloat16)
    return total[0], total[1], gate_up[0], gate_up[1], down_grad


def solution(mesh):
    tiles = P("col", None, None, None)
    tokens = P(("groups", "col"), None)
    grads = P(("groups", "col"), None, None, None)
    return jax.shard_map(
        functools.partial(local, mesh.shape["col"]),
        mesh=mesh,
        in_specs=(tokens, tokens, tiles, tiles, tiles, P("col", None), P("col")),
        out_specs=(tokens, tokens, grads, grads, grads),
        check_vma=False,
    )
```

```python
import functools

import jax
import jax.numpy as jnp
from jax import lax
from jax.experimental import pallas as pl
from jax.experimental.pallas import tpu as pltpu
from jax.sharding import PartitionSpec as P

TN = (((0,), (0,)), ((), ()))
CHUNK = 4
STEP = 4
LAG = 2


def seed_kernel(dead, rows_ref, count_ref, x_ref, dy_ref, live_ref, block_ref, slot_ref, total_ref, x_held, dy_held):
    x_held[0] = x_ref[...]
    dy_held[0] = dy_ref[...]
    blocks, capacity = rows_ref.shape
    chunks = capacity // CHUNK

    def block(c, position):
        count = count_ref[c]
        for s in range(capacity):
            live_ref[c, s] = jnp.where(s < count, rows_ref[c, s], dead)
        for q in range(chunks):
            block_ref[position + q] = c
            slot_ref[position + q] = q * CHUNK
        return position + jnp.clip((count + CHUNK - 1) // CHUNK, 1, chunks)

    total = lax.fori_loop(0, blocks, block, 0)
    total_ref[0] = total
    for s in range(capacity):
        live_ref[blocks, s] = dead
    for i in range(STEP):
        block_ref[total + i] = blocks
        slot_ref[total + i] = 0


def add_to_rows(acc, rows, parts, blk):
    old = [acc[r] for r in rows]
    for i, r in enumerate(rows):
        acc[r] = old[i] + parts[:, i * blk : (i + 1) * blk]


def row_blocks(pad, near, far):
    half = near.shape[0]
    count, _, blk = pad.shape
    for r in range(count - 1):
        pad[r, :half] = near[:, r * blk : (r + 1) * blk]
        pad[r, half:] = far[:, r * blk : (r + 1) * blk]
    pad[count - 1] = jnp.zeros(pad.shape[1:], pad.dtype)


def layer_kernel(
    live_ref, block_ref, slot_ref, total_ref, x_near, x_far, dy_near, dy_far, wg_hbm, wu_hbm, wd_hbm,
    hidden_ref, d_ref, xpad_ref, dypad_ref, keep_ref, send_ref,
    out_acc, grad_acc, pre_acc, tiles_ref, sems,
):
    half = x_near.shape[0]
    blocks, _, capacity, blk, _ = tiles_ref.shape
    for c in range(blocks):
        for k, source in enumerate((wg_hbm, wu_hbm, wd_hbm)):
            pltpu.make_async_copy(source.at[c], tiles_ref.at[c, k], sems.at[c]).start()
    row_blocks(xpad_ref, x_near, x_far)
    row_blocks(dypad_ref, dy_near, dy_far)
    out_acc[...] = jnp.zeros_like(out_acc)
    grad_acc[...] = jnp.zeros_like(grad_acc)
    pre_acc[...] = jnp.zeros_like(pre_acc)

    def item(position):
        c, s = block_ref[position], slot_ref[position]
        rows = [live_ref[c, s + i] for i in range(CHUNK)]
        return c, s, rows, jnp.where(c < blocks, c, 0)

    def arrived(g):
        before = jnp.where(g > 0, block_ref[jnp.maximum(g * STEP - 1, 0)] + 1, 0)
        after = jnp.minimum(block_ref[g * STEP + STEP - 1] + 1, blocks)

        def wait(c, carry):
            pltpu.make_async_copy(tiles_ref.at[c], tiles_ref.at[c], sems.at[c]).wait()
            return carry

        lax.fori_loop(before, after, wait, 0)

    def gate_up_tiles(tiles, s):
        return jnp.concatenate(
            [tiles_ref[tiles, k, pl.ds(s, CHUNK)].reshape(CHUNK * blk, blk) for k in range(2)],
            axis=1,
        )

    def down_tiles(tiles, s):
        return jnp.concatenate([tiles_ref[tiles, 2, s + i] for i in range(CHUNK)], axis=1)

    def inward(position):
        c, s, rows, tiles = item(position)
        xg = jnp.concatenate([xpad_ref[r] for r in rows], axis=1)
        dyg = jnp.concatenate([dypad_ref[r] for r in rows], axis=1)
        pre = jnp.dot(xg, gate_up_tiles(tiles, s), preferred_element_type=jnp.float32)
        turned = jnp.dot(down_tiles(tiles, s), dyg.T, preferred_element_type=jnp.float32)
        d_hidden = turned.T
        pre_acc[c, :, : 2 * blk] += pre
        pre_acc[c, :, 2 * blk :] += d_hidden

    def outward(position):
        c, s, rows, tiles = item(position)
        gate, up, d_hidden = [pre_acc[c, :, i * blk : (i + 1) * blk] for i in range(3)]
        sig = 1.0 / (1.0 + jnp.exp(-gate))
        act = gate * sig
        hidden = (act * up).astype(jnp.bfloat16)
        d_gate = (d_hidden * up * sig * (1.0 + gate * (1.0 - sig))).astype(jnp.bfloat16)
        d = jnp.concatenate([d_gate, (d_hidden * act).astype(jnp.bfloat16)], axis=1)
        hidden_ref[c] = hidden
        d_ref[c] = d
        y = jnp.dot(hidden, down_tiles(tiles, s), preferred_element_type=jnp.float32)
        turned = jnp.dot(gate_up_tiles(tiles, s), d.T, preferred_element_type=jnp.float32)
        x_slots = turned.T
        add_to_rows(out_acc, rows, y, blk)
        add_to_rows(grad_acc, rows, x_slots, blk)

    def step(g, do_inward, do_outward):
        if do_inward:
            arrived(g)
        if do_outward:
            for i in range(STEP):
                outward((g - LAG) * STEP + i)
        if do_inward:
            for i in range(STEP):
                inward(g * STEP + i)

    steps = (total_ref[0] + STEP - 1) // STEP
    lag = jnp.minimum(steps, LAG)

    def loop(first, last, *parts):
        def body(g, carry):
            step(g, *parts)
            return carry

        lax.fori_loop(first, last, body, 0)

    loop(0, lag, True, False)
    loop(LAG, steps, True, True)
    loop(steps - lag + LAG, steps + LAG, False, True)
    for r in range(out_acc.shape[0] - 1):
        columns = slice(r * blk, (r + 1) * blk)
        for i, acc in enumerate((out_acc, grad_acc)):
            keep_ref[i, :, columns] = acc[r, :half]
            send_ref[i, :, columns] = acc[r, half:].astype(send_ref.dtype)


def gate_up_products(pad_ref, d, rows, slots, blk, stages, i):
    for s in slots[::2]:
        xs = jnp.concatenate([pad_ref[r] for r in rows[s : s + 2]], axis=1)
        full = lax.dot_general(xs, d, TN, preferred_element_type=jnp.float32)
        full = full.astype(jnp.bfloat16)
        for k in range(2):
            stages[0][i, s + k] = full[k * blk : (k + 1) * blk, :blk]
            stages[1][i, s + k] = full[k * blk : (k + 1) * blk, blk:]


def down_products(pad_ref, hidden, rows, slots, blk, stages, i):
    for s in slots[::CHUNK]:
        dys = jnp.concatenate([pad_ref[r] for r in rows[s : s + CHUNK]], axis=1)
        full = lax.dot_general(hidden, dys, TN, preferred_element_type=jnp.float32)
        full = full.astype(jnp.bfloat16)
        for k in range(CHUNK):
            stages[0][i, s + k] = full[:, k * blk : (k + 1) * blk]


def grad_kernel(products, first, count, outs, behind, *refs):
    live_ref, pad_ref, factor_ref = refs[:3]
    grad_refs = refs[3 + behind : 3 + behind + outs]
    stages = refs[3 + behind + outs : -1]
    sems = refs[-1]
    capacity, blk = stages[0].shape[1], stages[0].shape[-1]
    cut = capacity // 2 // CHUNK * CHUNK
    parts = (range(cut), range(cut, capacity))

    def copies(i, h):
        part = pl.ds(parts[h].start, len(parts[h]))
        return [
            pltpu.make_async_copy(stage.at[i, part], grad.at[first + i, part], sems.at[k, i, h])
            for k, (stage, grad) in enumerate(zip(stages, grad_refs))
        ]

    group = max(k for k in range(1, 5) if count % k == 0)

    def step(g, carry):
        some = [g * group + k for k in range(group)]
        rows = [[live_ref[first + i, s] for s in range(capacity)] for i in some]
        for i, names in zip(some, rows):
            for h in range(2):
                products(pad_ref, factor_ref[first + i], names, parts[h], blk, stages, i)
                for copy in copies(i, h):
                    copy.start()
        return carry

    lax.fori_loop(0, count // group, step, 0)
    for i in range(count):
        for h in range(2):
            for copy in copies(i, h):
                copy.wait()


def hop_orders(n):
    bits = [1 << i for i in range(n.bit_length() - 2, 0, -1)]
    return bits, bits[:-2] + bits[:-3:-1]


def swap(value, bits, n):
    return lax.ppermute(value, "col", [(j, j ^ bits[j % 2]) for j in range(n)])


def gather_hops(held, value, hops, n):
    send = value[None]
    for i, bits in enumerate(hops):
        if i:
            send = held[: 1 << i]
        held = lax.dynamic_update_slice_in_dim(held, swap(send, bits, n), 1 << i, 0)
    return held


def rows_of(held, swapped):
    pieces, mine, width = held.shape
    if swapped:
        held = held.reshape(2, 2, pieces // 4, mine, width).transpose(1, 0, 2, 3, 4)
    return held.reshape(pieces * mine, width)


def local(n, inputs, cotangent, gate_tiles, up_tiles, down_tiles, kept_rows, kept_count):
    blocks, capacity, blk, _ = gate_tiles.shape
    mine, width = inputs.shape
    tokens = mine * n
    smem = pl.BlockSpec(memory_space=pltpu.SMEM)
    vmem = pl.BlockSpec(memory_space=pltpu.VMEM)
    hbm = pl.BlockSpec(memory_space=pltpu.HBM)
    tile_bytes = blocks * capacity * blk * blk * 2
    tiles_in = [
        pltpu.with_memory_space_constraint(t, pltpu.HBM) for t in (gate_tiles, up_tiles, down_tiles)
    ]

    def cost(products, tiles, part=1.0):
        return pl.CostEstimate(
            flops=int(products * tokens * tile_bytes * part),
            bytes_accessed=int(tiles * tile_bytes * part),
            transcendentals=0,
        )

    listed = pltpu.SMEM((blocks * (capacity // CHUNK) + capacity // CHUNK + STEP,), jnp.int32)
    live, item_block, item_slot, total, x_held, dy_held = pl.pallas_call(
        functools.partial(seed_kernel, width // blk),
        in_specs=[smem, smem, vmem, vmem],
        out_specs=[smem] * 4 + [vmem] * 2,
        out_shape=[
            pltpu.SMEM((blocks + 1, capacity), jnp.int32),
            listed,
            listed,
            pltpu.SMEM((1,), jnp.int32),
        ]
        + [pltpu.VMEM((n // 2, mine, width), inputs.dtype)] * 2,
        name="seed",
    )(kept_rows, kept_count, inputs, cotangent)
    cores = (1, 1)
    first, second = hop_orders(n)
    x_hops, dy_hops = list(zip(first, second)), list(zip(second, first))
    x_held = gather_hops(x_held, inputs, x_hops, n)
    dy_held = gather_hops(dy_held, cotangent, dy_hops, n)
    x_near, x_far = [rows_of(v, False) for v in (x_held, swap(x_held, cores, n))]
    dy_near, dy_far = [rows_of(v, True) for v in (dy_held, swap(dy_held, cores, n))]

    padded = pltpu.VMEM((width // blk + 1, tokens, blk), jnp.bfloat16)
    acc = pltpu.VMEM((width // blk + 1, tokens, blk), jnp.float32)
    hidden, d, xpad, dypad, keep, send = pl.pallas_call(
        layer_kernel,
        in_specs=[smem] * 4 + [vmem] * 4 + [hbm] * 3,
        out_specs=[vmem] * 6,
        out_shape=[
            pltpu.VMEM((blocks + 1, tokens, blk), jnp.bfloat16),
            pltpu.VMEM((blocks + 1, tokens, 2 * blk), jnp.bfloat16),
            padded,
            padded,
            pltpu.VMEM((2, tokens // 2, width), jnp.float32),
            pltpu.VMEM((2, tokens // 2, width), jnp.bfloat16),
        ],
        scratch_shapes=[acc, acc, pltpu.VMEM((blocks + 1, tokens, 3 * blk), jnp.float32)]
        + [
            pltpu.VMEM((blocks, 3) + gate_tiles.shape[1:], jnp.bfloat16),
            pltpu.SemaphoreType.DMA((blocks,)),
        ],
        compiler_params=pltpu.CompilerParams(vmem_limit_bytes=40 * 1024 * 1024),
        cost_estimate=cost(6, 3),
        name="layer",
    )(live, item_block, item_slot, total, x_near, x_far, dy_near, dy_far, *tiles_in)

    def grads(products, pad, factor, first, count, outs, earlier, after, name):
        behind = len(earlier) + len(after)
        return pl.pallas_call(
            functools.partial(grad_kernel, products, first, count, outs, behind),
            in_specs=[smem, vmem, vmem]
            + [hbm] * len(earlier)
            + [pl.BlockSpec(memory_space=pl.ANY)] * len(after),
            out_specs=[hbm] * outs,
            out_shape=[jax.ShapeDtypeStruct(gate_tiles.shape, jnp.bfloat16)] * outs,
            scratch_shapes=[pltpu.VMEM((count,) + gate_tiles.shape[1:], jnp.bfloat16)] * outs
            + [pltpu.SemaphoreType.DMA((outs, count, 2))],
            input_output_aliases={3 + k: k for k in range(len(earlier))},
            compiler_params=pltpu.CompilerParams(vmem_limit_bytes=24 * 1024 * 1024),
            cost_estimate=cost(outs, outs, count / blocks),
            name=name,
        )(live, pad, factor, *earlier, *after)

    near = max(1, blocks // 12)
    beside = near + blocks // 12
    middle = min(blocks - 1, beside + (3 * (blocks - beside) + 4) // 5)
    cuts = {0: (0, near), 1: (near, beside), 2: (beside, middle), 3: (middle, blocks)}
    gate_up, down_grad, after = [], [], []
    for i, bits in enumerate([cores] + x_hops[::-1]):
        got = swap(send, bits, n)
        if i == 1:
            down_grad = grads(
                down_products, dypad, hidden, 0, blocks, 1, [], after, "down_grad"
            )
        first, last = cuts.get(i, (0, 0))
        if first < last:
            gate_up = grads(
                gate_up_products, xpad, d, first, last - first, 2, gate_up, after, "gate_up_grad"
            )
        total = keep + got.astype(jnp.float32)
        if i < len(x_hops):
            half = total.shape[1] // 2
            keep, send = total[:, :half], total[:, half:].astype(jnp.bfloat16)
            send, done = lax.optimization_barrier((send, (gate_up, down_grad)))
            after = [send]
            gate_up, down_grad = done
    total = total.astype(jnp.bfloat16)
    return total[0], total[1], gate_up[0], gate_up[1], down_grad[0]


def solution(mesh):
    tiles = P("col", None, None, None)
    tokens = P(("groups", "col"), None)
    grads = P(("groups", "col"), None, None, None)
    return jax.shard_map(
        functools.partial(local, mesh.shape["col"]),
        mesh=mesh,
        in_specs=(tokens, tokens, tiles, tiles, tiles, P("col", None), P("col")),
        out_specs=(tokens, tokens, grads, grads, grads),
        check_vma=False,
    )
```

```python
import functools

import jax
import jax.numpy as jnp
from jax import lax
from jax.experimental import pallas as pl
from jax.experimental.pallas import tpu as pltpu
from jax.sharding import PartitionSpec as P

TN = (((0,), (0,)), ((), ()))
CHUNK = 4
STEP = 5
LAG = 2


def seed_kernel(dead, rows_ref, count_ref, x_ref, dy_ref, live_ref, block_ref, slot_ref, total_ref, x_held, dy_held):
    x_held[0] = x_ref[...]
    dy_held[0] = dy_ref[...]
    blocks, capacity = rows_ref.shape
    chunks = capacity // CHUNK

    def block(c, position):
        count = count_ref[c]
        for s in range(capacity):
            live_ref[c, s] = jnp.where(s < count, rows_ref[c, s], dead)
        for q in range(chunks):
            block_ref[position + q] = c
            slot_ref[position + q] = q * CHUNK
        return position + jnp.clip((count + CHUNK - 1) // CHUNK, 1, chunks)

    total = lax.fori_loop(0, blocks, block, 0)
    total_ref[0] = total
    for s in range(capacity):
        live_ref[blocks, s] = dead
    for i in range(STEP):
        block_ref[total + i] = blocks
        slot_ref[total + i] = 0


def add_to_rows(acc, rows, parts, blk):
    old = [acc[r] for r in rows]
    for i, r in enumerate(rows):
        acc[r] = old[i] + parts[:, i * blk : (i + 1) * blk]


def row_blocks(pad, near, far):
    half = near.shape[0]
    count, _, blk = pad.shape
    for r in range(count - 1):
        pad[r, :half] = near[:, r * blk : (r + 1) * blk]
        pad[r, half:] = far[:, r * blk : (r + 1) * blk]
    pad[count - 1] = jnp.zeros(pad.shape[1:], pad.dtype)


def layer_kernel(
    live_ref, block_ref, slot_ref, total_ref, x_near, x_far, dy_near, dy_far, wg_hbm, wu_hbm, wd_hbm,
    hidden_ref, d_ref, xpad_ref, dypad_ref, keep_ref, send_ref,
    out_acc, grad_acc, pre_acc, tiles_ref, sems,
):
    half = x_near.shape[0]
    blocks, _, capacity, blk, _ = tiles_ref.shape
    for c in range(blocks):
        for k, source in enumerate((wg_hbm, wu_hbm, wd_hbm)):
            pltpu.make_async_copy(source.at[c], tiles_ref.at[c, k], sems.at[c]).start()
    row_blocks(xpad_ref, x_near, x_far)
    row_blocks(dypad_ref, dy_near, dy_far)
    out_acc[...] = jnp.zeros_like(out_acc)
    grad_acc[...] = jnp.zeros_like(grad_acc)
    pre_acc[...] = jnp.zeros_like(pre_acc)

    def item(position):
        c, s = block_ref[position], slot_ref[position]
        rows = [live_ref[c, s + i] for i in range(CHUNK)]
        return c, s, rows, jnp.where(c < blocks, c, 0)

    def arrived(g):
        before = jnp.where(g > 0, block_ref[jnp.maximum(g * STEP - 1, 0)] + 1, 0)
        after = jnp.minimum(block_ref[g * STEP + STEP - 1] + 1, blocks)

        def wait(c, carry):
            pltpu.make_async_copy(tiles_ref.at[c], tiles_ref.at[c], sems.at[c]).wait()
            return carry

        lax.fori_loop(before, after, wait, 0)

    def gate_up_tiles(tiles, s):
        return jnp.concatenate(
            [tiles_ref[tiles, k, pl.ds(s, CHUNK)].reshape(CHUNK * blk, blk) for k in range(2)],
            axis=1,
        )

    def down_tiles(tiles, s):
        return jnp.concatenate([tiles_ref[tiles, 2, s + i] for i in range(CHUNK)], axis=1)

    def inward(position):
        c, s, rows, tiles = item(position)
        xg = jnp.concatenate([xpad_ref[r] for r in rows], axis=1)
        dyg = jnp.concatenate([dypad_ref[r] for r in rows], axis=1)
        pre = jnp.dot(xg, gate_up_tiles(tiles, s), preferred_element_type=jnp.float32)
        turned = jnp.dot(down_tiles(tiles, s), dyg.T, preferred_element_type=jnp.float32)
        d_hidden = turned.T
        pre_acc[c, :, : 2 * blk] += pre
        pre_acc[c, :, 2 * blk :] += d_hidden

    def outward(position):
        c, s, rows, tiles = item(position)
        gate, up, d_hidden = [pre_acc[c, :, i * blk : (i + 1) * blk] for i in range(3)]
        sig = 1.0 / (1.0 + jnp.exp(-gate))
        act = gate * sig
        hidden = (act * up).astype(jnp.bfloat16)
        d_gate = (d_hidden * up * sig * (1.0 + gate * (1.0 - sig))).astype(jnp.bfloat16)
        d = jnp.concatenate([d_gate, (d_hidden * act).astype(jnp.bfloat16)], axis=1)
        hidden_ref[c] = hidden
        d_ref[c] = d
        y = jnp.dot(hidden, down_tiles(tiles, s), preferred_element_type=jnp.float32)
        turned = jnp.dot(gate_up_tiles(tiles, s), d.T, preferred_element_type=jnp.float32)
        x_slots = turned.T
        add_to_rows(out_acc, rows, y, blk)
        add_to_rows(grad_acc, rows, x_slots, blk)

    def step(g, do_inward, do_outward):
        if do_inward:
            arrived(g)
        if do_outward:
            for i in range(STEP):
                outward((g - LAG) * STEP + i)
        if do_inward:
            for i in range(STEP):
                inward(g * STEP + i)

    steps = (total_ref[0] + STEP - 1) // STEP
    lag = jnp.minimum(steps, LAG)

    def loop(first, last, *parts):
        def body(g, carry):
            step(g, *parts)
            return carry

        lax.fori_loop(first, last, body, 0)

    loop(0, lag, True, False)
    loop(LAG, steps, True, True)
    loop(steps - lag + LAG, steps + LAG, False, True)
    for r in range(out_acc.shape[0] - 1):
        columns = slice(r * blk, (r + 1) * blk)
        for i, acc in enumerate((out_acc, grad_acc)):
            keep_ref[i, :, columns] = acc[r, :half]
            send_ref[i, :, columns] = acc[r, half:].astype(send_ref.dtype)


def gate_up_products(pad_ref, d, rows, slots, blk, stages, i):
    for s in slots[::2]:
        xs = jnp.concatenate([pad_ref[r] for r in rows[s : s + 2]], axis=1)
        full = lax.dot_general(xs, d, TN, preferred_element_type=jnp.float32)
        full = full.astype(jnp.bfloat16)
        for k in range(2):
            stages[0][i, s + k] = full[k * blk : (k + 1) * blk, :blk]
            stages[1][i, s + k] = full[k * blk : (k + 1) * blk, blk:]


def down_products(pad_ref, hidden, rows, slots, blk, stages, i):
    for s in slots[::CHUNK]:
        dys = jnp.concatenate([pad_ref[r] for r in rows[s : s + CHUNK]], axis=1)
        full = lax.dot_general(hidden, dys, TN, preferred_element_type=jnp.float32)
        full = full.astype(jnp.bfloat16)
        for k in range(CHUNK):
            stages[0][i, s + k] = full[:, k * blk : (k + 1) * blk]


def grad_kernel(products, first, count, outs, behind, *refs):
    live_ref, pad_ref, factor_ref = refs[:3]
    grad_refs = refs[3 + behind : 3 + behind + outs]
    stages = refs[3 + behind + outs : -1]
    sems = refs[-1]
    capacity, blk = stages[0].shape[1], stages[0].shape[-1]
    cut = capacity // 2 // CHUNK * CHUNK
    parts = (range(cut), range(cut, capacity))

    def copies(i, h):
        part = pl.ds(parts[h].start, len(parts[h]))
        return [
            pltpu.make_async_copy(stage.at[i, part], grad.at[first + i, part], sems.at[k, i, h])
            for k, (stage, grad) in enumerate(zip(stages, grad_refs))
        ]

    group = max(k for k in range(1, 5) if count % k == 0)

    def step(g, carry):
        some = [g * group + k for k in range(group)]
        rows = [[live_ref[first + i, s] for s in range(capacity)] for i in some]
        for i, names in zip(some, rows):
            for h in range(2):
                products(pad_ref, factor_ref[first + i], names, parts[h], blk, stages, i)
                for copy in copies(i, h):
                    copy.start()
        return carry

    lax.fori_loop(0, count // group, step, 0)
    for i in range(count):
        for h in range(2):
            for copy in copies(i, h):
                copy.wait()


def hop_orders(n):
    bits = [1 << i for i in range(n.bit_length() - 2, 0, -1)]
    return bits, bits[:-2] + bits[:-3:-1]


def swap(value, bits, n):
    return lax.ppermute(value, "col", [(j, j ^ bits[j % 2]) for j in range(n)])


def gather_hops(held, value, hops, n):
    send = value[None]
    for i, bits in enumerate(hops):
        if i:
            send = held[: 1 << i]
        held = lax.dynamic_update_slice_in_dim(held, swap(send, bits, n), 1 << i, 0)
    return held


def rows_of(held, swapped):
    pieces, mine, width = held.shape
    if swapped:
        held = held.reshape(2, 2, pieces // 4, mine, width).transpose(1, 0, 2, 3, 4)
    return held.reshape(pieces * mine, width)


def local(n, inputs, cotangent, gate_tiles, up_tiles, down_tiles, kept_rows, kept_count):
    blocks, capacity, blk, _ = gate_tiles.shape
    mine, width = inputs.shape
    tokens = mine * n
    smem = pl.BlockSpec(memory_space=pltpu.SMEM)
    vmem = pl.BlockSpec(memory_space=pltpu.VMEM)
    hbm = pl.BlockSpec(memory_space=pltpu.HBM)
    tile_bytes = blocks * capacity * blk * blk * 2
    tiles_in = [
        pltpu.with_memory_space_constraint(t, pltpu.HBM) for t in (gate_tiles, up_tiles, down_tiles)
    ]

    def cost(products, tiles, part=1.0):
        return pl.CostEstimate(
            flops=int(products * tokens * tile_bytes * part),
            bytes_accessed=int(tiles * tile_bytes * part),
            transcendentals=0,
        )

    listed = pltpu.SMEM((blocks * (capacity // CHUNK) + capacity // CHUNK + STEP,), jnp.int32)
    live, item_block, item_slot, total, x_held, dy_held = pl.pallas_call(
        functools.partial(seed_kernel, width // blk),
        in_specs=[smem, smem, vmem, vmem],
        out_specs=[smem] * 4 + [vmem] * 2,
        out_shape=[
            pltpu.SMEM((blocks + 1, capacity), jnp.int32),
            listed,
            listed,
            pltpu.SMEM((1,), jnp.int32),
        ]
        + [pltpu.VMEM((n // 2, mine, width), inputs.dtype)] * 2,
        name="seed",
    )(kept_rows, kept_count, inputs, cotangent)
    cores = (1, 1)
    first, second = hop_orders(n)
    x_hops, dy_hops = list(zip(first, second)), list(zip(second, first))
    x_held = gather_hops(x_held, inputs, x_hops, n)
    dy_held = gather_hops(dy_held, cotangent, dy_hops, n)
    x_near, x_far = [rows_of(v, False) for v in (x_held, swap(x_held, cores, n))]
    dy_near, dy_far = [rows_of(v, True) for v in (dy_held, swap(dy_held, cores, n))]

    padded = pltpu.VMEM((width // blk + 1, tokens, blk), jnp.bfloat16)
    acc = pltpu.VMEM((width // blk + 1, tokens, blk), jnp.float32)
    hidden, d, xpad, dypad, keep, send = pl.pallas_call(
        layer_kernel,
        in_specs=[smem] * 4 + [vmem] * 4 + [hbm] * 3,
        out_specs=[vmem] * 6,
        out_shape=[
            pltpu.VMEM((blocks + 1, tokens, blk), jnp.bfloat16),
            pltpu.VMEM((blocks + 1, tokens, 2 * blk), jnp.bfloat16),
            padded,
            padded,
            pltpu.VMEM((2, tokens // 2, width), jnp.float32),
            pltpu.VMEM((2, tokens // 2, width), jnp.bfloat16),
        ],
        scratch_shapes=[acc, acc, pltpu.VMEM((blocks + 1, tokens, 3 * blk), jnp.float32)]
        + [
            pltpu.VMEM((blocks, 3) + gate_tiles.shape[1:], jnp.bfloat16),
            pltpu.SemaphoreType.DMA((blocks,)),
        ],
        compiler_params=pltpu.CompilerParams(vmem_limit_bytes=40 * 1024 * 1024),
        cost_estimate=cost(6, 3),
        name="layer",
    )(live, item_block, item_slot, total, x_near, x_far, dy_near, dy_far, *tiles_in)

    def grads(products, pad, factor, first, count, outs, earlier, after, name):
        behind = len(earlier) + len(after)
        return pl.pallas_call(
            functools.partial(grad_kernel, products, first, count, outs, behind),
            in_specs=[smem, vmem, vmem]
            + [hbm] * len(earlier)
            + [pl.BlockSpec(memory_space=pl.ANY)] * len(after),
            out_specs=[hbm] * outs,
            out_shape=[jax.ShapeDtypeStruct(gate_tiles.shape, jnp.bfloat16)] * outs,
            scratch_shapes=[pltpu.VMEM((count,) + gate_tiles.shape[1:], jnp.bfloat16)] * outs
            + [pltpu.SemaphoreType.DMA((outs, count, 2))],
            input_output_aliases={3 + k: k for k in range(len(earlier))},
            compiler_params=pltpu.CompilerParams(vmem_limit_bytes=24 * 1024 * 1024),
            cost_estimate=cost(outs, outs, count / blocks),
            name=name,
        )(live, pad, factor, *earlier, *after)

    near = max(1, blocks // 6)
    middle = min(blocks - 1, near + (3 * (blocks - near) + 4) // 5)
    cuts = {0: (0, near), 2: (near, middle), 3: (middle, blocks)}
    gate_up, down_grad, after = [], None, []
    for i, bits in enumerate([cores] + x_hops[::-1]):
        got = swap(send, bits, n)
        done = []
        if i == 1:
            (down_grad,) = grads(
                down_products, dypad, hidden, 0, blocks, 1, [], after, "down_grad"
            )
            done = [down_grad]
        elif i in cuts:
            first, last = cuts[i]
            gate_up = grads(
                gate_up_products, xpad, d, first, last - first, 2, gate_up, after, "gate_up_grad"
            )
            done = gate_up
        total = keep + got.astype(jnp.float32)
        if i < len(x_hops):
            half = total.shape[1] // 2
            keep, send = total[:, :half], total[:, half:].astype(jnp.bfloat16)
            send, done = lax.optimization_barrier((send, done))
            after = [send]
            if i == 1:
                (down_grad,) = done
            elif i in cuts:
                gate_up = done
    total = total.astype(jnp.bfloat16)
    return total[0], total[1], gate_up[0], gate_up[1], down_grad


def solution(mesh):
    tiles = P("col", None, None, None)
    tokens = P(("groups", "col"), None)
    grads = P(("groups", "col"), None, None, None)
    return jax.shard_map(
        functools.partial(local, mesh.shape["col"]),
        mesh=mesh,
        in_specs=(tokens, tokens, tiles, tiles, tiles, P("col", None), P("col")),
        out_specs=(tokens, tokens, grads, grads, grads),
        check_vma=False,
    )
```
